32 devices in a mesh: groups: 2 (over y), map: 16 (over z, x, core).
Axes of the slice: x: 2, y: 2, z: 4, core: 2. Of those that a mesh axis runs over, the one named last changes fastest.
Arguments:
- amplitude_maps: bfloat16 [400, 512, 512], P('groups', 'map'), parts along dimension 0, may hold values from -6 to 6
- kept_blocks: int32 [512], P(('groups', 'map')), parts along dimension 0, may hold values from 0 to 2047, as said below
- block_owner: int32 [512, 1], P(('groups', 'map')), parts along dimension 0, may hold values from 0 to 15; in each aligned block of 16 rows (0 to 15, 16 to 31, ...) at most 2 rows name the same one
- observed: bfloat16 [8192], P(('groups', 'map')), parts along dimension 0, may hold values from -8 to 8
- error_scale: bfloat16 [8192], P(('groups', 'map')), parts along dimension 0, may hold values from 0.5 to 1.59375
- perturbation: bfloat16 [8192, 200], P(('groups', 'map')), parts along dimension 0, may hold values from -6 to 6
- model_slab: bfloat16 [200, 393216], P(None, ('groups', 'map')), parts along dimension 1, may hold values from -6 to 6
Outputs:
- updated_slab: bfloat16 [200, 393216], P(None, ('groups', 'map')), parts along dimension 1
- update_weights: float32 [400, 200], P('groups'), parts along dimension 0
- data_misfit: float32 [8192], P(('groups', 'map')), parts along dimension 0
The draws below stay inside these ranges and needn't reach their ends.
There are 2 independent parts, one for each index of `groups`. The reference program is written for one: setup_inputs(seed, part) draws one part's arguments, and reference() takes and returns one part's arrays. A program takes and returns all parts, laid end to end along the dimension named above; each array names one. Nothing has to cross between parts.
Inputs may be any that keep to these rules, and one draw needn't show every extreme that they name: `kept_blocks`: the 16 entries of one device are distinct numbers of that device's own 2048 blocks. `block_owner`: at most 2 of the 16 kept blocks of one device share an owner.
All inputs are finite; a program needn't handle non-finite values.
Results may differ from the reference program's by a relative error of at most 0.0018.
The reference program's roundings to bfloat16 on the way count: a program that leaves them out, or rounds other values in their place, can miss the bound.
Values may be sent and summed in bfloat16 or wider, within the bound.
No kernel may reach another device: no remote copies, remote signals or barrier semaphores. Data moves between devices by JAX's collectives and lax.ppermute only.
A program may use at most 128 MiB of HBM per device.

```python
import math
import jax
import jax.numpy as jnp
import numpy as np
from jax import lax

NE = 200
MAP_H = 512
MAP_W = 512
BLK = 8
CAP = 2
CD = 12288
KEEP = 16
COLS = 32
NBD = 2048
SLOTS = 256
KEPT = 2048
CELLS = 196608
N_MAP = 16


def draw_kept_blocks(key, part):
    base_key = jax.random.fold_in(key, 17)

    def per_device(device_index):
        device_key = jax.random.fold_in(base_key, device_index)
        inner_set = jax.random.permutation(device_key, NBD - 2)[:KEEP - 2] + 1
        chosen = jnp.concatenate([jnp.array([0, NBD - 1], dtype=jnp.int32), inner_set.astype(jnp.int32)])
        shuffle_order = jax.random.permutation(jax.random.fold_in(device_key, 3), KEEP)
        return chosen[shuffle_order]
    return jax.vmap(per_device)(jnp.arange(N_MAP, dtype=jnp.int32)).reshape(-1).astype(jnp.int32)


def levels(key, dims, pieces, least, largest):
    factor_of, own = 1.0, jax.random.fold_in(key, 6)
    for axis_at, parts in pieces:
        draws = jnp.exp(jax.random.uniform(jax.random.fold_in(own, axis_at), (parts,), jnp.float32, least / len(pieces), largest / len(pieces)))
        factor_of = factor_of * jnp.repeat(draws, dims[axis_at] // parts).reshape([-1 if axis == axis_at else 1 for axis in range(len(dims))])
    return factor_of


def routed_block(own_key, own, number, rows, number_of, top, reach, skew):
    order = jax.random.permutation(own_key, number_of)
    crowded, ordinary = shares(number_of, rows * top, reach, skew, True), shares(number_of, rows * top, reach, skew, False)
    places = jnp.arange(number_of)

    def named(sizes, turn):
        used = int((sizes > 0).sum())
        fixed = max(1, used // 4)
        moved = fixed + (places - fixed + turn * (used - fixed)) % max(1, number_of - fixed)
        return jnp.zeros((number_of,), jnp.int32).at[order[jnp.where(places < fixed, places, moved)]].set(jnp.asarray(sizes, jnp.int32))

    sizes = jnp.where(number % 4 == 0, named(crowded, number // 4), named(ordinary, number - number // 4 - 1))
    mixed = jax.random.permutation(jax.random.fold_in(own, 3), number_of)
    giver, sink = mixed[0:number_of // 2 * 2:2], mixed[1:number_of // 2 * 2:2]
    slack = jnp.minimum(sizes[giver] - 1, reach - sizes[sink]) // 2
    slack = jnp.where((giver == order[0]) | (sink == order[0]) | (sizes[sink] == 0), 0, jnp.maximum(slack, 0))
    moved = jax.random.randint(jax.random.fold_in(own, 4), (number_of // 2,), 0, 1 << 20) % (slack + 1)
    sizes = sizes.at[giver].add(-moved).at[sink].add(moved)
    labels = jnp.searchsorted(jnp.cumsum(sizes), jnp.arange(rows * top), side="right").astype(jnp.int32)
    grid = labels.reshape(top, rows).T
    grid = grid[jax.random.permutation(jax.random.fold_in(own, 1), rows)]
    turn = jax.random.randint(jax.random.fold_in(own, 2), (rows, 1), 0, top)
    return jnp.take_along_axis(grid, (jnp.arange(top)[None, :] + turn) % top, axis=1)


def shares(count, total, most, slope, full):
    loads = [(1 << 20) // math.isqrt(rank ** slope) + 1 for rank in range(1, count + 1)]
    largest = most if full else min(most, max(-(-total // count), total * loads[0] // sum(loads)))
    least = 1 if total - largest >= count - 1 else 0
    counts, surplus = [largest] + [least] * (count - 1), total - largest - least * (count - 1)
    while surplus > 0:
        free = [i for i in range(1, count) if counts[i] < largest] or [i for i in range(1, count) if counts[i] < most]
        mass, left = sum([loads[i] for i in free]), surplus
        for i in free:
            addition = min(most - counts[i], max(1, left * loads[i] // mass), surplus)
            counts[i] = counts[i] + addition
            surplus = surplus - addition
    return np.array(counts)


def centred(key, extent, scale, reach, shards=(), kind=jnp.bfloat16):
    values = jax.random.normal(key, extent, jnp.float32) * scale
    if len(shards) > 0:
        values = levels(key, extent, shards, -0.22, 0.18) * values
    return jnp.clip(values, min=-reach, max=reach).astype(kind)


def setup_inputs(seed: int = 0, part: int = 0) -> dict:
    streams_of = jax.random.split(jax.random.key(seed), 8)
    own_keys = jax.random.split(jax.random.fold_in(streams_of[7], part), 8)
    amplitude_maps = centred(own_keys[0], (NE, MAP_H, MAP_W), 1.0, 6.0, ((1, 16),))
    kept_blocks = draw_kept_blocks(jax.random.fold_in(jax.random.fold_in(streams_of[7], part), 71), part)
    block_owner_keys = jax.random.split(jax.random.fold_in(own_keys[2], 1), (N_MAP * KEEP) // KEEP)
    block_owner_turns = jax.random.permutation(jax.random.fold_in(own_keys[2], 3), (N_MAP * KEEP) // KEEP)
    block_owner = jax.vmap(lambda own, number: routed_block(jax.random.fold_in(own_keys[2], 2), own, number, KEEP, N_MAP, 1, CAP, 2))(block_owner_keys, block_owner_turns).reshape((N_MAP * KEEP, 1))
    observed = centred(own_keys[3], (N_MAP * SLOTS,), 2.0, 8.0, ((0, 16),))
    error_scale = jnp.clip(jnp.exp(math.log(1.59375) - 1.1592369 * jax.random.uniform(own_keys[4], (N_MAP * SLOTS,), jnp.float32) ** levels(own_keys[4], (N_MAP * SLOTS,), ((0, 16),), -0.2, 0.2)), 0.5, 1.59375).astype(jnp.bfloat16)
    perturbation = centred(own_keys[5], (N_MAP * SLOTS, NE), 1.0, 6.0, ((0, 16),))
    model_slab = centred(own_keys[6], (NE, CELLS), 1.0, 6.0, ((1, 16),))
    return dict(amplitude_maps=amplitude_maps, kept_blocks=kept_blocks, block_owner=block_owner, observed=observed, error_scale=error_scale, perturbation=perturbation, model_slab=model_slab)


inflation = 4.0
epsilon = 1e-06

def dct_table(length):
    frequency = jnp.arange(length, dtype=jnp.float32)[:, None]
    sample = jnp.arange(length, dtype=jnp.float32)[None, :]
    cosine_table = jnp.cos(math.pi * (2.0 * sample + 1.0) * frequency / (2.0 * length))
    factor = jnp.where(frequency == 0, math.sqrt(1.0 / length), math.sqrt(2.0 / length))
    return (cosine_table * factor).astype(jnp.bfloat16)

def gram_terms(predicted, observed_rows, scale_rows, noise_rows, live_mask, weight_scale):
    members = predicted.shape[1]
    center = lax.optimization_barrier(jnp.mean(predicted, axis=1, keepdims=True))
    anomaly = (predicted - center) / math.sqrt(members - 1)
    weight = live_mask * weight_scale / (scale_rows * scale_rows)
    mismatch = observed_rows[:, None] + math.sqrt(inflation) * scale_rows[:, None] * noise_rows - predicted
    weighted = anomaly * weight[:, None]
    contract = (((0,), (0,)), ((), ()))
    gram_matrix = lax.dot_general(anomaly, weighted, contract, precision=lax.Precision.HIGHEST)
    cross_terms = lax.dot_general(weighted, mismatch, contract, precision=lax.Precision.HIGHEST)
    relative = mismatch / scale_rows[:, None]
    misfit_rows = live_mask * jnp.sqrt(lax.optimization_barrier(jnp.mean(relative * relative, axis=1)) + epsilon)
    return (gram_matrix, cross_terms, misfit_rows)

def solve_weights(gram_matrix, cross_terms):
    members = gram_matrix.shape[0]
    factor = jnp.linalg.cholesky(gram_matrix + inflation * jnp.eye(members, dtype=jnp.float32))
    return jax.scipy.linalg.cho_solve((factor, True), cross_terms)

def update_state(block, update_weights):
    state = block.astype(jnp.float32)
    members = state.shape[0]
    anomaly = (state - lax.optimization_barrier(jnp.mean(state, axis=0, keepdims=True))) / math.sqrt(members - 1)
    moved = state + lax.dot_general(update_weights, anomaly, (((0,), (0,)), ((), ())), precision=lax.Precision.HIGHEST)
    return moved.astype(jnp.bfloat16)

def reference(amplitude_maps, kept_blocks, block_owner, observed, error_scale, perturbation, model_slab):
    table_w = dct_table(MAP_W)
    table_h = dct_table(MAP_H)
    flat_maps = amplitude_maps.reshape(NE * MAP_H, MAP_W)
    rowwise = jnp.dot(flat_maps.astype(jnp.float32), table_w.T.astype(jnp.float32), preferred_element_type=jnp.float32).astype(jnp.bfloat16)
    rowwise = rowwise.reshape(NE, MAP_H, MAP_W).transpose(1, 0, 2).reshape(MAP_H, NE * MAP_W)
    coefficients = jnp.dot(table_h.astype(jnp.float32), rowwise.astype(jnp.float32), preferred_element_type=jnp.float32).astype(jnp.bfloat16)
    coefficients = coefficients.reshape(MAP_H, NE, MAP_W)
    per_column = MAP_H // BLK
    chosen = kept_blocks.reshape(N_MAP, KEEP)
    device_ids = jnp.arange(N_MAP, dtype=jnp.int32)[:, None]
    column_ids = device_ids * COLS + chosen // per_column
    row_starts = chosen % per_column * BLK
    within = jnp.arange(BLK, dtype=jnp.int32)
    row_ids = (row_starts[:, :, None] + within[None, None, :]).astype(jnp.int32)
    column_full = jnp.broadcast_to(column_ids[:, :, None], row_ids.shape).astype(jnp.int32)
    predicted = coefficients[row_ids, :, column_full]
    predicted = predicted.reshape(KEPT, NE).astype(jnp.float32)
    owners = block_owner.reshape(N_MAP, KEEP)
    positions = jnp.arange(KEEP, dtype=jnp.int32)
    earlier = (owners[:, :, None] == owners[:, None, :]) & (positions[None, None, :] < positions[None, :, None])
    slot_rank = lax.optimization_barrier(jnp.sum(earlier.astype(jnp.int32), axis=2))
    slot_rows = owners * SLOTS + device_ids * (CAP * BLK) + slot_rank * BLK
    data_rows = (slot_rows[:, :, None] + within[None, None, :]).reshape(KEPT).astype(jnp.int32)
    observed_rows = observed[data_rows].astype(jnp.float32)
    scale_rows = error_scale[data_rows].astype(jnp.float32)
    noise_rows = perturbation[data_rows].astype(jnp.float32)
    live_mask = jnp.ones((KEPT,), jnp.float32)
    gram_matrix, cross_terms, misfit_rows = gram_terms(predicted, observed_rows, scale_rows, noise_rows, live_mask, NE / KEPT)
    update_weights = solve_weights(gram_matrix, cross_terms)
    data_misfit = jnp.zeros((N_MAP * SLOTS,), jnp.float32).at[data_rows].set(misfit_rows)
    slab_blocks = model_slab.reshape(NE, N_MAP, CD).transpose(1, 0, 2)
    updated = lax.map(lambda block: update_state(block, update_weights), slab_blocks)
    updated_slab = updated.transpose(1, 0, 2).reshape(NE, CELLS)
    return (updated_slab, update_weights, data_misfit)
```

```python
import functools
import math

import jax
import jax.numpy as jnp
from jax import lax
from jax.experimental import pallas as pl
from jax.experimental.pallas import tpu as pltpu
from jax.sharding import PartitionSpec as P

BLK = 8
CAP = 2
LANE = 128

inflation = 4.0
epsilon = 1e-06

VMEM_LIMIT = 56 * 1024 * 1024


def dct_rows(frequency, sample, length):
    cosine_table = jnp.cos(math.pi * (2.0 * sample + 1.0) * frequency / (2.0 * length))
    factor = jnp.where(frequency == 0, math.sqrt(1.0 / length), math.sqrt(2.0 / length))
    return (cosine_table * factor).astype(jnp.bfloat16)


def dct_table(length):
    frequency = jnp.arange(length, dtype=jnp.float32)[:, None]
    sample = jnp.arange(length, dtype=jnp.float32)[None, :]
    return dct_rows(frequency, sample, length)


def gram_terms(predicted, observed_rows, scale_rows, noise_rows, live_mask, weight_scale):
    members = predicted.shape[1]
    center = jnp.mean(predicted, axis=1, keepdims=True)
    anomaly = (predicted - center) / math.sqrt(members - 1)
    weight = live_mask * weight_scale / (scale_rows * scale_rows)
    mismatch = (
        observed_rows[:, None] + math.sqrt(inflation) * scale_rows[:, None] * noise_rows - predicted
    )
    weighted = anomaly * weight[:, None]
    contract = (((0,), (0,)), ((), ()))
    gram_matrix = lax.dot_general(anomaly, weighted, contract, precision=lax.Precision.HIGHEST)
    cross_terms = lax.dot_general(weighted, mismatch, contract, precision=lax.Precision.HIGHEST)
    relative = mismatch / scale_rows[:, None]
    misfit_rows = live_mask * jnp.sqrt(jnp.mean(relative * relative, axis=1) + epsilon)
    return (gram_matrix, cross_terms, misfit_rows)


def solve_weights(gram_matrix, cross_terms):
    members = gram_matrix.shape[0]
    factor = jnp.linalg.cholesky(gram_matrix + inflation * jnp.eye(members, dtype=jnp.float32))
    return jax.scipy.linalg.cho_solve((factor, True), cross_terms)


def update_state(block, update_weights):
    state = block.astype(jnp.float32)
    members = state.shape[0]
    anomaly = (state - jnp.mean(state, axis=0, keepdims=True)) / math.sqrt(members - 1)
    moved = state + lax.dot_general(
        update_weights, anomaly, (((0,), (0,)), ((), ())), precision=lax.Precision.HIGHEST
    )
    return moved.astype(jnp.bfloat16)


def dense_body(
    amplitude_maps, kept_blocks, block_owner, observed, error_scale, perturbation, model_slab
):
    members, rows_here, map_width = amplitude_maps.shape
    devices = lax.axis_size("map")
    map_height = rows_here * devices
    table_w = dct_table(map_width)
    table_h = dct_table(map_height)
    rowwise = jnp.einsum(
        "ehw,kw->hke", amplitude_maps, table_w, preferred_element_type=jnp.float32
    ).astype(jnp.bfloat16)
    coefficients = jnp.einsum(
        "kh,hwe->wke",
        table_h,
        lax.all_to_all(rowwise, "map", split_axis=1, concat_axis=0, tiled=True),
        preferred_element_type=jnp.float32,
    ).astype(jnp.bfloat16)
    block_rows = coefficients.reshape(-1, BLK * members)
    candidates = block_rows.shape[0]
    keep_count = kept_blocks.shape[0]
    slot_count = devices * CAP
    dest_owner = block_owner[:, 0]
    positions = jnp.arange(keep_count, dtype=jnp.int32)
    earlier = (dest_owner[:, None] == dest_owner[None, :]) & (
        positions[None, :] < positions[:, None]
    )
    slot_rank = jnp.sum(earlier.astype(jnp.int32), axis=1)
    slot_index = dest_owner * CAP + slot_rank
    pick_slot = (slot_index[:, None] == jnp.arange(slot_count, dtype=jnp.int32)[None, :]).astype(
        jnp.bfloat16
    )
    weight_scale = members / (devices * keep_count * BLK)
    contract = (((0,), (0,)), ((), ()))
    pick_block = (kept_blocks[:, None] == jnp.arange(candidates, dtype=jnp.int32)[None, :]).astype(
        jnp.bfloat16
    )
    routing = lax.dot_general(
        pick_slot, pick_block, contract, preferred_element_type=jnp.float32
    ).astype(jnp.bfloat16)
    outgoing = jnp.dot(routing, block_rows, preferred_element_type=jnp.float32).astype(jnp.bfloat16)
    live_slots = jnp.sum(pick_slot.astype(jnp.float32), axis=0).astype(jnp.bfloat16)
    arrived, arrived_live = (
        lax.all_to_all(
            outgoing.reshape(devices, CAP, BLK * members),
            "map",
            split_axis=0,
            concat_axis=0,
            tiled=True,
        ),
        lax.all_to_all(
            live_slots.reshape(devices, CAP), "map", split_axis=0, concat_axis=0, tiled=True
        ),
    )
    predicted = arrived.reshape(-1, members).astype(jnp.float32)
    live_mask = jnp.repeat(arrived_live.astype(jnp.float32).reshape(-1), BLK)
    gram_matrix, cross_terms, data_misfit = gram_terms(
        predicted,
        observed.astype(jnp.float32),
        error_scale.astype(jnp.float32),
        perturbation.astype(jnp.float32),
        live_mask,
        weight_scale,
    )
    gram_matrix, cross_terms = lax.psum((gram_matrix, cross_terms), "map")
    update_weights = solve_weights(gram_matrix, cross_terms)
    updated_slab = update_state(model_slab, update_weights)
    return (updated_slab, update_weights, data_misfit)


def swap(value, delta):
    pairs = [(i, i ^ delta) for i in range(lax.axis_size("map"))]
    return lax.ppermute(value, "map", pairs)


def by_row_kernel(maps_ref, out_ref, wide_ref):
    members, rows, width = maps_ref.shape
    wide_ref[...] = maps_ref[...].reshape(members * rows, width).astype(jnp.float32)
    for row in range(rows):
        out_ref[row] = wide_ref[pl.ds(row, members, stride=rows), :].astype(jnp.bfloat16)


def by_row(amplitude_maps):
    members, rows, width = amplitude_maps.shape
    return pl.pallas_call(
        by_row_kernel,
        grid=(width // LANE,),
        in_specs=[pl.BlockSpec((members, rows, LANE), lambda i: (0, 0, i))],
        out_specs=pl.BlockSpec((rows, members, LANE), lambda i: (0, 0, i)),
        out_shape=jax.ShapeDtypeStruct((rows, members, width), jnp.bfloat16),
        scratch_shapes=[pltpu.VMEM((members * rows, LANE), jnp.float32)],
        compiler_params=pltpu.CompilerParams(vmem_limit_bytes=VMEM_LIMIT),
        cost_estimate=pl.CostEstimate(
            flops=0, bytes_accessed=8 * members * rows * width, transcendentals=0
        ),
        name="maps_by_row",
    )(amplitude_maps)


def shares_kernel(
    starts_ref, maps_ref, column_ref, table_w_ref, table_h_ref, k0_ref, k1_ref, s0_ref, s1_ref,
    pick_ref, row_ref, wide_ref,
):
    step = pl.program_id(0)
    rows, members, width = maps_ref.shape
    keep = row_ref.shape[1] // (rows * pl.num_programs(0))
    devices = row_ref.shape[0]

    @pl.when(step == 0)
    def _():
        lanes = lax.broadcasted_iota(jnp.int32, (column_ref.shape[0], width), 1)
        one_hot = (column_ref[...] == lanes).astype(jnp.bfloat16)
        pick_ref[...] = jnp.dot(
            one_hot, table_w_ref[...], preferred_element_type=jnp.float32
        ).astype(jnp.bfloat16)

    for row in range(rows):
        rowwise = lax.dot_general(
            pick_ref[...], maps_ref[row], (((1,), (1,)), ((), ())),
            preferred_element_type=jnp.float32,
        ).astype(jnp.bfloat16)
        place = pl.ds(pl.multiple_of((step * rows + row) * keep, keep), keep)
        row_ref[:, place, :] = rowwise.reshape(devices, keep, members)

    @pl.when(step == pl.num_programs(0) - 1)
    def _():
        depth = row_ref.shape[1]
        position = lax.broadcasted_iota(jnp.int32, (BLK, depth), 1) % keep
        outs = ((k0_ref, 0), (k1_ref, 2), (s0_ref, 1), (s1_ref, 3))
        for out_ref, low in outs:
            for high in range(out_ref.shape[0]):
                delta = high * 4 + low
                for p in range(keep):
                    start = pl.multiple_of(starts_ref[delta * keep + p], BLK)
                    block = table_h_ref[pl.ds(start, BLK), :]
                    wide_ref[pl.ds(p * BLK, BLK), :] = jnp.where(position == p, block, 0.0)
                share = jnp.dot(
                    wide_ref[...].astype(jnp.bfloat16), row_ref[delta],
                    preferred_element_type=jnp.float32,
                )
                out_ref[high] = share.T


def shares(maps, columns, starts, table_w, table_h):
    rows, members, width = maps.shape
    kept = columns.shape[0]
    devices = lax.axis_size("map")
    keep = kept // devices
    steps = 4
    depth = rows * keep
    out = jax.ShapeDtypeStruct((devices // 4, members, keep * BLK), jnp.float32)
    whole = lambda *shape: pl.BlockSpec(shape, lambda i, s: (0,) * len(shape))
    return pl.pallas_call(
        shares_kernel,
        grid_spec=pltpu.PrefetchScalarGridSpec(
            num_scalar_prefetch=1,
            grid=(steps,),
            in_specs=[
                pl.BlockSpec((rows // steps, members, width), lambda i, s: (i, 0, 0)),
                whole(kept, 1),
                whole(*table_w.shape),
                whole(*table_h.shape),
            ],
            out_specs=[whole(*out.shape)] * 4,
            scratch_shapes=[
                pltpu.VMEM((kept, width), jnp.bfloat16),
                pltpu.VMEM((devices, depth, members), jnp.bfloat16),
                pltpu.VMEM((keep * BLK, depth), jnp.float32),
            ],
        ),
        out_shape=[out] * 4,
        compiler_params=pltpu.CompilerParams(vmem_limit_bytes=VMEM_LIMIT),
        cost_estimate=pl.CostEstimate(
            flops=2 * kept * width * rows * members,
            bytes_accessed=2 * rows * members * width,
            transcendentals=0,
        ),
        name="coefficient_shares",
    )(starts, maps, columns, table_w, table_h)


def gram_kernel(
    starts_ref, place_ref, target_ref, *refs
):
    predicted_refs, noise_refs = refs[:8], refs[8:12]
    out_ref, predicted_ref, wide_ref, noise_ref, left_ref, right_ref, misfit_ref = refs[12:]
    groups, members, per = predicted_ref.shape
    keep = per // BLK
    coefficients = groups * per
    weight_scale = members / (2 * coefficients)
    chip = place_ref[0]
    for i, ref in enumerate(predicted_refs):
        predicted_ref[chip ^ i] = ref[...].astype(jnp.float32)
    span = wide_ref.shape[0] // 4
    for i, ref in enumerate(noise_refs):
        wide_ref[pl.ds(i * span, span), :] = ref[...].reshape(span, -1).astype(jnp.float32)
    right_ref[...] = jnp.zeros_like(right_ref)
    for g in range(groups):
        for p in range(keep):
            start = pl.multiple_of(starts_ref[g * keep + p], BLK)
            noise_ref[pl.ds(p * BLK, BLK), :] = wide_ref[pl.ds(start, BLK), :]
        noise = noise_ref[...].T
        observed = noise[members : members + 1]
        scale = noise[members + 1 : members + 2]
        predicted = predicted_ref[g]
        center = jnp.sum(predicted, axis=0, keepdims=True) * (1.0 / members)
        anomaly = (predicted - center) * (1.0 / math.sqrt(members - 1))
        weight = weight_scale / (scale * scale)
        mismatch = observed + math.sqrt(inflation) * scale * noise[:members] - predicted
        here = pl.ds(g * per, per)
        left_ref[:, here] = anomaly * weight
        right_ref[0:members, here] = anomaly
        right_ref[256 : 256 + members, here] = mismatch
        relative = mismatch / scale
        misfit = jnp.sqrt(
            jnp.sum(relative * relative, axis=0, keepdims=True) * (1.0 / members) + epsilon
        )
        high = misfit.astype(jnp.bfloat16)
        rest = misfit - high.astype(jnp.float32)
        middle = rest.astype(jnp.bfloat16)
        low = (rest - middle.astype(jnp.float32)).astype(jnp.bfloat16)
        misfit_ref[0:1, here] = high.astype(jnp.float32)
        misfit_ref[1:2, here] = middle.astype(jnp.float32)
        misfit_ref[2:3, here] = low.astype(jnp.float32)
        misfit_ref[3:8, here] = jnp.zeros((5, per), jnp.float32)
    out_ref[0:members, :] = lax.dot_general(
        left_ref[...], right_ref[...], (((1,), (1,)), ((), ())),
        precision=lax.Precision.HIGHEST, preferred_element_type=jnp.float32,
    )
    lanes = lax.broadcasted_iota(jnp.int32, (coefficients, out_ref.shape[1]), 1)
    one_hot = (target_ref[...] == lanes).astype(jnp.bfloat16)
    routed = jnp.dot(
        misfit_ref[...].astype(jnp.bfloat16), one_hot, preferred_element_type=jnp.float32
    )
    out_ref[members : members + 8, :] = jnp.broadcast_to(
        routed[0:1] + routed[1:2] + routed[2:3], (8, out_ref.shape[1])
    )


def gram(starts, place, target, predicted, noise):
    members, per = predicted[0].shape
    groups = len(predicted)
    coefficients = groups * per
    rows = 4 * noise[0].shape[0] * noise[0].shape[1] * noise[0].shape[2]
    smem = pl.BlockSpec(memory_space=pltpu.SMEM)
    vmem = pl.BlockSpec(memory_space=pltpu.VMEM)
    return pl.pallas_call(
        gram_kernel,
        in_specs=[smem, smem] + [vmem] * (1 + len(predicted) + len(noise)),
        out_specs=vmem,
        out_shape=jax.ShapeDtypeStruct((members + 8, 512), jnp.float32),
        scratch_shapes=[
            pltpu.VMEM((groups, members, per), jnp.float32),
            pltpu.VMEM((rows, 256), jnp.float32),
            pltpu.VMEM((per, 256), jnp.float32),
            pltpu.VMEM((members, coefficients), jnp.float32),
            pltpu.VMEM((512, coefficients), jnp.float32),
            pltpu.VMEM((8, coefficients), jnp.float32),
        ],
        compiler_params=pltpu.CompilerParams(vmem_limit_bytes=VMEM_LIMIT),
        name="gram_and_cross",
    )(starts, place, target, *predicted, *noise)


def solve_kernel(mine_ref, other_ref, weights_ref, parts_ref, misfit_ref, state_ref, power_ref):
    members = weights_ref.shape[0]
    total = mine_ref[0:members, :] + other_ref[0:members, :]
    misfit_ref[...] = (
        mine_ref[members : members + 8, 0:256] + other_ref[members : members + 8, 256:512]
    )
    row = lax.broadcasted_iota(jnp.int32, (members, 256), 0)
    lane = lax.broadcasted_iota(jnp.int32, (members, 256), 1)
    unit = jnp.where(row == lane, 1.0, 0.0)
    matrix = total[:, 0:256] + inflation * unit
    bound = jnp.max(jnp.sum(jnp.abs(matrix), axis=1, keepdims=True), axis=0, keepdims=True)
    step = 2.0 / (inflation + bound)
    state_ref[members:256, :] = jnp.zeros((256 - members, 512), jnp.float32)
    state_ref[0:members, 0:256] = unit - step * matrix
    state_ref[0:members, 256:512] = step * total[:, 256:512]

    def more(carry):
        return carry[0] > 2.0**-24

    def double(carry):
        power = state_ref[:, 0:256]
        size = jnp.sum(power * power)
        moved = jnp.dot(
            power, state_ref[...], precision=lax.Precision.HIGHEST,
            preferred_element_type=jnp.float32,
        )
        state_ref[:, 0:256] = moved[:, 0:256]
        state_ref[:, 256:512] = state_ref[:, 256:512] + moved[:, 256:512]
        return (size,)

    lax.while_loop(more, double, (jnp.float32(1.0),))
    weights = state_ref[0:members, 256 : 256 + members]
    weights_ref[...] = weights
    full = state_ref[:, 256:512]
    center = jnp.sum(full, axis=0, keepdims=True) * (1.0 / members)
    spread = ((full - center) * (1.0 / math.sqrt(members - 1))).T[0:members, 0:members]
    high = spread.astype(jnp.bfloat16)
    rest = spread - high.astype(jnp.float32)
    middle = rest.astype(jnp.bfloat16)
    low = (rest - middle.astype(jnp.float32)).astype(jnp.bfloat16)
    parts_ref[0] = high
    parts_ref[1] = middle
    parts_ref[2] = low


def solve(mine, other):
    members = mine.shape[0] - 8
    vmem = pl.BlockSpec(memory_space=pltpu.VMEM)
    return pl.pallas_call(
        solve_kernel,
        in_specs=[vmem, vmem],
        out_specs=[vmem] * 3,
        out_shape=[
            jax.ShapeDtypeStruct((members, members), jnp.float32),
            jax.ShapeDtypeStruct((3, members, members), jnp.bfloat16),
            jax.ShapeDtypeStruct((8, 256), jnp.float32),
        ],
        scratch_shapes=[pltpu.VMEM((256, 512), jnp.float32), pltpu.VMEM((256, 512), jnp.float32)],
        compiler_params=pltpu.CompilerParams(vmem_limit_bytes=VMEM_LIMIT),
        name="solve_weights",
    )(mine, other)


def slab_kernel(parts_ref, slab_ref, out_ref):
    state = slab_ref[...]
    moved = jnp.dot(parts_ref[2], state, preferred_element_type=jnp.float32)
    moved = moved + jnp.dot(parts_ref[1], state, preferred_element_type=jnp.float32)
    moved = moved + jnp.dot(parts_ref[0], state, preferred_element_type=jnp.float32)
    out_ref[...] = (state.astype(jnp.float32) + moved).astype(jnp.bfloat16)


def move_slab(parts, slab):
    members, cells = slab.shape
    tile = 2048
    return pl.pallas_call(
        slab_kernel,
        grid=(cells // tile,),
        in_specs=[
            pl.BlockSpec(parts.shape, lambda i: (0, 0, 0)),
            pl.BlockSpec((members, tile), lambda i: (0, i)),
        ],
        out_specs=pl.BlockSpec((members, tile), lambda i: (0, i)),
        out_shape=jax.ShapeDtypeStruct(slab.shape, slab.dtype),
        compiler_params=pltpu.CompilerParams(vmem_limit_bytes=VMEM_LIMIT),
        name="slab_update",
    )(parts, slab)


def sparse_body(
    amplitude_maps, kept_blocks, block_owner, observed, error_scale, perturbation, model_slab
):
    members, rows_here, map_width = amplitude_maps.shape
    devices = lax.axis_size("map")
    map_height = rows_here * devices
    per_column = map_height // BLK
    columns_here = map_width // devices
    keep = kept_blocks.shape[0]
    slots = observed.shape[0]
    me = lax.axis_index("map").astype(jnp.int32)

    lists = jnp.stack([kept_blocks, block_owner[:, 0]])
    lists = jnp.stack([lists] + [swap(lists, delta) for delta in range(1, devices)])

    extra = jnp.zeros((slots, 256 - members - 2), jnp.bfloat16)
    noise = jnp.concatenate(
        [perturbation, observed[:, None], error_scale[:, None], extra], axis=1
    ).reshape(devices // 2, 2, CAP * BLK, 256)
    core = me & 1
    noise_keep = lax.dynamic_index_in_dim(noise, core, 1, keepdims=False)
    noise_send = lax.dynamic_index_in_dim(noise, 1 - core, 1, keepdims=False)
    noise = jnp.stack([noise_keep, swap(noise_send, 1)]).reshape(2, -1, 256)
    noise = jnp.stack([noise, swap(noise, 2)])
    noises = [noise] + [swap(noise, delta) for delta in (4, 8, 12)]

    maps = by_row(amplitude_maps)
    table_w = dct_table(map_width)
    frequency = jnp.arange(map_height, dtype=jnp.float32)[:, None]
    sample = jnp.repeat(jnp.arange(rows_here, dtype=jnp.int32), keep)[None, :] + me * rows_here
    table_h = dct_rows(frequency, sample.astype(jnp.float32), map_height).astype(jnp.float32)

    device = me ^ jnp.arange(devices, dtype=jnp.int32)
    columns = device[:, None] * columns_here + lists[:, 0] // per_column
    starts = (lists[:, 0] % per_column * BLK).reshape(-1)
    keep_0, keep_1, send_0, send_1 = shares(
        maps, columns.reshape(-1, 1), starts, table_w, table_h
    )

    share_1 = keep_1 + swap(send_1, 1)
    got_1 = swap(share_1, 2)
    share_0 = keep_0 + swap(send_0, 1)
    share = [share_0[i] + got_1[i] for i in range(devices // 4)]
    got = [swap(share[i], 4 * i) for i in range(1, devices // 4)]
    predicted = (share[0] + got[0] + got[1] + got[2]).astype(jnp.bfloat16)

    near = [predicted] + [swap(predicted, 4 * i) for i in range(1, devices // 4)]
    gathered = []
    for value in near:
        gathered += [value, swap(value, 2)]

    owner = lists[:, 1]
    positions = jnp.arange(keep, dtype=jnp.int32)
    earlier = (owner[:, :, None] == owner[:, None, :]) & (
        positions[None, None, :] < positions[None, :, None]
    )
    rank = jnp.sum(earlier.astype(jnp.int32), axis=2)
    chip = me >> 1
    chips = jnp.arange(devices // 2, dtype=jnp.int32)
    owner = jnp.take(owner[0::2], chip ^ chips, axis=0)
    rank = jnp.take(rank[0::2], chip ^ chips, axis=0)
    noise_rows = (owner ^ me) * (slots // 2) + chips[:, None] * (CAP * BLK) + rank * BLK
    data_row = (chips[:, None] * 2 + core) * (CAP * BLK) + rank * BLK
    away = owner ^ me
    target = jnp.where(away < 2, away * slots + data_row, -1024)
    target = (target[:, :, None] + jnp.arange(BLK, dtype=jnp.int32)).reshape(-1, 1)

    mine = gram(noise_rows.reshape(-1), chip.reshape(1), target, gathered, noises)
    update_weights, parts, data_misfit = solve(mine, swap(mine, 1))
    updated_slab = move_slab(parts, model_slab)
    return (updated_slab, update_weights, data_misfit[0])


def solution(mesh):
    in_specs = (
        P("groups", "map", None),
        P(("groups", "map")),
        P(("groups", "map"), None),
        P(("groups", "map")),
        P(("groups", "map")),
        P(("groups", "map"), None),
        P(None, ("groups", "map")),
    )
    out_specs = (P(None, ("groups", "map")), P("groups", None), P(("groups", "map")))

    def body(amplitude_maps, kept_blocks, *rest):
        few = mesh.shape["map"] == 16 and kept_blocks.shape[0] * BLK == LANE
        chosen = sparse_body if few else dense_body
        return chosen(amplitude_maps, kept_blocks, *rest)

    return jax.shard_map(body, mesh=mesh, in_specs=in_specs, out_specs=out_specs, check_vma=False)
```

```python
import math

import jax
import jax.numpy as jnp
import numpy as np
from jax import lax
from jax.experimental import pallas as pl
from jax.experimental.pallas import tpu as pltpu
from jax.sharding import PartitionSpec as P

BLK = 8
CAP = 2
LANE = 128

inflation = 4.0
epsilon = 1e-06

VMEM_LIMIT = 56 * 1024 * 1024


def dct_table(length):
    frequency = jnp.arange(length, dtype=jnp.float32)[:, None]
    sample = jnp.arange(length, dtype=jnp.float32)[None, :]
    cosine_table = jnp.cos(math.pi * (2.0 * sample + 1.0) * frequency / (2.0 * length))
    factor = jnp.where(frequency == 0, math.sqrt(1.0 / length), math.sqrt(2.0 / length))
    return (cosine_table * factor).astype(jnp.bfloat16)


def dct_constant(length):
    frequency = np.arange(length, dtype=np.float32)[:, None]
    sample = np.arange(length, dtype=np.float32)[None, :]
    angle = np.float32(math.pi) * (np.float32(2.0) * sample + np.float32(1.0)) * frequency
    cosine_table = np.cos(angle / np.float32(2.0 * length))
    factor = np.where(
        frequency == 0, np.float32(math.sqrt(1.0 / length)), np.float32(math.sqrt(2.0 / length))
    )
    return (cosine_table * factor).astype(jnp.bfloat16)


def gram_terms(predicted, observed_rows, scale_rows, noise_rows, live_mask, weight_scale):
    members = predicted.shape[1]
    center = jnp.mean(predicted, axis=1, keepdims=True)
    anomaly = (predicted - center) / math.sqrt(members - 1)
    weight = live_mask * weight_scale / (scale_rows * scale_rows)
    mismatch = (
        observed_rows[:, None] + math.sqrt(inflation) * scale_rows[:, None] * noise_rows - predicted
    )
    weighted = anomaly * weight[:, None]
    contract = (((0,), (0,)), ((), ()))
    gram_matrix = lax.dot_general(anomaly, weighted, contract, precision=lax.Precision.HIGHEST)
    cross_terms = lax.dot_general(weighted, mismatch, contract, precision=lax.Precision.HIGHEST)
    relative = mismatch / scale_rows[:, None]
    misfit_rows = live_mask * jnp.sqrt(jnp.mean(relative * relative, axis=1) + epsilon)
    return (gram_matrix, cross_terms, misfit_rows)


def solve_weights(gram_matrix, cross_terms):
    members = gram_matrix.shape[0]
    factor = jnp.linalg.cholesky(gram_matrix + inflation * jnp.eye(members, dtype=jnp.float32))
    return jax.scipy.linalg.cho_solve((factor, True), cross_terms)


def update_state(block, update_weights):
    state = block.astype(jnp.float32)
    members = state.shape[0]
    anomaly = (state - jnp.mean(state, axis=0, keepdims=True)) / math.sqrt(members - 1)
    moved = state + lax.dot_general(
        update_weights, anomaly, (((0,), (0,)), ((), ())), precision=lax.Precision.HIGHEST
    )
    return moved.astype(jnp.bfloat16)


def dense_body(
    amplitude_maps, kept_blocks, block_owner, observed, error_scale, perturbation, model_slab
):
    members, rows_here, map_width = amplitude_maps.shape
    devices = lax.axis_size("map")
    map_height = rows_here * devices
    table_w = dct_table(map_width)
    table_h = dct_table(map_height)
    rowwise = jnp.einsum(
        "ehw,kw->hke", amplitude_maps, table_w, preferred_element_type=jnp.float32
    ).astype(jnp.bfloat16)
    coefficients = jnp.einsum(
        "kh,hwe->wke",
        table_h,
        lax.all_to_all(rowwise, "map", split_axis=1, concat_axis=0, tiled=True),
        preferred_element_type=jnp.float32,
    ).astype(jnp.bfloat16)
    block_rows = coefficients.reshape(-1, BLK * members)
    candidates = block_rows.shape[0]
    keep_count = kept_blocks.shape[0]
    slot_count = devices * CAP
    dest_owner = block_owner[:, 0]
    positions = jnp.arange(keep_count, dtype=jnp.int32)
    earlier = (dest_owner[:, None] == dest_owner[None, :]) & (
        positions[None, :] < positions[:, None]
    )
    slot_rank = jnp.sum(earlier.astype(jnp.int32), axis=1)
    slot_index = dest_owner * CAP + slot_rank
    pick_slot = (slot_index[:, None] == jnp.arange(slot_count, dtype=jnp.int32)[None, :]).astype(
        jnp.bfloat16
    )
    weight_scale = members / (devices * keep_count * BLK)
    contract = (((0,), (0,)), ((), ()))
    pick_block = (kept_blocks[:, None] == jnp.arange(candidates, dtype=jnp.int32)[None, :]).astype(
        jnp.bfloat16
    )
    routing = lax.dot_general(
        pick_slot, pick_block, contract, preferred_element_type=jnp.float32
    ).astype(jnp.bfloat16)
    outgoing = jnp.dot(routing, block_rows, preferred_element_type=jnp.float32).astype(jnp.bfloat16)
    live_slots = jnp.sum(pick_slot.astype(jnp.float32), axis=0).astype(jnp.bfloat16)
    arrived, arrived_live = (
        lax.all_to_all(
            outgoing.reshape(devices, CAP, BLK * members),
            "map",
            split_axis=0,
            concat_axis=0,
            tiled=True,
        ),
        lax.all_to_all(
            live_slots.reshape(devices, CAP), "map", split_axis=0, concat_axis=0, tiled=True
        ),
    )
    predicted = arrived.reshape(-1, members).astype(jnp.float32)
    live_mask = jnp.repeat(arrived_live.astype(jnp.float32).reshape(-1), BLK)
    gram_matrix, cross_terms, data_misfit = gram_terms(
        predicted,
        observed.astype(jnp.float32),
        error_scale.astype(jnp.float32),
        perturbation.astype(jnp.float32),
        live_mask,
        weight_scale,
    )
    gram_matrix, cross_terms = lax.psum((gram_matrix, cross_terms), "map")
    update_weights = solve_weights(gram_matrix, cross_terms)
    updated_slab = update_state(model_slab, update_weights)
    return (updated_slab, update_weights, data_misfit)


def swap(value, delta):
    pairs = [(i, i ^ delta) for i in range(lax.axis_size("map"))]
    return lax.ppermute(value, "map", pairs)


def by_row_kernel(maps_ref, out_ref):
    out_ref[...] = jnp.swapaxes(maps_ref[...], 0, 1)


def by_row(amplitude_maps):
    members, rows, width = amplitude_maps.shape
    return pl.pallas_call(
        by_row_kernel,
        grid=(width // LANE,),
        in_specs=[pl.BlockSpec((members, rows, LANE), lambda i: (0, 0, i))],
        out_specs=pl.BlockSpec((rows, members, LANE), lambda i: (0, 0, i)),
        out_shape=jax.ShapeDtypeStruct((rows, members, width), jnp.bfloat16),
        compiler_params=pltpu.CompilerParams(vmem_limit_bytes=VMEM_LIMIT),
        cost_estimate=pl.CostEstimate(
            flops=0, bytes_accessed=4 * members * rows * width, transcendentals=0
        ),
        name="maps_by_row",
    )(amplitude_maps)


def shares_kernel(
    starts_ref, place_ref, maps_ref, column_ref, table_w_ref, table_h_ref,
    k0_ref, k1_ref, s0_ref, s1_ref,
    pick_ref, row_ref, spread_ref, wide_ref,
):
    step = pl.program_id(0)
    rows, members, width = maps_ref.shape
    keep = row_ref.shape[1] // (rows * pl.num_programs(0))
    devices = row_ref.shape[0]
    depth = row_ref.shape[1]
    me = place_ref[0]

    @pl.when(step == 0)
    def _():
        height = table_h_ref.shape[1]
        sample = lax.broadcasted_iota(jnp.int32, (height, depth), 0) - me * (depth // keep)
        held = lax.broadcasted_iota(jnp.int32, (height, depth), 1) // keep
        spread_ref[...] = jnp.dot(
            table_h_ref[...], (sample == held).astype(jnp.bfloat16),
            preferred_element_type=jnp.float32,
        )
        lanes = lax.broadcasted_iota(jnp.int32, (column_ref.shape[0], width), 1)
        one_hot = (column_ref[...] == lanes).astype(jnp.bfloat16)
        pick_ref[...] = jnp.dot(
            one_hot, table_w_ref[...], preferred_element_type=jnp.float32
        ).astype(jnp.bfloat16)

    for row in range(rows):
        rowwise = lax.dot_general(
            pick_ref[...], maps_ref[row], (((1,), (1,)), ((), ())),
            preferred_element_type=jnp.float32,
        ).astype(jnp.bfloat16)
        place = pl.ds(pl.multiple_of((step * rows + row) * keep, keep), keep)
        row_ref[:, place, :] = rowwise.reshape(devices, keep, members)

    @pl.when(step == pl.num_programs(0) - 1)
    def _():
        position = lax.broadcasted_iota(jnp.int32, (BLK, depth), 1) % keep
        outs = ((k0_ref, 0), (k1_ref, 2), (s0_ref, 1), (s1_ref, 3))
        for out_ref, low in outs:
            for high in range(out_ref.shape[0]):
                delta = high * 4 + low
                for p in range(keep):
                    start = pl.multiple_of(starts_ref[(me ^ delta) * keep + p], BLK)
                    block = spread_ref[pl.ds(start, BLK), :]
                    wide_ref[pl.ds(p * BLK, BLK), :] = jnp.where(position == p, block, 0.0)
                share = jnp.dot(
                    wide_ref[...].astype(jnp.bfloat16), row_ref[me ^ delta],
                    preferred_element_type=jnp.float32,
                )
                out_ref[high] = share.T


def shares(maps, columns, starts, place, table_w, table_h):
    rows, members, width = maps.shape
    kept = columns.shape[0]
    devices = lax.axis_size("map")
    keep = kept // devices
    steps = 4
    depth = rows * keep
    out = jax.ShapeDtypeStruct((devices // 4, members, keep * BLK), jnp.float32)
    whole = lambda *shape: pl.BlockSpec(shape, lambda i, s, t: (0,) * len(shape))
    return pl.pallas_call(
        shares_kernel,
        grid_spec=pltpu.PrefetchScalarGridSpec(
            num_scalar_prefetch=2,
            grid=(steps,),
            in_specs=[
                pl.BlockSpec((rows // steps, members, width), lambda i, s, t: (i, 0, 0)),
                whole(kept, 1),
                whole(*table_w.shape),
                whole(*table_h.shape),
            ],
            out_specs=[whole(*out.shape)] * 4,
            scratch_shapes=[
                pltpu.VMEM((kept, width), jnp.bfloat16),
                pltpu.VMEM((devices, depth, members), jnp.bfloat16),
                pltpu.VMEM((table_h.shape[0], depth), jnp.float32),
                pltpu.VMEM((keep * BLK, depth), jnp.float32),
            ],
        ),
        out_shape=[out] * 4,
        compiler_params=pltpu.CompilerParams(vmem_limit_bytes=VMEM_LIMIT),
        cost_estimate=pl.CostEstimate(
            flops=2 * kept * width * rows * members,
            bytes_accessed=2 * rows * members * width,
            transcendentals=0,
        ),
        name="coefficient_shares",
    )(starts, place, maps, columns, table_w, table_h)


def gram_kernel(
    starts_ref, place_ref, target_ref, *refs
):
    predicted_refs, noise_refs = refs[:8], refs[8:10]
    out_ref, predicted_ref, wide_ref, noise_ref, left_ref, right_ref, misfit_ref = refs[10:]
    groups, members, per = predicted_ref.shape
    keep = per // BLK
    coefficients = groups * per
    weight_scale = members / (2 * coefficients)
    chip = place_ref[0]
    for i, ref in enumerate(predicted_refs):
        predicted_ref[chip ^ i] = ref[...].astype(jnp.float32)
    span = wide_ref.shape[0] // len(noise_refs)
    for i, ref in enumerate(noise_refs):
        wide_ref[pl.ds(i * span, span), :] = ref[...].reshape(span, -1).astype(jnp.float32)
    right_ref[...] = jnp.zeros_like(right_ref)
    for g in range(groups):
        for p in range(keep):
            start = pl.multiple_of(starts_ref[g * keep + p], BLK)
            noise_ref[pl.ds(p * BLK, BLK), :] = wide_ref[pl.ds(start, BLK), :]
        noise = noise_ref[...].T
        observed = noise[members : members + 1]
        scale = noise[members + 1 : members + 2]
        predicted = predicted_ref[g]
        center = jnp.sum(predicted, axis=0, keepdims=True) * (1.0 / members)
        anomaly = (predicted - center) * (1.0 / math.sqrt(members - 1))
        weight = weight_scale / (scale * scale)
        mismatch = observed + math.sqrt(inflation) * scale * noise[:members] - predicted
        here = pl.ds(g * per, per)
        left_ref[:, here] = anomaly * weight
        right_ref[0:members, here] = anomaly
        right_ref[256 : 256 + members, here] = mismatch
        relative = mismatch / scale
        misfit = jnp.sqrt(
            jnp.sum(relative * relative, axis=0, keepdims=True) * (1.0 / members) + epsilon
        )
        high = misfit.astype(jnp.bfloat16)
        rest = misfit - high.astype(jnp.float32)
        middle = rest.astype(jnp.bfloat16)
        low = (rest - middle.astype(jnp.float32)).astype(jnp.bfloat16)
        misfit_ref[0:1, here] = high.astype(jnp.float32)
        misfit_ref[1:2, here] = middle.astype(jnp.float32)
        misfit_ref[2:3, here] = low.astype(jnp.float32)
        misfit_ref[3:8, here] = jnp.zeros((5, per), jnp.float32)
    out_ref[0:members, :] = lax.dot_general(
        left_ref[...], right_ref[...], (((1,), (1,)), ((), ())),
        precision=lax.Precision.HIGHEST, preferred_element_type=jnp.float32,
    )
    lanes = lax.broadcasted_iota(jnp.int32, (coefficients, out_ref.shape[1]), 1)
    one_hot = (target_ref[...] == lanes).astype(jnp.bfloat16)
    routed = jnp.dot(
        misfit_ref[...].astype(jnp.bfloat16), one_hot, preferred_element_type=jnp.float32
    )
    out_ref[members : members + 8, :] = jnp.broadcast_to(
        routed[0:1] + routed[1:2] + routed[2:3], (8, out_ref.shape[1])
    )


def gram(starts, place, target, predicted, noise):
    members, per = predicted[0].shape
    groups = len(predicted)
    coefficients = groups * per
    rows = len(noise) * math.prod(noise[0].shape[:-1])
    smem = pl.BlockSpec(memory_space=pltpu.SMEM)
    vmem = pl.BlockSpec(memory_space=pltpu.VMEM)
    return pl.pallas_call(
        gram_kernel,
        in_specs=[smem, smem] + [vmem] * (1 + len(predicted) + len(noise)),
        out_specs=vmem,
        out_shape=jax.ShapeDtypeStruct((members + 8, 512), jnp.float32),
        scratch_shapes=[
            pltpu.VMEM((groups, members, per), jnp.float32),
            pltpu.VMEM((rows, 256), jnp.float32),
            pltpu.VMEM((per, 256), jnp.float32),
            pltpu.VMEM((members, coefficients), jnp.float32),
            pltpu.VMEM((512, coefficients), jnp.float32),
            pltpu.VMEM((8, coefficients), jnp.float32),
        ],
        compiler_params=pltpu.CompilerParams(vmem_limit_bytes=VMEM_LIMIT),
        name="gram_and_cross",
    )(starts, place, target, *predicted, *noise)


def solve_kernel(mine_ref, other_ref, weights_ref, parts_ref, lean_ref, misfit_ref, state_ref):
    members = weights_ref.shape[0]
    total = mine_ref[0:members, :] + other_ref[0:members, :]
    misfit_ref[...] = (
        mine_ref[members : members + 1, 0:256] + other_ref[members : members + 1, 256:512]
    )
    row = lax.broadcasted_iota(jnp.int32, (members, 256), 0)
    lane = lax.broadcasted_iota(jnp.int32, (members, 256), 1)
    unit = jnp.where(row == lane, 1.0, 0.0)
    matrix = total[:, 0:256] + inflation * unit
    bound = jnp.max(jnp.sum(jnp.abs(matrix), axis=1, keepdims=True), axis=0, keepdims=True)
    step = 2.0 / (inflation + bound)
    state_ref[members:256, :] = jnp.zeros((256 - members, 512), jnp.float32)
    state_ref[0:members, 0:256] = unit - step * matrix
    state_ref[0:members, 256:512] = step * total[:, 256:512]

    def more(carry):
        return carry[0] > 2.0**-24

    def double(carry):
        power = state_ref[:, 0:256]
        size = jnp.sum(power * power)
        moved = jnp.dot(
            power, state_ref[...], precision=lax.Precision.HIGHEST,
            preferred_element_type=jnp.float32,
        )
        state_ref[:, 0:256] = moved[:, 0:256]
        state_ref[:, 256:512] = state_ref[:, 256:512] + moved[:, 256:512]
        return (size,)

    lax.while_loop(more, double, (jnp.float32(1.0),))
    weights = state_ref[0:members, 256 : 256 + members]
    weights_ref[...] = weights
    full = state_ref[:, 256:512]
    center = jnp.sum(full, axis=0, keepdims=True) * (1.0 / members)
    spread = ((full - center) * (1.0 / math.sqrt(members - 1))).T[0:members, 0:members]
    high = spread.astype(jnp.bfloat16)
    low = (spread - high.astype(jnp.float32)).astype(jnp.bfloat16)
    kept = high.astype(jnp.float32) + low.astype(jnp.float32)
    lean_ref[...] = jnp.broadcast_to(jnp.sum(kept, axis=1, keepdims=True), lean_ref.shape)
    ones = jnp.ones((16, members), jnp.float32)
    parts_ref[...] = jnp.concatenate(
        [high.astype(jnp.float32), low.astype(jnp.float32), ones], axis=0
    ).astype(jnp.bfloat16)


def solve(mine, other):
    members = mine.shape[0] - 8
    vmem = pl.BlockSpec(memory_space=pltpu.VMEM)
    return pl.pallas_call(
        solve_kernel,
        in_specs=[vmem, vmem],
        out_specs=[vmem] * 4,
        out_shape=[
            jax.ShapeDtypeStruct((members, members), jnp.float32),
            jax.ShapeDtypeStruct((2 * members + 16, members), jnp.bfloat16),
            jax.ShapeDtypeStruct((members, LANE), jnp.float32),
            jax.ShapeDtypeStruct((1, 256), jnp.float32),
        ],
        scratch_shapes=[pltpu.VMEM((256, 512), jnp.float32)],
        compiler_params=pltpu.CompilerParams(vmem_limit_bytes=VMEM_LIMIT),
        name="solve_weights",
    )(mine, other)


def slab_kernel(parts_ref, lean_ref, slab_ref, out_ref):
    members = slab_ref.shape[0]
    state = slab_ref[...]
    moved = jnp.dot(parts_ref[...], state, preferred_element_type=jnp.float32)
    center = moved[2 * members : 2 * members + 1] * (1.0 / members)
    moved = moved[0:members] + (moved[members : 2 * members] - lean_ref[:, 0:1] * center)
    out_ref[...] = (state.astype(jnp.float32) + moved).astype(jnp.bfloat16)


def move_slab(parts, lean, slab):
    members, cells = slab.shape
    tile = 2048
    return pl.pallas_call(
        slab_kernel,
        grid=(cells // tile,),
        in_specs=[
            pl.BlockSpec(parts.shape, lambda i: (0, 0)),
            pl.BlockSpec(lean.shape, lambda i: (0, 0)),
            pl.BlockSpec((members, tile), lambda i: (0, i)),
        ],
        out_specs=pl.BlockSpec((members, tile), lambda i: (0, i)),
        out_shape=jax.ShapeDtypeStruct(slab.shape, slab.dtype),
        compiler_params=pltpu.CompilerParams(vmem_limit_bytes=VMEM_LIMIT),
        name="slab_update",
    )(parts, lean, slab)


def sparse_body(
    amplitude_maps, kept_blocks, block_owner, observed, error_scale, perturbation, model_slab
):
    members, rows_here, map_width = amplitude_maps.shape
    devices = lax.axis_size("map")
    map_height = rows_here * devices
    per_column = map_height // BLK
    columns_here = map_width // devices
    keep = kept_blocks.shape[0]
    slots = observed.shape[0]
    me = lax.axis_index("map").astype(jnp.int32)

    core, chip = me & 1, me >> 1

    lists = jnp.stack([kept_blocks, block_owner[:, 0]]).reshape(1, -1)
    lists = lax.all_to_all(
        jnp.broadcast_to(lists, (devices, 2 * keep)), "map", split_axis=0, concat_axis=0, tiled=True
    ).reshape(devices, 2, keep)
    blocks, owner = lists[:, 0], lists[:, 1]

    extra = jnp.zeros((slots, 256 - members - 2), jnp.bfloat16)
    noise = jnp.concatenate(
        [perturbation, observed[:, None], error_scale[:, None], extra], axis=1
    ).reshape(devices // 2, 2, CAP * BLK, 256)
    noise_keep = lax.dynamic_index_in_dim(noise, core, 1, keepdims=False)
    noise_send = lax.dynamic_index_in_dim(noise, 1 - core, 1, keepdims=False)
    noise = jnp.stack([noise_keep, swap(noise_send, 1)]).reshape(slots, 256)
    noises = [noise] + [swap(noise, 4 * i) for i in range(1, devices // 4)]

    maps = by_row(amplitude_maps)
    table_w = jnp.asarray(dct_constant(map_width))
    table_h = table_w if map_height == map_width else jnp.asarray(dct_constant(map_height))
    device = jnp.arange(devices, dtype=jnp.int32)
    columns = device[:, None] * columns_here + blocks // per_column
    starts = (blocks % per_column * BLK).reshape(-1)
    keep_0, keep_1, send_0, send_1 = shares(
        maps, columns.reshape(-1, 1), starts, me.reshape(1), table_w, table_h
    )

    share_1 = keep_1 + swap(send_1, 1)
    got_1 = swap(share_1, 2)
    share_0 = keep_0 + swap(send_0, 1)
    share = [share_0[i] + got_1[i] for i in range(devices // 4)]
    share, noises = lax.optimization_barrier((share, noises))
    near_noise = jnp.stack(noises)
    far_noise = swap(near_noise, 2)
    got = [swap(share[i], 4 * i) for i in range(1, devices // 4)]
    predicted = (share[0] + got[0] + got[1] + got[2]).astype(jnp.bfloat16)
    predicted, far_noise = lax.optimization_barrier((predicted, far_noise))

    near = [predicted] + [swap(predicted, 4 * i) for i in range(1, devices // 4)]
    gathered = []
    for value in near:
        gathered += [value, swap(value, 2)]

    positions = jnp.arange(keep, dtype=jnp.int32)
    earlier = (owner[:, :, None] == owner[:, None, :]) & (
        positions[None, None, :] < positions[None, :, None]
    )
    rank = jnp.sum(earlier.astype(jnp.int32), axis=2)
    pairs = jnp.stack([owner, rank]).reshape(2, devices // 2, 2, keep)
    owner, rank = lax.dynamic_index_in_dim(pairs, core, 2, keepdims=False)
    chips = jnp.arange(devices // 2, dtype=jnp.int32)[:, None]
    away = owner ^ me
    held = (away >> 1 & 1) * 8 + (away >> 2) * 2 + (away & 1)
    noise_rows = held * (slots // 2) + chips * (CAP * BLK) + rank * BLK
    data_row = (chips * 2 + core) * (CAP * BLK) + rank * BLK
    target = jnp.where(away < 2, away * slots + data_row, -1024)
    target = (target[:, :, None] + jnp.arange(BLK, dtype=jnp.int32)).reshape(-1, 1)

    mine = gram(
        noise_rows.reshape(-1), chip.reshape(1), target, gathered, [near_noise, far_noise]
    )
    update_weights, parts, lean, data_misfit = solve(mine, swap(mine, 1))
    updated_slab = move_slab(parts, lean, model_slab)
    return (updated_slab, update_weights, data_misfit.reshape(-1))


def solution(mesh):
    in_specs = (
        P("groups", "map", None),
        P(("groups", "map")),
        P(("groups", "map"), None),
        P(("groups", "map")),
        P(("groups", "map")),
        P(("groups", "map"), None),
        P(None, ("groups", "map")),
    )
    out_specs = (P(None, ("groups", "map")), P("groups", None), P(("groups", "map")))

    def body(amplitude_maps, kept_blocks, *rest):
        few = mesh.shape["map"] == 16 and kept_blocks.shape[0] * BLK == LANE
        chosen = sparse_body if few else dense_body
        return chosen(amplitude_maps, kept_blocks, *rest)

    return jax.shard_map(body, mesh=mesh, in_specs=in_specs, out_specs=out_specs, check_vma=False)
```

```python
import math

import jax
import jax.numpy as jnp
import numpy as np
from jax import lax
from jax.experimental import pallas as pl
from jax.experimental.pallas import tpu as pltpu
from jax.sharding import PartitionSpec as P

BLK = 8
CAP = 2
LANE = 128

inflation = 4.0
epsilon = 1e-06

VMEM_LIMIT = 24 * 1024 * 1024
MAPS_LIMIT = 44 * 1024 * 1024
SLAB_LIMIT = 50 * 1024 * 1024


def dct_table(length):
    frequency = jnp.arange(length, dtype=jnp.float32)[:, None]
    sample = jnp.arange(length, dtype=jnp.float32)[None, :]
    cosine_table = jnp.cos(math.pi * (2.0 * sample + 1.0) * frequency / (2.0 * length))
    factor = jnp.where(frequency == 0, math.sqrt(1.0 / length), math.sqrt(2.0 / length))
    return (cosine_table * factor).astype(jnp.bfloat16)


def dct_constant(length):
    frequency = np.arange(length, dtype=np.float32)[:, None]
    sample = np.arange(length, dtype=np.float32)[None, :]
    angle = np.float32(math.pi) * (np.float32(2.0) * sample + np.float32(1.0)) * frequency
    cosine_table = np.cos(angle / np.float32(2.0 * length))
    factor = np.where(
        frequency == 0, np.float32(math.sqrt(1.0 / length)), np.float32(math.sqrt(2.0 / length))
    )
    return (cosine_table * factor).astype(jnp.bfloat16)


def gram_terms(predicted, observed_rows, scale_rows, noise_rows, live_mask, weight_scale):
    members = predicted.shape[1]
    center = jnp.mean(predicted, axis=1, keepdims=True)
    anomaly = (predicted - center) / math.sqrt(members - 1)
    weight = live_mask * weight_scale / (scale_rows * scale_rows)
    mismatch = (
        observed_rows[:, None] + math.sqrt(inflation) * scale_rows[:, None] * noise_rows - predicted
    )
    weighted = anomaly * weight[:, None]
    contract = (((0,), (0,)), ((), ()))
    gram_matrix = lax.dot_general(anomaly, weighted, contract, precision=lax.Precision.HIGHEST)
    cross_terms = lax.dot_general(weighted, mismatch, contract, precision=lax.Precision.HIGHEST)
    relative = mismatch / scale_rows[:, None]
    misfit_rows = live_mask * jnp.sqrt(jnp.mean(relative * relative, axis=1) + epsilon)
    return (gram_matrix, cross_terms, misfit_rows)


def solve_weights(gram_matrix, cross_terms):
    members = gram_matrix.shape[0]
    factor = jnp.linalg.cholesky(gram_matrix + inflation * jnp.eye(members, dtype=jnp.float32))
    return jax.scipy.linalg.cho_solve((factor, True), cross_terms)


def update_state(block, update_weights):
    state = block.astype(jnp.float32)
    members = state.shape[0]
    anomaly = (state - jnp.mean(state, axis=0, keepdims=True)) / math.sqrt(members - 1)
    moved = state + lax.dot_general(
        update_weights, anomaly, (((0,), (0,)), ((), ())), precision=lax.Precision.HIGHEST
    )
    return moved.astype(jnp.bfloat16)


def dense_body(
    amplitude_maps, kept_blocks, block_owner, observed, error_scale, perturbation, model_slab
):
    members, rows_here, map_width = amplitude_maps.shape
    devices = lax.axis_size("map")
    map_height = rows_here * devices
    table_w = dct_table(map_width)
    table_h = dct_table(map_height)
    rowwise = jnp.einsum(
        "ehw,kw->hke", amplitude_maps, table_w, preferred_element_type=jnp.float32
    ).astype(jnp.bfloat16)
    coefficients = jnp.einsum(
        "kh,hwe->wke",
        table_h,
        lax.all_to_all(rowwise, "map", split_axis=1, concat_axis=0, tiled=True),
        preferred_element_type=jnp.float32,
    ).astype(jnp.bfloat16)
    block_rows = coefficients.reshape(-1, BLK * members)
    candidates = block_rows.shape[0]
    keep_count = kept_blocks.shape[0]
    slot_count = devices * CAP
    dest_owner = block_owner[:, 0]
    positions = jnp.arange(keep_count, dtype=jnp.int32)
    earlier = (dest_owner[:, None] == dest_owner[None, :]) & (
        positions[None, :] < positions[:, None]
    )
    slot_rank = jnp.sum(earlier.astype(jnp.int32), axis=1)
    slot_index = dest_owner * CAP + slot_rank
    pick_slot = (slot_index[:, None] == jnp.arange(slot_count, dtype=jnp.int32)[None, :]).astype(
        jnp.bfloat16
    )
    weight_scale = members / (devices * keep_count * BLK)
    contract = (((0,), (0,)), ((), ()))
    pick_block = (kept_blocks[:, None] == jnp.arange(candidates, dtype=jnp.int32)[None, :]).astype(
        jnp.bfloat16
    )
    routing = lax.dot_general(
        pick_slot, pick_block, contract, preferred_element_type=jnp.float32
    ).astype(jnp.bfloat16)
    outgoing = jnp.dot(routing, block_rows, preferred_element_type=jnp.float32).astype(jnp.bfloat16)
    live_slots = jnp.sum(pick_slot.astype(jnp.float32), axis=0).astype(jnp.bfloat16)
    arrived, arrived_live = (
        lax.all_to_all(
            outgoing.reshape(devices, CAP, BLK * members),
            "map",
            split_axis=0,
            concat_axis=0,
            tiled=True,
        ),
        lax.all_to_all(
            live_slots.reshape(devices, CAP), "map", split_axis=0, concat_axis=0, tiled=True
        ),
    )
    predicted = arrived.reshape(-1, members).astype(jnp.float32)
    live_mask = jnp.repeat(arrived_live.astype(jnp.float32).reshape(-1), BLK)
    gram_matrix, cross_terms, data_misfit = gram_terms(
        predicted,
        observed.astype(jnp.float32),
        error_scale.astype(jnp.float32),
        perturbation.astype(jnp.float32),
        live_mask,
        weight_scale,
    )
    gram_matrix, cross_terms = lax.psum((gram_matrix, cross_terms), "map")
    update_weights = solve_weights(gram_matrix, cross_terms)
    updated_slab = update_state(model_slab, update_weights)
    return (updated_slab, update_weights, data_misfit)


def swap(value, delta):
    pairs = [(i, i ^ delta) for i in range(lax.axis_size("map"))]
    return lax.ppermute(value, "map", pairs)


VMEM = pl.BlockSpec(memory_space=pltpu.VMEM)
SMEM = pl.BlockSpec(memory_space=pltpu.SMEM)
HBM = pl.BlockSpec(memory_space=pltpu.HBM)


def by_row_kernel(maps_ref, out_ref, held_ref, arrived):
    width = maps_ref.shape[2]
    copies = []
    for i in range(width // LANE):
        part = pl.ds(i * LANE, LANE)
        copies.append(
            pltpu.make_async_copy(maps_ref.at[:, :, part], held_ref.at[i], arrived.at[i])
        )
        copies[i].start()
    for i in range(width // LANE):
        copies[i].wait()
        out_ref[:, :, i * LANE : (i + 1) * LANE] = jnp.swapaxes(held_ref[i], 0, 1)


def by_row(amplitude_maps):
    members, rows, width = amplitude_maps.shape
    parts = width // LANE
    return pl.pallas_call(
        by_row_kernel,
        in_specs=[HBM],
        out_specs=VMEM,
        out_shape=jax.ShapeDtypeStruct((rows, members, width), jnp.bfloat16),
        scratch_shapes=[
            pltpu.VMEM((parts, members, rows, LANE), jnp.bfloat16),
            pltpu.SemaphoreType.DMA((parts,)),
        ],
        compiler_params=pltpu.CompilerParams(vmem_limit_bytes=MAPS_LIMIT),
        cost_estimate=pl.CostEstimate(
            flops=0, bytes_accessed=4 * members * rows * width, transcendentals=0
        ),
        name="maps_by_row",
    )(amplitude_maps)


def shares_kernel(
    list0_ref, list1_ref, list2_ref, list3_ref, place_ref, maps_ref, table_w_ref, table_h_ref, k0_ref, k1_ref, s0_ref, s1_ref,
    full_ref, pick_ref, row_ref, spread_ref, wide_ref,
):
    rows, members, width = maps_ref.shape
    devices, depth, _ = row_ref.shape
    keep = depth // rows
    height = table_h_ref.shape[0]
    per_column = height // BLK
    columns_here = width // devices
    me = place_ref[0]
    list_refs = (list0_ref, list1_ref, list2_ref, list3_ref)

    def block(delta, p):
        return list_refs[delta // 4][delta % 4, p]

    full_ref[...] = table_w_ref[...].astype(jnp.float32)
    for delta in range(devices):
        for p in range(keep):
            column = (me ^ delta) * columns_here + block(delta, p) // per_column
            pick_ref[pl.ds(delta * keep + p, 1), :] = full_ref[pl.ds(column, 1), :]
    sample = lax.broadcasted_iota(jnp.int32, (height, depth), 0) - me * rows
    held = lax.broadcasted_iota(jnp.int32, (height, depth), 1) // keep
    spread_ref[...] = jnp.dot(
        table_h_ref[...], (sample == held).astype(jnp.bfloat16), preferred_element_type=jnp.float32
    )

    pick = pick_ref[...].astype(jnp.bfloat16)
    for row in range(rows):
        rowwise = lax.dot_general(
            pick, maps_ref[row], (((1,), (1,)), ((), ())), preferred_element_type=jnp.float32
        ).astype(jnp.bfloat16)
        row_ref[:, row * keep : (row + 1) * keep, :] = rowwise.reshape(devices, keep, members)

    position = lax.broadcasted_iota(jnp.int32, (BLK, depth), 1) % keep
    for out_ref, low in ((s1_ref, 3), (k1_ref, 2), (s0_ref, 1), (k0_ref, 0)):
        for high in range(out_ref.shape[0]):
            delta = high * 4 + low
            for p in range(keep):
                start = pl.multiple_of(block(delta, p) % per_column * BLK, BLK)
                cosines = spread_ref[pl.ds(start, BLK), :]
                wide_ref[p * BLK : (p + 1) * BLK, :] = jnp.where(position == p, cosines, 0.0)
            share = jnp.dot(
                wide_ref[...].astype(jnp.bfloat16), row_ref[delta],
                preferred_element_type=jnp.float32,
            )
            out_ref[high] = share.T


def shares(lists, place, maps, table_w, table_h):
    rows, members, width = maps.shape
    devices = sum(part.shape[0] for part in lists)
    keep = lists[0].shape[1] // 2
    depth = rows * keep
    out = jax.ShapeDtypeStruct((devices // 4, members, keep * BLK), jnp.float32)
    return pl.pallas_call(
        shares_kernel,
        in_specs=[SMEM] * 5 + [VMEM] * 3,
        out_specs=[VMEM] * 4,
        out_shape=[out] * 4,
        scratch_shapes=[
            pltpu.VMEM(table_w.shape, jnp.float32),
            pltpu.VMEM((devices * keep, width), jnp.float32),
            pltpu.VMEM((devices, depth, members), jnp.bfloat16),
            pltpu.VMEM((table_h.shape[0], depth), jnp.float32),
            pltpu.VMEM((keep * BLK, depth), jnp.float32),
        ],
        compiler_params=pltpu.CompilerParams(vmem_limit_bytes=VMEM_LIMIT),
        cost_estimate=pl.CostEstimate(
            flops=2 * devices * keep * width * rows * members,
            bytes_accessed=2 * rows * members * width,
            transcendentals=0,
        ),
        name="coefficient_shares",
    )(*lists, place, maps, table_w, table_h)


def split_noise_kernel(place_ref, noise_ref, observed_ref, scale_ref, keep_ref, send_ref):
    members, slots = noise_ref.shape
    half = slots // 2
    core = place_ref[0] & 1
    span = 2 * CAP * BLK // 2
    row = lax.broadcasted_iota(jnp.int32, (slots, slots), 0)
    lane = lax.broadcasted_iota(jnp.int32, (slots, slots), 1)
    kind = lane // half ^ core
    source = lane % half // span * (2 * span) + kind * span + lane % span
    picked = (row == source).astype(jnp.bfloat16)
    extra = jnp.zeros((keep_ref.shape[0] - members - 2, slots), jnp.float32)
    value = jnp.concatenate(
        [
            noise_ref[...].astype(jnp.float32),
            observed_ref[...].astype(jnp.float32),
            scale_ref[...].astype(jnp.float32),
            extra,
        ],
        axis=0,
    ).astype(jnp.bfloat16)
    moved = jnp.dot(value, picked, preferred_element_type=jnp.float32).astype(jnp.bfloat16)
    keep_ref[...] = moved[:, 0:half]
    send_ref[...] = moved[:, half:slots]


def split_noise(place, noise, observed, scale):
    members, slots = noise.shape
    rows = -(-(members + 2) // 16) * 16
    out = jax.ShapeDtypeStruct((rows, slots // 2), jnp.bfloat16)
    return pl.pallas_call(
        split_noise_kernel,
        in_specs=[SMEM] + [VMEM] * 3,
        out_specs=[VMEM] * 2,
        out_shape=[out] * 2,
        compiler_params=pltpu.CompilerParams(vmem_limit_bytes=VMEM_LIMIT),
        name="split_noise",
    )(place, noise, observed, scale)


def select_noise_kernel(starts_ref, place_ref, near_ref, far_ref, out_ref, wide_ref, rows_ref):
    rows, per = near_ref.shape[-2:]
    chips = out_ref.shape[0]
    keep = per // BLK
    chip = place_ref[0]
    units = near_ref.shape[0] * near_ref.shape[1]
    wide_ref[:, rows:256] = jnp.zeros((wide_ref.shape[0], 256 - rows), jnp.float32)
    for i, ref in enumerate((near_ref, far_ref)):
        for z in range(near_ref.shape[0]):
            for c in range(near_ref.shape[1]):
                unit = i * units + z * near_ref.shape[1] + c
                wide_ref[unit * per : (unit + 1) * per, 0:rows] = ref[z, c].astype(jnp.float32).T
    for i in range(chips):
        for p in range(keep):
            start = pl.multiple_of(starts_ref[i * keep + p], BLK)
            rows_ref[p * BLK : (p + 1) * BLK, :] = wide_ref[pl.ds(start, BLK), :]
        out_ref[chip ^ i] = rows_ref[...].T[0:rows]


def select_noise(starts, place, near, far):
    rows, per = near.shape[-2:]
    chips = starts.shape[0] * BLK // per
    return pl.pallas_call(
        select_noise_kernel,
        in_specs=[SMEM, SMEM, VMEM, VMEM],
        out_specs=VMEM,
        out_shape=jax.ShapeDtypeStruct((chips, rows, per), jnp.float32),
        scratch_shapes=[
            pltpu.VMEM((2 * near.shape[0] * near.shape[1] * per, 256), jnp.float32),
            pltpu.VMEM((per, 256), jnp.float32),
        ],
        compiler_params=pltpu.CompilerParams(vmem_limit_bytes=VMEM_LIMIT),
        name="select_noise",
    )(starts, place, near, far)


def gram_kernel(place_ref, target_ref, noise_ref, *refs):
    predicted_refs = refs[:8]
    out_ref, predicted_ref, left_ref, right_ref, misfit_ref = refs[8:]
    groups, members, per = predicted_ref.shape
    coefficients = groups * per
    weight_scale = members / (2 * coefficients)
    chip = place_ref[0]
    for i, ref in enumerate(predicted_refs):
        predicted_ref[chip ^ i] = ref[...].astype(jnp.float32)
    right_ref[...] = jnp.zeros_like(right_ref)
    for g in range(groups):
        noise = noise_ref[g]
        observed = noise[members : members + 1]
        scale = noise[members + 1 : members + 2]
        predicted = predicted_ref[g]
        center = jnp.sum(predicted, axis=0, keepdims=True) * (1.0 / members)
        anomaly = (predicted - center) * (1.0 / math.sqrt(members - 1))
        weight = weight_scale / (scale * scale)
        mismatch = observed + math.sqrt(inflation) * scale * noise[:members] - predicted
        here = pl.ds(g * per, per)
        left_ref[:, here] = anomaly * weight
        right_ref[0:members, here] = anomaly
        right_ref[256 : 256 + members, here] = mismatch
        relative = mismatch / scale
        misfit = jnp.sqrt(
            jnp.sum(relative * relative, axis=0, keepdims=True) * (1.0 / members) + epsilon
        )
        high = misfit.astype(jnp.bfloat16)
        rest = misfit - high.astype(jnp.float32)
        middle = rest.astype(jnp.bfloat16)
        low = (rest - middle.astype(jnp.float32)).astype(jnp.bfloat16)
        misfit_ref[0:1, here] = high.astype(jnp.float32)
        misfit_ref[1:2, here] = middle.astype(jnp.float32)
        misfit_ref[2:3, here] = low.astype(jnp.float32)
        misfit_ref[3:8, here] = jnp.zeros((5, per), jnp.float32)
    out_ref[0:members, :] = lax.dot_general(
        left_ref[...], right_ref[...], (((1,), (1,)), ((), ())),
        precision=lax.Precision.HIGHEST, preferred_element_type=jnp.float32,
    )
    lanes = lax.broadcasted_iota(jnp.int32, (per, out_ref.shape[1]), 1)
    one_hot = jnp.concatenate(
        [(target_ref[chip ^ g] == lanes).astype(jnp.bfloat16) for g in range(groups)], axis=0
    )
    routed = jnp.dot(
        misfit_ref[...].astype(jnp.bfloat16), one_hot, preferred_element_type=jnp.float32
    )
    out_ref[members : members + 8, :] = jnp.broadcast_to(
        routed[0:1] + routed[1:2] + routed[2:3], (8, out_ref.shape[1])
    )


def gram(place, target, noise, predicted):
    members, per = predicted[0].shape
    groups = len(predicted)
    coefficients = groups * per
    return pl.pallas_call(
        gram_kernel,
        in_specs=[SMEM] + [VMEM] * (2 + len(predicted)),
        out_specs=VMEM,
        out_shape=jax.ShapeDtypeStruct((members + 8, 512), jnp.float32),
        scratch_shapes=[
            pltpu.VMEM((groups, members, per), jnp.float32),
            pltpu.VMEM((members, coefficients), jnp.float32),
            pltpu.VMEM((512, coefficients), jnp.float32),
            pltpu.VMEM((8, coefficients), jnp.float32),
        ],
        compiler_params=pltpu.CompilerParams(vmem_limit_bytes=VMEM_LIMIT),
        name="gram_and_cross",
    )(place, target, noise, *predicted)


def update_kernel(
    mine_ref, other_ref, slab_ref, out_ref, weights_ref, misfit_ref,
    state_ref, held_ref, arrived, left,
):
    members, cells = held_ref.shape
    tiles = arrived.shape[0]
    tile = cells // tiles
    parts = [pl.ds(i * tile, tile) for i in range(tiles)]
    reads = [
        pltpu.make_async_copy(slab_ref.at[:, part], held_ref.at[:, part], arrived.at[i])
        for i, part in enumerate(parts)
    ]
    writes = [
        pltpu.make_async_copy(held_ref.at[:, part], out_ref.at[:, part], left.at[i])
        for i, part in enumerate(parts)
    ]
    for read in reads:
        read.start()

    total = mine_ref[0:members, :] + other_ref[0:members, :]
    misfit_ref[...] = (
        mine_ref[members : members + 1, 0:256] + other_ref[members : members + 1, 256:512]
    )
    row = lax.broadcasted_iota(jnp.int32, (members, 256), 0)
    lane = lax.broadcasted_iota(jnp.int32, (members, 256), 1)
    unit = jnp.where(row == lane, 1.0, 0.0)
    matrix = total[:, 0:256] + inflation * unit
    bound = jnp.max(jnp.sum(jnp.abs(matrix), axis=1, keepdims=True), axis=0, keepdims=True)
    step = 2.0 / (inflation + bound)
    state_ref[members:256, :] = jnp.zeros((256 - members, 512), jnp.float32)
    state_ref[0:members, 0:256] = unit - step * matrix
    state_ref[0:members, 256:512] = step * total[:, 256:512]

    def more(carry):
        return carry[0] > 2.0**-24

    def double(carry):
        power = state_ref[:, 0:256]
        size = jnp.sum(power * power)
        moved = jnp.dot(
            power, state_ref[...], precision=lax.Precision.HIGHEST,
            preferred_element_type=jnp.float32,
        )
        state_ref[:, 0:256] = moved[:, 0:256]
        state_ref[:, 256:512] = state_ref[:, 256:512] + moved[:, 256:512]
        return (size,)

    lax.while_loop(more, double, (jnp.float32(1.0),))
    weights_ref[...] = state_ref[0:members, 256 : 256 + members]

    full = state_ref[:, 256:512]
    center = jnp.sum(full, axis=0, keepdims=True) * (1.0 / members)
    spread = ((full - center) * (1.0 / math.sqrt(members - 1))).T[0:members, 0:members]
    high = spread.astype(jnp.bfloat16)
    rest = spread - high.astype(jnp.float32)
    middle = rest.astype(jnp.bfloat16)
    low = (rest - middle.astype(jnp.float32)).astype(jnp.bfloat16)
    for i in range(tiles):
        reads[i].wait()
        for j in range(i * tile, (i + 1) * tile, 256):
            state = held_ref[:, j : j + 256]
            moved = jnp.dot(low, state, preferred_element_type=jnp.float32)
            moved = moved + jnp.dot(middle, state, preferred_element_type=jnp.float32)
            moved = moved + jnp.dot(high, state, preferred_element_type=jnp.float32)
            held_ref[:, j : j + 256] = (state.astype(jnp.float32) + moved).astype(jnp.bfloat16)
        writes[i].start()
    for write in writes:
        write.wait()


def update(mine, other, slab):
    members, cells = slab.shape
    tiles = cells // 1024
    return pl.pallas_call(
        update_kernel,
        in_specs=[VMEM, VMEM, HBM],
        out_specs=[HBM, VMEM, VMEM],
        out_shape=[
            jax.ShapeDtypeStruct(slab.shape, slab.dtype),
            jax.ShapeDtypeStruct((members, members), jnp.float32),
            jax.ShapeDtypeStruct((1, 256), jnp.float32),
        ],
        scratch_shapes=[
            pltpu.VMEM((256, 512), jnp.float32),
            pltpu.VMEM(slab.shape, slab.dtype),
            pltpu.SemaphoreType.DMA((tiles,)),
            pltpu.SemaphoreType.DMA((tiles,)),
        ],
        compiler_params=pltpu.CompilerParams(vmem_limit_bytes=SLAB_LIMIT),
        name="solve_and_update",
    )(mine, other, slab)


def sparse_body(
    amplitude_maps, kept_blocks, block_owner, observed, error_scale, perturbation, model_slab
):
    members, rows_here, map_width = amplitude_maps.shape
    devices = lax.axis_size("map")
    map_height = rows_here * devices
    keep = kept_blocks.shape[0]
    slots = observed.shape[0]
    me = lax.axis_index("map").astype(jnp.int32)
    core, chip = me & 1, me >> 1

    lists = jnp.concatenate([kept_blocks, block_owner[:, 0]])
    lists = jnp.stack([lists] + [swap(lists, delta) for delta in range(1, 4)])

    noise_keep, noise_send = split_noise(
        me.reshape(1), perturbation.T, observed[None, :], error_scale[None, :]
    )
    noise = jnp.stack([noise_keep, swap(noise_send, 1)])
    amplitude_maps, noise, lists = lax.optimization_barrier((amplitude_maps, noise, lists))
    lists = [lists] + [swap(lists, 4 * i) for i in range(1, devices // 4)]
    noises = [noise] + [swap(noise, 4 * i) for i in range(1, devices // 4)]

    maps = by_row(amplitude_maps)
    table_w = jnp.asarray(dct_constant(map_width))
    table_h = table_w if map_height == map_width else jnp.asarray(dct_constant(map_height))
    keep_0, keep_1, send_0, send_1 = shares(lists, me.reshape(1), maps, table_w, table_h)

    share_1 = keep_1 + swap(send_1, 1)
    got_1 = swap(share_1, 2)
    share_0 = keep_0 + swap(send_0, 1)
    share = [share_0[i] + got_1[i] for i in range(devices // 4)]
    share, noises = lax.optimization_barrier((share, noises))
    near_noise = jnp.stack(noises)
    far_noise = swap(near_noise, 2)
    got = [swap(share[i], 4 * i) for i in range(1, devices // 4)]
    predicted = (share[0] + got[0] + got[1] + got[2]).astype(jnp.bfloat16)
    predicted, far_noise = lax.optimization_barrier((predicted, far_noise))

    near = [predicted] + [swap(predicted, 4 * i) for i in range(1, devices // 4)]
    gathered = []
    for value in near:
        gathered += [value, swap(value, 2)]

    owner = jnp.concatenate(lists)[0::2, keep:]
    positions = jnp.arange(keep, dtype=jnp.int32)
    earlier = (owner[:, :, None] == owner[:, None, :]) & (
        positions[None, None, :] < positions[None, :, None]
    )
    rank = jnp.sum(earlier.astype(jnp.int32), axis=2)
    chips = chip ^ jnp.arange(devices // 2, dtype=jnp.int32)[:, None]
    away = owner ^ me
    held = (away >> 1 & 1) * 8 + (away >> 2) * 2 + (away & 1)
    noise_rows = held * (slots // 2) + chips * (CAP * BLK) + rank * BLK
    data_row = (chips * 2 + core) * (CAP * BLK) + rank * BLK
    target = jnp.where(away < 2, away * slots + data_row, -1024)
    target = (target[:, :, None] + jnp.arange(BLK, dtype=jnp.int32)).reshape(
        devices // 2, keep * BLK, 1
    )
    noise = select_noise(noise_rows.reshape(-1), chip.reshape(1), near_noise, far_noise)
    mine = gram(chip.reshape(1), target, noise, gathered)
    updated_slab, update_weights, data_misfit = update(mine, swap(mine, 1), model_slab)
    return (updated_slab, update_weights, data_misfit.reshape(-1))


def solution(mesh):
    in_specs = (
        P("groups", "map", None),
        P(("groups", "map")),
        P(("groups", "map"), None),
        P(("groups", "map")),
        P(("groups", "map")),
        P(("groups", "map"), None),
        P(None, ("groups", "map")),
    )
    out_specs = (P(None, ("groups", "map")), P("groups", None), P(("groups", "map")))

    def body(amplitude_maps, kept_blocks, *rest):
        few = mesh.shape["map"] == 16 and kept_blocks.shape[0] * BLK == LANE
        chosen = sparse_body if few else dense_body
        return chosen(amplitude_maps, kept_blocks, *rest)

    return jax.shard_map(body, mesh=mesh, in_specs=in_specs, out_specs=out_specs, check_vma=False)
```

```python
import math

import jax
import jax.numpy as jnp
import numpy as np
from jax import lax
from jax.experimental import pallas as pl
from jax.experimental.pallas import tpu as pltpu
from jax.sharding import PartitionSpec as P

BLK = 8
CAP = 2
LANE = 128

inflation = 4.0
epsilon = 1e-06

VMEM_LIMIT = 24 * 1024 * 1024
MAPS_LIMIT = 44 * 1024 * 1024
SLAB_LIMIT = 50 * 1024 * 1024


def dct_table(length):
    frequency = jnp.arange(length, dtype=jnp.float32)[:, None]
    sample = jnp.arange(length, dtype=jnp.float32)[None, :]
    cosine_table = jnp.cos(math.pi * (2.0 * sample + 1.0) * frequency / (2.0 * length))
    factor = jnp.where(frequency == 0, math.sqrt(1.0 / length), math.sqrt(2.0 / length))
    return (cosine_table * factor).astype(jnp.bfloat16)


def dct_constant(length):
    frequency = np.arange(length, dtype=np.float32)[:, None]
    sample = np.arange(length, dtype=np.float32)[None, :]
    angle = np.float32(math.pi) * (np.float32(2.0) * sample + np.float32(1.0)) * frequency
    cosine_table = np.cos(angle / np.float32(2.0 * length))
    factor = np.where(
        frequency == 0, np.float32(math.sqrt(1.0 / length)), np.float32(math.sqrt(2.0 / length))
    )
    return (cosine_table * factor).astype(jnp.bfloat16)


def gram_terms(predicted, observed_rows, scale_rows, noise_rows, live_mask, weight_scale):
    members = predicted.shape[1]
    center = jnp.mean(predicted, axis=1, keepdims=True)
    anomaly = (predicted - center) / math.sqrt(members - 1)
    weight = live_mask * weight_scale / (scale_rows * scale_rows)
    mismatch = (
        observed_rows[:, None] + math.sqrt(inflation) * scale_rows[:, None] * noise_rows - predicted
    )
    weighted = anomaly * weight[:, None]
    contract = (((0,), (0,)), ((), ()))
    gram_matrix = lax.dot_general(anomaly, weighted, contract, precision=lax.Precision.HIGHEST)
    cross_terms = lax.dot_general(weighted, mismatch, contract, precision=lax.Precision.HIGHEST)
    relative = mismatch / scale_rows[:, None]
    misfit_rows = live_mask * jnp.sqrt(jnp.mean(relative * relative, axis=1) + epsilon)
    return (gram_matrix, cross_terms, misfit_rows)


def solve_weights(gram_matrix, cross_terms):
    members = gram_matrix.shape[0]
    factor = jnp.linalg.cholesky(gram_matrix + inflation * jnp.eye(members, dtype=jnp.float32))
    return jax.scipy.linalg.cho_solve((factor, True), cross_terms)


def update_state(block, update_weights):
    state = block.astype(jnp.float32)
    members = state.shape[0]
    anomaly = (state - jnp.mean(state, axis=0, keepdims=True)) / math.sqrt(members - 1)
    moved = state + lax.dot_general(
        update_weights, anomaly, (((0,), (0,)), ((), ())), precision=lax.Precision.HIGHEST
    )
    return moved.astype(jnp.bfloat16)


def dense_body(
    amplitude_maps, kept_blocks, block_owner, observed, error_scale, perturbation, model_slab
):
    members, rows_here, map_width = amplitude_maps.shape
    devices = lax.axis_size("map")
    map_height = rows_here * devices
    table_w = dct_table(map_width)
    table_h = dct_table(map_height)
    rowwise = jnp.einsum(
        "ehw,kw->hke", amplitude_maps, table_w, preferred_element_type=jnp.float32
    ).astype(jnp.bfloat16)
    coefficients = jnp.einsum(
        "kh,hwe->wke",
        table_h,
        lax.all_to_all(rowwise, "map", split_axis=1, concat_axis=0, tiled=True),
        preferred_element_type=jnp.float32,
    ).astype(jnp.bfloat16)
    block_rows = coefficients.reshape(-1, BLK * members)
    candidates = block_rows.shape[0]
    keep_count = kept_blocks.shape[0]
    slot_count = devices * CAP
    dest_owner = block_owner[:, 0]
    positions = jnp.arange(keep_count, dtype=jnp.int32)
    earlier = (dest_owner[:, None] == dest_owner[None, :]) & (
        positions[None, :] < positions[:, None]
    )
    slot_rank = jnp.sum(earlier.astype(jnp.int32), axis=1)
    slot_index = dest_owner * CAP + slot_rank
    pick_slot = (slot_index[:, None] == jnp.arange(slot_count, dtype=jnp.int32)[None, :]).astype(
        jnp.bfloat16
    )
    weight_scale = members / (devices * keep_count * BLK)
    contract = (((0,), (0,)), ((), ()))
    pick_block = (kept_blocks[:, None] == jnp.arange(candidates, dtype=jnp.int32)[None, :]).astype(
        jnp.bfloat16
    )
    routing = lax.dot_general(
        pick_slot, pick_block, contract, preferred_element_type=jnp.float32
    ).astype(jnp.bfloat16)
    outgoing = jnp.dot(routing, block_rows, preferred_element_type=jnp.float32).astype(jnp.bfloat16)
    live_slots = jnp.sum(pick_slot.astype(jnp.float32), axis=0).astype(jnp.bfloat16)
    arrived, arrived_live = (
        lax.all_to_all(
            outgoing.reshape(devices, CAP, BLK * members),
            "map",
            split_axis=0,
            concat_axis=0,
            tiled=True,
        ),
        lax.all_to_all(
            live_slots.reshape(devices, CAP), "map", split_axis=0, concat_axis=0, tiled=True
        ),
    )
    predicted = arrived.reshape(-1, members).astype(jnp.float32)
    live_mask = jnp.repeat(arrived_live.astype(jnp.float32).reshape(-1), BLK)
    gram_matrix, cross_terms, data_misfit = gram_terms(
        predicted,
        observed.astype(jnp.float32),
        error_scale.astype(jnp.float32),
        perturbation.astype(jnp.float32),
        live_mask,
        weight_scale,
    )
    gram_matrix, cross_terms = lax.psum((gram_matrix, cross_terms), "map")
    update_weights = solve_weights(gram_matrix, cross_terms)
    updated_slab = update_state(model_slab, update_weights)
    return (updated_slab, update_weights, data_misfit)


def swap(value, delta):
    pairs = [(i, i ^ delta) for i in range(lax.axis_size("map"))]
    return lax.ppermute(value, "map", pairs)


VMEM = pl.BlockSpec(memory_space=pltpu.VMEM)
SMEM = pl.BlockSpec(memory_space=pltpu.SMEM)
HBM = pl.BlockSpec(memory_space=pltpu.HBM)


def by_row_kernel(maps_ref, out_ref, held_ref, arrived):
    width = maps_ref.shape[2]
    copies = []
    for i in range(width // LANE):
        part = pl.ds(i * LANE, LANE)
        copies.append(
            pltpu.make_async_copy(maps_ref.at[:, :, part], held_ref.at[i], arrived.at[i])
        )
        copies[i].start()
    for i in range(width // LANE):
        copies[i].wait()
        out_ref[:, :, i * LANE : (i + 1) * LANE] = jnp.swapaxes(held_ref[i], 0, 1)


def by_row(amplitude_maps):
    members, rows, width = amplitude_maps.shape
    parts = width // LANE
    return pl.pallas_call(
        by_row_kernel,
        in_specs=[HBM],
        out_specs=VMEM,
        out_shape=jax.ShapeDtypeStruct((rows, members, width), jnp.bfloat16),
        scratch_shapes=[
            pltpu.VMEM((parts, members, rows, LANE), jnp.bfloat16),
            pltpu.SemaphoreType.DMA((parts,)),
        ],
        compiler_params=pltpu.CompilerParams(vmem_limit_bytes=MAPS_LIMIT),
        cost_estimate=pl.CostEstimate(
            flops=0, bytes_accessed=4 * members * rows * width, transcendentals=0
        ),
        name="maps_by_row",
    )(amplitude_maps)


def shares_kernel(
    list0_ref, list1_ref, list2_ref, list3_ref, place_ref, maps_ref, table_w_ref, table_h_ref, k0_ref, k1_ref, s0_ref, s1_ref,
    full_ref, pick_ref, row_ref, spread_ref,
):
    rows, members, width = maps_ref.shape
    devices, depth, _ = row_ref.shape
    keep = depth // rows
    height = table_h_ref.shape[0]
    per_column = height // BLK
    columns_here = width // devices
    me = place_ref[0]
    list_refs = (list0_ref, list1_ref, list2_ref, list3_ref)

    def block(delta, p):
        return list_refs[delta // 4][delta % 4, p]

    full_ref[...] = table_w_ref[...].astype(jnp.float32)
    for delta in range(devices):
        for p in range(keep):
            column = (me ^ delta) * columns_here + block(delta, p) // per_column
            pick_ref[pl.ds(delta * keep + p, 1), :] = full_ref[pl.ds(column, 1), :]
    sample = lax.broadcasted_iota(jnp.int32, (height, depth), 0) - me * rows
    held = lax.broadcasted_iota(jnp.int32, (height, depth), 1) // keep
    spread_ref[...] = jnp.dot(
        table_h_ref[...], (sample == held).astype(jnp.bfloat16), preferred_element_type=jnp.float32
    )

    pick = pick_ref[...].astype(jnp.bfloat16)
    for row in range(rows):
        rowwise = lax.dot_general(
            pick, maps_ref[row], (((1,), (1,)), ((), ())), preferred_element_type=jnp.float32
        ).astype(jnp.bfloat16)
        row_ref[:, row * keep : (row + 1) * keep, :] = rowwise.reshape(devices, keep, members)

    position = lax.broadcasted_iota(jnp.int32, (BLK, depth), 1) % keep
    for out_ref, low in ((s1_ref, 3), (k1_ref, 2), (s0_ref, 1), (k0_ref, 0)):
        for high in range(out_ref.shape[0]):
            delta = high * 4 + low
            wide = []
            for p in range(keep):
                start = pl.multiple_of(block(delta, p) % per_column * BLK, BLK)
                wide.append(jnp.where(position == p, spread_ref[pl.ds(start, BLK), :], 0.0))
            wide = jnp.concatenate(wide, axis=0).astype(jnp.bfloat16)
            out_ref[high] = jnp.dot(
                wide, row_ref[delta], preferred_element_type=jnp.float32
            ).T


def shares(lists, place, maps, table_w, table_h):
    rows, members, width = maps.shape
    devices = sum(part.shape[0] for part in lists)
    keep = lists[0].shape[1] // 2
    depth = rows * keep
    out = jax.ShapeDtypeStruct((devices // 4, members, keep * BLK), jnp.float32)
    return pl.pallas_call(
        shares_kernel,
        in_specs=[SMEM] * 5 + [VMEM] * 3,
        out_specs=[VMEM] * 4,
        out_shape=[out] * 4,
        scratch_shapes=[
            pltpu.VMEM(table_w.shape, jnp.float32),
            pltpu.VMEM((devices * keep, width), jnp.float32),
            pltpu.VMEM((devices, depth, members), jnp.bfloat16),
            pltpu.VMEM((table_h.shape[0], depth), jnp.float32),
        ],
        compiler_params=pltpu.CompilerParams(vmem_limit_bytes=VMEM_LIMIT),
        cost_estimate=pl.CostEstimate(
            flops=2 * devices * keep * width * rows * members,
            bytes_accessed=2 * rows * members * width,
            transcendentals=0,
        ),
        name="coefficient_shares",
    )(*lists, place, maps, table_w, table_h)


def split_noise_kernel(place_ref, noise_ref, data_ref, keep_ref, send_ref):
    members, slots = noise_ref.shape
    half = slots // 2
    core = place_ref[0] & 1
    span = 2 * CAP * BLK // 2
    row = lax.broadcasted_iota(jnp.int32, (slots, slots), 0)
    lane = lax.broadcasted_iota(jnp.int32, (slots, slots), 1)
    kind = lane // half ^ core
    source = lane % half // span * (2 * span) + kind * span + lane % span
    picked = (row == source).astype(jnp.bfloat16)
    extra = jnp.zeros((keep_ref.shape[0] - members - 2, slots), jnp.float32)
    value = jnp.concatenate(
        [
            noise_ref[...].astype(jnp.float32),
            data_ref[...].astype(jnp.float32),
            extra,
        ],
        axis=0,
    ).astype(jnp.bfloat16)
    moved = jnp.dot(value, picked, preferred_element_type=jnp.float32).astype(jnp.bfloat16)
    keep_ref[...] = moved[:, 0:half]
    send_ref[...] = moved[:, half:slots]


def split_noise(place, noise, data):
    members, slots = noise.shape
    rows = -(-(members + 2) // 16) * 16
    out = jax.ShapeDtypeStruct((rows, slots // 2), jnp.bfloat16)
    return pl.pallas_call(
        split_noise_kernel,
        in_specs=[SMEM] + [VMEM] * 2,
        out_specs=[VMEM] * 2,
        out_shape=[out] * 2,
        compiler_params=pltpu.CompilerParams(vmem_limit_bytes=VMEM_LIMIT),
        name="split_noise",
    )(place, noise, data)


def select_noise_kernel(starts_ref, place_ref, near_ref, far_ref, out_ref, wide_ref, rows_ref):
    rows, per = near_ref.shape[-2:]
    chips = out_ref.shape[0]
    keep = per // BLK
    chip = place_ref[0]
    units = near_ref.shape[0] * near_ref.shape[1]
    wide_ref[:, rows:256] = jnp.zeros((wide_ref.shape[0], 256 - rows), jnp.float32)
    for i, ref in enumerate((near_ref, far_ref)):
        for z in range(near_ref.shape[0]):
            for c in range(near_ref.shape[1]):
                unit = i * units + z * near_ref.shape[1] + c
                wide_ref[unit * per : (unit + 1) * per, 0:rows] = ref[z, c].astype(jnp.float32).T
    for i in range(chips):
        for p in range(keep):
            start = pl.multiple_of(starts_ref[i * keep + p], BLK)
            rows_ref[p * BLK : (p + 1) * BLK, :] = wide_ref[pl.ds(start, BLK), :]
        out_ref[chip ^ i] = rows_ref[...].T[0:rows]


def select_noise(starts, place, near, far):
    rows, per = near.shape[-2:]
    chips = starts.shape[0] * BLK // per
    return pl.pallas_call(
        select_noise_kernel,
        in_specs=[SMEM, SMEM, VMEM, VMEM],
        out_specs=VMEM,
        out_shape=jax.ShapeDtypeStruct((chips, rows, per), jnp.float32),
        scratch_shapes=[
            pltpu.VMEM((2 * near.shape[0] * near.shape[1] * per, 256), jnp.float32),
            pltpu.VMEM((per, 256), jnp.float32),
        ],
        compiler_params=pltpu.CompilerParams(vmem_limit_bytes=VMEM_LIMIT),
        name="select_noise",
    )(starts, place, near, far)


def gram_kernel(place_ref, target_ref, noise_ref, *refs):
    predicted_refs = refs[:8]
    out_ref, predicted_ref, left_ref, right_ref, misfit_ref = refs[8:]
    groups, members, per = predicted_ref.shape
    coefficients = groups * per
    weight_scale = members / (2 * coefficients)
    chip = place_ref[0]
    for i, ref in enumerate(predicted_refs):
        predicted_ref[chip ^ i] = ref[...].astype(jnp.float32)
    right_ref[...] = jnp.zeros_like(right_ref)
    for g in range(groups):
        noise = noise_ref[g]
        observed = noise[members : members + 1]
        scale = noise[members + 1 : members + 2]
        predicted = predicted_ref[g]
        center = jnp.sum(predicted, axis=0, keepdims=True) * (1.0 / members)
        anomaly = (predicted - center) * (1.0 / math.sqrt(members - 1))
        weight = weight_scale / (scale * scale)
        mismatch = observed + math.sqrt(inflation) * scale * noise[:members] - predicted
        here = pl.ds(g * per, per)
        left_ref[:, here] = anomaly * weight
        right_ref[0:members, here] = anomaly
        right_ref[256 : 256 + members, here] = mismatch
        relative = mismatch / scale
        misfit = jnp.sqrt(
            jnp.sum(relative * relative, axis=0, keepdims=True) * (1.0 / members) + epsilon
        )
        high = misfit.astype(jnp.bfloat16)
        rest = misfit - high.astype(jnp.float32)
        middle = rest.astype(jnp.bfloat16)
        low = (rest - middle.astype(jnp.float32)).astype(jnp.bfloat16)
        misfit_ref[0:1, here] = high.astype(jnp.float32)
        misfit_ref[1:2, here] = middle.astype(jnp.float32)
        misfit_ref[2:3, here] = low.astype(jnp.float32)
        misfit_ref[3:8, here] = jnp.zeros((5, per), jnp.float32)
    out_ref[0:members, :] = lax.dot_general(
        left_ref[...], right_ref[...], (((1,), (1,)), ((), ())),
        precision=lax.Precision.HIGHEST, preferred_element_type=jnp.float32,
    )
    lanes = lax.broadcasted_iota(jnp.int32, (per, out_ref.shape[1]), 1)
    one_hot = jnp.concatenate(
        [(target_ref[chip ^ g] == lanes).astype(jnp.bfloat16) for g in range(groups)], axis=0
    )
    routed = jnp.dot(
        misfit_ref[...].astype(jnp.bfloat16), one_hot, preferred_element_type=jnp.float32
    )
    out_ref[members : members + 8, :] = jnp.broadcast_to(
        routed[0:1] + routed[1:2] + routed[2:3], (8, out_ref.shape[1])
    )


def gram(place, target, noise, predicted):
    members, per = predicted[0].shape
    groups = len(predicted)
    coefficients = groups * per
    return pl.pallas_call(
        gram_kernel,
        in_specs=[SMEM] + [VMEM] * (2 + len(predicted)),
        out_specs=VMEM,
        out_shape=jax.ShapeDtypeStruct((members + 8, 512), jnp.float32),
        scratch_shapes=[
            pltpu.VMEM((groups, members, per), jnp.float32),
            pltpu.VMEM((members, coefficients), jnp.float32),
            pltpu.VMEM((512, coefficients), jnp.float32),
            pltpu.VMEM((8, coefficients), jnp.float32),
        ],
        compiler_params=pltpu.CompilerParams(vmem_limit_bytes=VMEM_LIMIT),
        name="gram_and_cross",
    )(place, target, noise, *predicted)


def update_kernel(
    mine_ref, other_ref, slab_ref, out_ref, weights_ref, misfit_ref,
    state_ref, held_ref, arrived, left,
):
    members, cells = held_ref.shape
    tiles = left.shape[0]
    tile = cells // tiles
    parts = [pl.ds(i * tile, tile) for i in range(tiles)]
    writes = [
        pltpu.make_async_copy(held_ref.at[:, part], out_ref.at[:, part], left.at[i])
        for i, part in enumerate(parts)
    ]
    read = pltpu.make_async_copy(slab_ref, held_ref, arrived)
    read.start()

    total = mine_ref[0:members, :] + other_ref[0:members, :]
    misfit_ref[...] = (
        mine_ref[members : members + 1, 0:256] + other_ref[members : members + 1, 256:512]
    )
    row = lax.broadcasted_iota(jnp.int32, (members, 256), 0)
    lane = lax.broadcasted_iota(jnp.int32, (members, 256), 1)
    unit = jnp.where(row == lane, 1.0, 0.0)
    matrix = total[:, 0:256] + inflation * unit
    bound = jnp.max(jnp.sum(jnp.abs(matrix), axis=1, keepdims=True), axis=0, keepdims=True)
    step = 2.0 / (inflation + bound)
    state_ref[members:256, :] = jnp.zeros((256 - members, 512), jnp.float32)
    state_ref[0:members, 0:256] = unit - step * matrix
    state_ref[0:members, 256:512] = step * total[:, 256:512]

    def more(carry):
        return carry[0] > 2.0**-24

    def double(carry):
        power = state_ref[:, 0:256]
        size = jnp.sum(power * power)
        moved = jnp.dot(
            power, state_ref[...], precision=lax.Precision.HIGHEST,
            preferred_element_type=jnp.float32,
        )
        state_ref[:, 0:256] = moved[:, 0:256]
        state_ref[:, 256:512] = state_ref[:, 256:512] + moved[:, 256:512]
        return (size,)

    lax.while_loop(more, double, (jnp.float32(1.0),))
    weights_ref[...] = state_ref[0:members, 256 : 256 + members]

    full = state_ref[:, 256:512]
    center = jnp.sum(full, axis=0, keepdims=True) * (1.0 / members)
    spread = ((full - center) * (1.0 / math.sqrt(members - 1))).T[0:members, 0:members]
    high = spread.astype(jnp.bfloat16)
    rest = spread - high.astype(jnp.float32)
    low = rest.astype(jnp.bfloat16).astype(jnp.float32)
    over = jnp.sum(rest - low, axis=1, keepdims=True)
    lane = lax.broadcasted_iota(jnp.int32, (members, members), 1)
    low = (low + jnp.where(lane == 0, over, 0.0)).astype(jnp.bfloat16)
    read.wait()
    for i in range(tiles):
        for j in range(i * tile, (i + 1) * tile, 256):
            state = held_ref[:, j : j + 256]
            moved = jnp.dot(low, state, preferred_element_type=jnp.float32)
            moved = moved + jnp.dot(high, state, preferred_element_type=jnp.float32)
            held_ref[:, j : j + 256] = (state.astype(jnp.float32) + moved).astype(jnp.bfloat16)
        writes[i].start()
    for write in writes:
        write.wait()


def update(mine, other, slab):
    members, cells = slab.shape
    tiles = cells // 1024
    return pl.pallas_call(
        update_kernel,
        in_specs=[VMEM, VMEM, HBM],
        out_specs=[HBM, VMEM, VMEM],
        out_shape=[
            jax.ShapeDtypeStruct(slab.shape, slab.dtype),
            jax.ShapeDtypeStruct((members, members), jnp.float32),
            jax.ShapeDtypeStruct((1, 256), jnp.float32),
        ],
        scratch_shapes=[
            pltpu.VMEM((256, 512), jnp.float32),
            pltpu.VMEM(slab.shape, slab.dtype),
            pltpu.SemaphoreType.DMA,
            pltpu.SemaphoreType.DMA((tiles,)),
        ],
        compiler_params=pltpu.CompilerParams(vmem_limit_bytes=SLAB_LIMIT),
        name="solve_and_update",
    )(mine, other, slab)


def sparse_body(
    amplitude_maps, kept_blocks, block_owner, observed, error_scale, perturbation, model_slab
):
    members, rows_here, map_width = amplitude_maps.shape
    devices = lax.axis_size("map")
    map_height = rows_here * devices
    keep = kept_blocks.shape[0]
    slots = observed.shape[0]
    me = lax.axis_index("map").astype(jnp.int32)
    core, chip = me & 1, me >> 1

    lists = jnp.concatenate([kept_blocks, block_owner[:, 0]])
    lists = jnp.stack([lists] + [swap(lists, delta) for delta in range(1, 4)])

    noise_keep, noise_send = split_noise(
        me.reshape(1), perturbation.T, jnp.stack([observed, error_scale])
    )
    noise = jnp.stack([noise_keep, swap(noise_send, 1)])
    amplitude_maps, noise, lists = lax.optimization_barrier((amplitude_maps, noise, lists))
    lists = [lists] + [swap(lists, 4 * i) for i in range(1, devices // 4)]
    near_z = swap(noise, 4)

    maps = by_row(amplitude_maps)
    table_w = jnp.asarray(dct_constant(map_width))
    table_h = table_w if map_height == map_width else jnp.asarray(dct_constant(map_height))
    lists, near_z = lax.optimization_barrier((lists, near_z))
    keep_0, keep_1, send_0, send_1 = shares(lists, me.reshape(1), maps, table_w, table_h)

    share_1 = keep_1 + swap(send_1, 1)
    got_1 = swap(share_1, 2)
    share_0 = keep_0 + swap(send_0, 1)
    share = [share_0[i] + got_1[i] for i in range(devices // 4)]
    noise = jnp.stack([noise, near_z])
    far_z = swap(noise, 8)
    share, far_z = lax.optimization_barrier((share, far_z))
    near_noise = jnp.concatenate([noise, far_z])
    far_noise = swap(near_noise, 2)
    got = [swap(share[i], 4 * i) for i in range(1, devices // 4)]
    predicted = (share[0] + got[0] + got[1] + got[2]).astype(jnp.bfloat16)
    predicted, far_noise = lax.optimization_barrier((predicted, far_noise))

    near = [predicted] + [swap(predicted, 4 * i) for i in range(1, devices // 4)]
    gathered = []
    for value in near:
        gathered += [value, swap(value, 2)]

    owner = jnp.concatenate(lists)[0::2, keep:]
    positions = jnp.arange(keep, dtype=jnp.int32)
    earlier = (owner[:, :, None] == owner[:, None, :]) & (
        positions[None, None, :] < positions[None, :, None]
    )
    rank = jnp.sum(earlier.astype(jnp.int32), axis=2)
    chips = chip ^ jnp.arange(devices // 2, dtype=jnp.int32)[:, None]
    away = owner ^ me
    held = (away >> 1 & 1) * 8 + (away >> 2) * 2 + (away & 1)
    noise_rows = held * (slots // 2) + chips * (CAP * BLK) + rank * BLK
    data_row = (chips * 2 + core) * (CAP * BLK) + rank * BLK
    target = jnp.where(away < 2, away * slots + data_row, -1024)
    target = (target[:, :, None] + jnp.arange(BLK, dtype=jnp.int32)).reshape(
        devices // 2, keep * BLK, 1
    )
    noise = select_noise(noise_rows.reshape(-1), chip.reshape(1), near_noise, far_noise)
    mine = gram(chip.reshape(1), target, noise, gathered)
    updated_slab, update_weights, data_misfit = update(mine, swap(mine, 1), model_slab)
    return (updated_slab, update_weights, data_misfit.reshape(-1))


def solution(mesh):
    in_specs = (
        P("groups", "map", None),
        P(("groups", "map")),
        P(("groups", "map"), None),
        P(("groups", "map")),
        P(("groups", "map")),
        P(("groups", "map"), None),
        P(None, ("groups", "map")),
    )
    out_specs = (P(None, ("groups", "map")), P("groups", None), P(("groups", "map")))

    def body(amplitude_maps, kept_blocks, *rest):
        few = mesh.shape["map"] == 16 and kept_blocks.shape[0] * BLK == LANE
        chosen = sparse_body if few else dense_body
        return chosen(amplitude_maps, kept_blocks, *rest)

    return jax.shard_map(body, mesh=mesh, in_specs=in_specs, out_specs=out_specs, check_vma=False)
```

```python
import math

import jax
import jax.numpy as jnp
import numpy as np
from jax import lax
from jax.experimental import pallas as pl
from jax.experimental.pallas import tpu as pltpu
from jax.sharding import PartitionSpec as P

BLK = 8
CAP = 2
LANE = 128

inflation = 4.0
epsilon = 1e-06

VMEM_LIMIT = 24 * 1024 * 1024
MAPS_LIMIT = 44 * 1024 * 1024
SLAB_LIMIT = 50 * 1024 * 1024


def dct_table(length):
    frequency = jnp.arange(length, dtype=jnp.float32)[:, None]
    sample = jnp.arange(length, dtype=jnp.float32)[None, :]
    cosine_table = jnp.cos(math.pi * (2.0 * sample + 1.0) * frequency / (2.0 * length))
    factor = jnp.where(frequency == 0, math.sqrt(1.0 / length), math.sqrt(2.0 / length))
    return (cosine_table * factor).astype(jnp.bfloat16)


def dct_constant(length):
    frequency = np.arange(length, dtype=np.float32)[:, None]
    sample = np.arange(length, dtype=np.float32)[None, :]
    angle = np.float32(math.pi) * (np.float32(2.0) * sample + np.float32(1.0)) * frequency
    cosine_table = np.cos(angle / np.float32(2.0 * length))
    factor = np.where(
        frequency == 0, np.float32(math.sqrt(1.0 / length)), np.float32(math.sqrt(2.0 / length))
    )
    return (cosine_table * factor).astype(jnp.bfloat16)


def gram_terms(predicted, observed_rows, scale_rows, noise_rows, live_mask, weight_scale):
    members = predicted.shape[1]
    center = jnp.mean(predicted, axis=1, keepdims=True)
    anomaly = (predicted - center) / math.sqrt(members - 1)
    weight = live_mask * weight_scale / (scale_rows * scale_rows)
    mismatch = (
        observed_rows[:, None] + math.sqrt(inflation) * scale_rows[:, None] * noise_rows - predicted
    )
    weighted = anomaly * weight[:, None]
    contract = (((0,), (0,)), ((), ()))
    gram_matrix = lax.dot_general(anomaly, weighted, contract, precision=lax.Precision.HIGHEST)
    cross_terms = lax.dot_general(weighted, mismatch, contract, precision=lax.Precision.HIGHEST)
    relative = mismatch / scale_rows[:, None]
    misfit_rows = live_mask * jnp.sqrt(jnp.mean(relative * relative, axis=1) + epsilon)
    return (gram_matrix, cross_terms, misfit_rows)


def solve_weights(gram_matrix, cross_terms):
    members = gram_matrix.shape[0]
    factor = jnp.linalg.cholesky(gram_matrix + inflation * jnp.eye(members, dtype=jnp.float32))
    return jax.scipy.linalg.cho_solve((factor, True), cross_terms)


def update_state(block, update_weights):
    state = block.astype(jnp.float32)
    members = state.shape[0]
    anomaly = (state - jnp.mean(state, axis=0, keepdims=True)) / math.sqrt(members - 1)
    moved = state + lax.dot_general(
        update_weights, anomaly, (((0,), (0,)), ((), ())), precision=lax.Precision.HIGHEST
    )
    return moved.astype(jnp.bfloat16)


def dense_body(
    amplitude_maps, kept_blocks, block_owner, observed, error_scale, perturbation, model_slab
):
    members, rows_here, map_width = amplitude_maps.shape
    devices = lax.axis_size("map")
    map_height = rows_here * devices
    table_w = dct_table(map_width)
    table_h = dct_table(map_height)
    rowwise = jnp.einsum(
        "ehw,kw->hke", amplitude_maps, table_w, preferred_element_type=jnp.float32
    ).astype(jnp.bfloat16)
    coefficients = jnp.einsum(
        "kh,hwe->wke",
        table_h,
        lax.all_to_all(rowwise, "map", split_axis=1, concat_axis=0, tiled=True),
        preferred_element_type=jnp.float32,
    ).astype(jnp.bfloat16)
    block_rows = coefficients.reshape(-1, BLK * members)
    candidates = block_rows.shape[0]
    keep_count = kept_blocks.shape[0]
    slot_count = devices * CAP
    dest_owner = block_owner[:, 0]
    positions = jnp.arange(keep_count, dtype=jnp.int32)
    earlier = (dest_owner[:, None] == dest_owner[None, :]) & (
        positions[None, :] < positions[:, None]
    )
    slot_rank = jnp.sum(earlier.astype(jnp.int32), axis=1)
    slot_index = dest_owner * CAP + slot_rank
    pick_slot = (slot_index[:, None] == jnp.arange(slot_count, dtype=jnp.int32)[None, :]).astype(
        jnp.bfloat16
    )
    weight_scale = members / (devices * keep_count * BLK)
    contract = (((0,), (0,)), ((), ()))
    pick_block = (kept_blocks[:, None] == jnp.arange(candidates, dtype=jnp.int32)[None, :]).astype(
        jnp.bfloat16
    )
    routing = lax.dot_general(
        pick_slot, pick_block, contract, preferred_element_type=jnp.float32
    ).astype(jnp.bfloat16)
    outgoing = jnp.dot(routing, block_rows, preferred_element_type=jnp.float32).astype(jnp.bfloat16)
    live_slots = jnp.sum(pick_slot.astype(jnp.float32), axis=0).astype(jnp.bfloat16)
    arrived, arrived_live = (
        lax.all_to_all(
            outgoing.reshape(devices, CAP, BLK * members),
            "map",
            split_axis=0,
            concat_axis=0,
            tiled=True,
        ),
        lax.all_to_all(
            live_slots.reshape(devices, CAP), "map", split_axis=0, concat_axis=0, tiled=True
        ),
    )
    predicted = arrived.reshape(-1, members).astype(jnp.float32)
    live_mask = jnp.repeat(arrived_live.astype(jnp.float32).reshape(-1), BLK)
    gram_matrix, cross_terms, data_misfit = gram_terms(
        predicted,
        observed.astype(jnp.float32),
        error_scale.astype(jnp.float32),
        perturbation.astype(jnp.float32),
        live_mask,
        weight_scale,
    )
    gram_matrix, cross_terms = lax.psum((gram_matrix, cross_terms), "map")
    update_weights = solve_weights(gram_matrix, cross_terms)
    updated_slab = update_state(model_slab, update_weights)
    return (updated_slab, update_weights, data_misfit)


def swap(value, delta):
    pairs = [(i, i ^ delta) for i in range(lax.axis_size("map"))]
    return lax.ppermute(value, "map", pairs)


VMEM = pl.BlockSpec(memory_space=pltpu.VMEM)
SMEM = pl.BlockSpec(memory_space=pltpu.SMEM)
HBM = pl.BlockSpec(memory_space=pltpu.HBM)


def by_row_kernel(maps_ref, out_ref, held_ref, arrived):
    width = maps_ref.shape[2]
    copies = []
    for i in range(width // LANE):
        part = pl.ds(i * LANE, LANE)
        copies.append(
            pltpu.make_async_copy(maps_ref.at[:, :, part], held_ref.at[i], arrived.at[i])
        )
        copies[i].start()
    for i in range(width // LANE):
        copies[i].wait()
        out_ref[:, :, i * LANE : (i + 1) * LANE] = jnp.swapaxes(held_ref[i], 0, 1)


def by_row(amplitude_maps):
    members, rows, width = amplitude_maps.shape
    parts = width // LANE
    return pl.pallas_call(
        by_row_kernel,
        in_specs=[HBM],
        out_specs=VMEM,
        out_shape=jax.ShapeDtypeStruct((rows, members, width), jnp.bfloat16),
        scratch_shapes=[
            pltpu.VMEM((parts, members, rows, LANE), jnp.bfloat16),
            pltpu.SemaphoreType.DMA((parts,)),
        ],
        compiler_params=pltpu.CompilerParams(vmem_limit_bytes=MAPS_LIMIT),
        cost_estimate=pl.CostEstimate(
            flops=0, bytes_accessed=4 * members * rows * width, transcendentals=0
        ),
        name="maps_by_row",
    )(amplitude_maps)


def shares_kernel(
    list0_ref, list1_ref, list2_ref, list3_ref, maps_ref, table_w_ref, table_h_ref,
    k0_ref, k1_ref, s0_ref, s1_ref,
    lists_ref, arrived, full_ref, pick_ref, row_ref, spread_ref,
):
    rows, members, width = maps_ref.shape
    devices, depth, _ = row_ref.shape
    keep = depth // rows
    height = table_h_ref.shape[0]
    per_column = height // BLK
    columns_here = width // devices
    me = lax.axis_index("map")
    copies = [
        pltpu.make_async_copy(ref, lists_ref.at[i], arrived.at[i])
        for i, ref in enumerate((list0_ref, list1_ref, list2_ref, list3_ref))
    ]
    for copy in copies:
        copy.start()

    def column_of(delta, p):
        number = lists_ref[delta // 4, delta % 4, p]
        if per_column & (per_column - 1) == 0:
            return number >> per_column.bit_length() - 1
        return lax.div(number, per_column)

    def row_of(delta, p):
        number = lists_ref[delta // 4, delta % 4, p]
        if per_column & (per_column - 1) == 0:
            return (number & per_column - 1) * BLK
        return lax.rem(number, per_column) * BLK

    full_ref[...] = table_w_ref[...].astype(jnp.float32)
    sample = lax.broadcasted_iota(jnp.int32, (height, depth), 0) - me * rows
    held = lax.broadcasted_iota(jnp.int32, (height, depth), 1) // keep
    spread_ref[...] = jnp.dot(
        table_h_ref[...], (sample == held).astype(jnp.bfloat16), preferred_element_type=jnp.float32
    )
    for copy in copies:
        copy.wait()
    for delta in range(devices):
        for p in range(keep):
            column = (me ^ delta) * columns_here + column_of(delta, p)
            pick_ref[pl.ds(delta * keep + p, 1), :] = full_ref[pl.ds(column, 1), :]
    pick = pick_ref[...].astype(jnp.bfloat16)
    for row in range(rows):
        rowwise = lax.dot_general(
            pick, maps_ref[row], (((1,), (1,)), ((), ())), preferred_element_type=jnp.float32
        ).astype(jnp.bfloat16)
        row_ref[:, row * keep : (row + 1) * keep, :] = rowwise.reshape(devices, keep, members)

    position = lax.broadcasted_iota(jnp.int32, (BLK, depth), 1) % keep
    for out_ref, low in ((s1_ref, 3), (k1_ref, 2), (s0_ref, 1), (k0_ref, 0)):
        for high in range(out_ref.shape[0]):
            delta = high * 4 + low
            wide = []
            for p in range(keep):
                start = pl.multiple_of(row_of(delta, p), BLK)
                wide.append(jnp.where(position == p, spread_ref[pl.ds(start, BLK), :], 0.0))
            wide = jnp.concatenate(wide, axis=0).astype(jnp.bfloat16)
            out_ref[high] = jnp.dot(
                wide, row_ref[delta], preferred_element_type=jnp.float32
            ).T


def shares(lists, maps, table_w, table_h):
    rows, members, width = maps.shape
    devices = sum(part.shape[0] for part in lists)
    keep = lists[0].shape[1] // 2
    depth = rows * keep
    out = jax.ShapeDtypeStruct((devices // 4, members, keep * BLK), jnp.float32)
    return pl.pallas_call(
        shares_kernel,
        in_specs=[VMEM] * 7,
        out_specs=[VMEM] * 4,
        out_shape=[out] * 4,
        scratch_shapes=[
            pltpu.SMEM((len(lists),) + lists[0].shape, jnp.int32),
            pltpu.SemaphoreType.DMA((len(lists),)),
            pltpu.VMEM(table_w.shape, jnp.float32),
            pltpu.VMEM((devices * keep, width), jnp.float32),
            pltpu.VMEM((devices, depth, members), jnp.bfloat16),
            pltpu.VMEM((table_h.shape[0], depth), jnp.float32),
        ],
        compiler_params=pltpu.CompilerParams(vmem_limit_bytes=VMEM_LIMIT),
        cost_estimate=pl.CostEstimate(
            flops=2 * devices * keep * width * rows * members,
            bytes_accessed=2 * rows * members * width,
            transcendentals=0,
        ),
        name="coefficient_shares",
    )(*lists, maps, table_w, table_h)


def split_noise_kernel(noise_ref, observed_ref, scale_ref, keep_ref, send_ref):
    members, slots = noise_ref.shape
    half = slots // 2
    core = lax.axis_index("map") & 1
    span = 2 * CAP * BLK // 2
    row = lax.broadcasted_iota(jnp.int32, (slots, slots), 0)
    lane = lax.broadcasted_iota(jnp.int32, (slots, slots), 1)
    kind = lane // half ^ core
    source = lane % half // span * (2 * span) + kind * span + lane % span
    picked = (row == source).astype(jnp.bfloat16)
    extra = jnp.zeros((keep_ref.shape[0] - members - 2, slots), jnp.float32)
    value = jnp.concatenate(
        [
            noise_ref[...].astype(jnp.float32),
            observed_ref[...].astype(jnp.float32).reshape(1, slots),
            scale_ref[...].astype(jnp.float32).reshape(1, slots),
            extra,
        ],
        axis=0,
    ).astype(jnp.bfloat16)
    moved = jnp.dot(value, picked, preferred_element_type=jnp.float32).astype(jnp.bfloat16)
    keep_ref[...] = moved[:, 0:half]
    send_ref[...] = moved[:, half:slots]


def split_noise(noise, observed, scale):
    members, slots = noise.shape
    rows = -(-(members + 2) // 16) * 16
    out = jax.ShapeDtypeStruct((rows, slots // 2), jnp.bfloat16)
    return pl.pallas_call(
        split_noise_kernel,
        in_specs=[VMEM] * 3,
        out_specs=[VMEM] * 2,
        out_shape=[out] * 2,
        compiler_params=pltpu.CompilerParams(vmem_limit_bytes=VMEM_LIMIT),
        name="split_noise",
    )(noise, observed, scale)


def select_noise_kernel(starts_ref, near_ref, far_ref, out_ref, wide_ref, rows_ref):
    rows, per = near_ref.shape[-2:]
    chips = out_ref.shape[0]
    keep = per // BLK
    chip = lax.axis_index("map") >> 1
    units = near_ref.shape[0] * near_ref.shape[1]
    wide_ref[:, rows:256] = jnp.zeros((wide_ref.shape[0], 256 - rows), jnp.float32)
    for i, ref in enumerate((near_ref, far_ref)):
        for z in range(near_ref.shape[0]):
            for c in range(near_ref.shape[1]):
                unit = i * units + z * near_ref.shape[1] + c
                wide_ref[unit * per : (unit + 1) * per, 0:rows] = ref[z, c].astype(jnp.float32).T
    for i in range(chips):
        for p in range(keep):
            start = pl.multiple_of(starts_ref[i * keep + p], BLK)
            rows_ref[p * BLK : (p + 1) * BLK, :] = wide_ref[pl.ds(start, BLK), :]
        out_ref[chip ^ i] = rows_ref[...].T[0:rows]


def select_noise(starts, near, far):
    rows, per = near.shape[-2:]
    chips = starts.shape[0] * BLK // per
    return pl.pallas_call(
        select_noise_kernel,
        in_specs=[SMEM, VMEM, VMEM],
        out_specs=VMEM,
        out_shape=jax.ShapeDtypeStruct((chips, rows, per), jnp.float32),
        scratch_shapes=[
            pltpu.VMEM((2 * near.shape[0] * near.shape[1] * per, 256), jnp.float32),
            pltpu.VMEM((per, 256), jnp.float32),
        ],
        compiler_params=pltpu.CompilerParams(vmem_limit_bytes=VMEM_LIMIT),
        name="select_noise",
    )(starts, near, far)


def gram_kernel(target_ref, noise_ref, *refs):
    predicted_refs = refs[:8]
    out_ref, predicted_ref, left_ref, right_ref, misfit_ref = refs[8:]
    groups, members, per = predicted_ref.shape
    coefficients = groups * per
    weight_scale = members / (2 * coefficients)
    chip = lax.axis_index("map") >> 1
    for i, ref in enumerate(predicted_refs):
        predicted_ref[chip ^ i] = ref[...].astype(jnp.float32)
    right_ref[...] = jnp.zeros_like(right_ref)
    for g in range(groups):
        noise = noise_ref[g]
        observed = noise[members : members + 1]
        scale = noise[members + 1 : members + 2]
        predicted = predicted_ref[g]
        center = jnp.sum(predicted, axis=0, keepdims=True) * (1.0 / members)
        anomaly = (predicted - center) * (1.0 / math.sqrt(members - 1))
        weight = weight_scale / (scale * scale)
        mismatch = observed + math.sqrt(inflation) * scale * noise[:members] - predicted
        here = pl.ds(g * per, per)
        left_ref[:, here] = anomaly * weight
        right_ref[0:members, here] = anomaly
        right_ref[256 : 256 + members, here] = mismatch
        relative = mismatch / scale
        misfit = jnp.sqrt(
            jnp.sum(relative * relative, axis=0, keepdims=True) * (1.0 / members) + epsilon
        )
        high = misfit.astype(jnp.bfloat16)
        rest = misfit - high.astype(jnp.float32)
        middle = rest.astype(jnp.bfloat16)
        low = (rest - middle.astype(jnp.float32)).astype(jnp.bfloat16)
        misfit_ref[0:1, here] = high.astype(jnp.float32)
        misfit_ref[1:2, here] = middle.astype(jnp.float32)
        misfit_ref[2:3, here] = low.astype(jnp.float32)
        misfit_ref[3:8, here] = jnp.zeros((5, per), jnp.float32)
    out_ref[0:members, :] = lax.dot_general(
        left_ref[...], right_ref[...], (((1,), (1,)), ((), ())),
        precision=lax.Precision.HIGHEST, preferred_element_type=jnp.float32,
    )
    lanes = lax.broadcasted_iota(jnp.int32, (per, out_ref.shape[1]), 1)
    one_hot = jnp.concatenate(
        [(target_ref[chip ^ g] == lanes).astype(jnp.bfloat16) for g in range(groups)], axis=0
    )
    routed = jnp.dot(
        misfit_ref[...].astype(jnp.bfloat16), one_hot, preferred_element_type=jnp.float32
    )
    out_ref[members : members + 8, :] = jnp.broadcast_to(
        routed[0:1] + routed[1:2] + routed[2:3], (8, out_ref.shape[1])
    )


def gram(target, noise, predicted):
    members, per = predicted[0].shape
    groups = len(predicted)
    coefficients = groups * per
    return pl.pallas_call(
        gram_kernel,
        in_specs=[VMEM] * (2 + len(predicted)),
        out_specs=VMEM,
        out_shape=jax.ShapeDtypeStruct((members + 8, 512), jnp.float32),
        scratch_shapes=[
            pltpu.VMEM((groups, members, per), jnp.float32),
            pltpu.VMEM((members, coefficients), jnp.float32),
            pltpu.VMEM((512, coefficients), jnp.float32),
            pltpu.VMEM((8, coefficients), jnp.float32),
        ],
        compiler_params=pltpu.CompilerParams(vmem_limit_bytes=VMEM_LIMIT),
        name="gram_and_cross",
    )(target, noise, *predicted)


def update_kernel(
    mine_ref, other_ref, slab_ref, out_ref, weights_ref, misfit_ref,
    state_ref, held_ref, arrived, left,
):
    members, cells = held_ref.shape
    tiles = left.shape[0]
    tile = cells // tiles
    parts = [pl.ds(i * tile, tile) for i in range(tiles)]
    writes = [
        pltpu.make_async_copy(held_ref.at[:, part], out_ref.at[:, part], left.at[i])
        for i, part in enumerate(parts)
    ]
    read = pltpu.make_async_copy(slab_ref, held_ref, arrived)
    read.start()

    total = mine_ref[0:members, :] + other_ref[0:members, :]
    misfit_ref[...] = (
        mine_ref[members : members + 1, 0:256] + other_ref[members : members + 1, 256:512]
    )
    row = lax.broadcasted_iota(jnp.int32, (members, 256), 0)
    lane = lax.broadcasted_iota(jnp.int32, (members, 256), 1)
    unit = jnp.where(row == lane, 1.0, 0.0)
    matrix = total[:, 0:256] + inflation * unit
    bound = jnp.max(jnp.sum(jnp.abs(matrix), axis=1, keepdims=True), axis=0, keepdims=True)
    step = 2.0 / (inflation + bound)
    state_ref[members:256, :] = jnp.zeros((256 - members, 512), jnp.float32)
    state_ref[0:members, 0:256] = unit - step * matrix
    state_ref[0:members, 256:512] = step * total[:, 256:512]

    def more(carry):
        return carry[0] > 2.0**-24

    def double(carry):
        power = state_ref[:, 0:256]
        size = jnp.sum(power * power)
        moved = jnp.dot(
            power, state_ref[...], precision=lax.Precision.HIGHEST,
            preferred_element_type=jnp.float32,
        )
        state_ref[:, 0:256] = moved[:, 0:256]
        state_ref[:, 256:512] = state_ref[:, 256:512] + moved[:, 256:512]
        return (size,)

    lax.while_loop(more, double, (jnp.float32(1.0),))
    weights_ref[...] = state_ref[0:members, 256 : 256 + members]

    full = state_ref[:, 256:512]
    center = jnp.sum(full, axis=0, keepdims=True) * (1.0 / members)
    spread = ((full - center) * (1.0 / math.sqrt(members - 1))).T[0:members, 0:members]
    high = spread.astype(jnp.bfloat16)
    rest = spread - high.astype(jnp.float32)
    low = rest.astype(jnp.bfloat16).astype(jnp.float32)
    over = jnp.sum(rest - low, axis=1, keepdims=True)
    lane = lax.broadcasted_iota(jnp.int32, (members, members), 1)
    low = (low + jnp.where(lane == 0, over, 0.0)).astype(jnp.bfloat16)
    read.wait()
    for i in range(tiles):
        for j in range(i * tile, (i + 1) * tile, 256):
            state = held_ref[:, j : j + 256]
            moved = jnp.dot(low, state, preferred_element_type=jnp.float32)
            moved = moved + jnp.dot(high, state, preferred_element_type=jnp.float32)
            held_ref[:, j : j + 256] = (state.astype(jnp.float32) + moved).astype(jnp.bfloat16)
        writes[i].start()
    for write in writes:
        write.wait()


def update(mine, other, slab):
    members, cells = slab.shape
    tiles = cells // 1024
    return pl.pallas_call(
        update_kernel,
        in_specs=[VMEM, VMEM, HBM],
        out_specs=[HBM, VMEM, VMEM],
        out_shape=[
            jax.ShapeDtypeStruct(slab.shape, slab.dtype),
            jax.ShapeDtypeStruct((members, members), jnp.float32),
            jax.ShapeDtypeStruct((1, 256), jnp.float32),
        ],
        scratch_shapes=[
            pltpu.VMEM((256, 512), jnp.float32),
            pltpu.VMEM(slab.shape, slab.dtype),
            pltpu.SemaphoreType.DMA,
            pltpu.SemaphoreType.DMA((tiles,)),
        ],
        compiler_params=pltpu.CompilerParams(vmem_limit_bytes=SLAB_LIMIT),
        name="solve_and_update",
    )(mine, other, slab)


def sparse_body(
    amplitude_maps, kept_blocks, block_owner, observed, error_scale, perturbation, model_slab
):
    members, rows_here, map_width = amplitude_maps.shape
    devices = lax.axis_size("map")
    map_height = rows_here * devices
    keep = kept_blocks.shape[0]
    slots = observed.shape[0]
    me = lax.axis_index("map").astype(jnp.int32)
    core, chip = me & 1, me >> 1

    lists = jnp.concatenate([kept_blocks, block_owner[:, 0]])
    lists = jnp.stack([lists] + [swap(lists, delta) for delta in range(1, 4)])

    noise_keep, noise_send = split_noise(perturbation.T, observed, error_scale)
    noise = jnp.stack([noise_keep, swap(noise_send, 1)])
    amplitude_maps, noise, lists = lax.optimization_barrier((amplitude_maps, noise, lists))
    lists = [lists] + [swap(lists, 4 * i) for i in range(1, devices // 4)]
    far_z = swap(noise, 8)

    maps = by_row(amplitude_maps)
    table_w = jnp.asarray(dct_constant(map_width))
    table_h = table_w if map_height == map_width else jnp.asarray(dct_constant(map_height))
    lists, far_z = lax.optimization_barrier((lists, far_z))
    keep_0, keep_1, send_0, send_1 = shares(lists, maps, table_w, table_h)

    share_1 = keep_1 + swap(send_1, 1)
    got_1 = swap(share_1, 2)
    share_0 = keep_0 + swap(send_0, 1)
    share = [share_0[i] + got_1[i] for i in range(devices // 4)]
    noise = jnp.stack([noise, far_z])
    near_z = swap(noise, 4)
    share, near_z = lax.optimization_barrier((share, near_z))
    near_noise = jnp.concatenate([noise, near_z])
    far_noise = swap(near_noise, 2)
    got = [swap(share[i], 4 * i) for i in range(1, devices // 4)]
    predicted = (share[0] + got[0] + got[1] + got[2]).astype(jnp.bfloat16)
    predicted, far_noise = lax.optimization_barrier((predicted, far_noise))

    near = [predicted] + [swap(predicted, 4 * i) for i in range(1, devices // 4)]
    gathered = []
    for value in near:
        gathered += [value, swap(value, 2)]

    owner = jnp.concatenate(lists)[0::2, keep:]
    positions = jnp.arange(keep, dtype=jnp.int32)
    earlier = (owner[:, :, None] == owner[:, None, :]) & (
        positions[None, None, :] < positions[None, :, None]
    )
    rank = jnp.sum(earlier.astype(jnp.int32), axis=2)
    chips = chip ^ jnp.arange(devices // 2, dtype=jnp.int32)[:, None]
    away = owner ^ me
    held = (away >> 1 & 1) * 8 + (away >> 2 & 1) * 4 + (away >> 3) * 2 + (away & 1)
    noise_rows = held * (slots // 2) + chips * (CAP * BLK) + rank * BLK
    data_row = (chips * 2 + core) * (CAP * BLK) + rank * BLK
    target = jnp.where(away < 2, away * slots + data_row, -1024)
    target = (target[:, :, None] + jnp.arange(BLK, dtype=jnp.int32)).reshape(
        devices // 2, keep * BLK, 1
    )
    noise = select_noise(noise_rows.reshape(-1), near_noise, far_noise)
    mine = gram(target, noise, gathered)
    updated_slab, update_weights, data_misfit = update(mine, swap(mine, 1), model_slab)
    return (updated_slab, update_weights, data_misfit.reshape(-1))


def solution(mesh):
    in_specs = (
        P("groups", "map", None),
        P(("groups", "map")),
        P(("groups", "map"), None),
        P(("groups", "map")),
        P(("groups", "map")),
        P(("groups", "map"), None),
        P(None, ("groups", "map")),
    )
    out_specs = (P(None, ("groups", "map")), P("groups", None), P(("groups", "map")))

    def body(amplitude_maps, kept_blocks, *rest):
        few = mesh.shape["map"] == 16 and kept_blocks.shape[0] * BLK == LANE
        chosen = sparse_body if few else dense_body
        return chosen(amplitude_maps, kept_blocks, *rest)

    return jax.shard_map(body, mesh=mesh, in_specs=in_specs, out_specs=out_specs, check_vma=False)
```

```python
import math

import jax
import jax.numpy as jnp
import numpy as np
from jax import lax
from jax.experimental import pallas as pl
from jax.experimental.pallas import tpu as pltpu
from jax.sharding import PartitionSpec as P

BLK = 8
CAP = 2
LANE = 128

inflation = 4.0
epsilon = 1e-06

VMEM_LIMIT = 24 * 1024 * 1024
MAPS_LIMIT = 44 * 1024 * 1024
SLAB_LIMIT = 50 * 1024 * 1024


def dct_table(length):
    frequency = jnp.arange(length, dtype=jnp.float32)[:, None]
    sample = jnp.arange(length, dtype=jnp.float32)[None, :]
    cosine_table = jnp.cos(math.pi * (2.0 * sample + 1.0) * frequency / (2.0 * length))
    factor = jnp.where(frequency == 0, math.sqrt(1.0 / length), math.sqrt(2.0 / length))
    return (cosine_table * factor).astype(jnp.bfloat16)


def dct_constant(length):
    frequency = np.arange(length, dtype=np.float32)[:, None]
    sample = np.arange(length, dtype=np.float32)[None, :]
    angle = np.float32(math.pi) * (np.float32(2.0) * sample + np.float32(1.0)) * frequency
    cosine_table = np.cos(angle / np.float32(2.0 * length))
    factor = np.where(
        frequency == 0, np.float32(math.sqrt(1.0 / length)), np.float32(math.sqrt(2.0 / length))
    )
    return (cosine_table * factor).astype(jnp.bfloat16)


def gram_terms(predicted, observed_rows, scale_rows, noise_rows, live_mask, weight_scale):
    members = predicted.shape[1]
    center = jnp.mean(predicted, axis=1, keepdims=True)
    anomaly = (predicted - center) / math.sqrt(members - 1)
    weight = live_mask * weight_scale / (scale_rows * scale_rows)
    mismatch = (
        observed_rows[:, None] + math.sqrt(inflation) * scale_rows[:, None] * noise_rows - predicted
    )
    weighted = anomaly * weight[:, None]
    contract = (((0,), (0,)), ((), ()))
    gram_matrix = lax.dot_general(anomaly, weighted, contract, precision=lax.Precision.HIGHEST)
    cross_terms = lax.dot_general(weighted, mismatch, contract, precision=lax.Precision.HIGHEST)
    relative = mismatch / scale_rows[:, None]
    misfit_rows = live_mask * jnp.sqrt(jnp.mean(relative * relative, axis=1) + epsilon)
    return (gram_matrix, cross_terms, misfit_rows)


def solve_weights(gram_matrix, cross_terms):
    members = gram_matrix.shape[0]
    factor = jnp.linalg.cholesky(gram_matrix + inflation * jnp.eye(members, dtype=jnp.float32))
    return jax.scipy.linalg.cho_solve((factor, True), cross_terms)


def update_state(block, update_weights):
    state = block.astype(jnp.float32)
    members = state.shape[0]
    anomaly = (state - jnp.mean(state, axis=0, keepdims=True)) / math.sqrt(members - 1)
    moved = state + lax.dot_general(
        update_weights, anomaly, (((0,), (0,)), ((), ())), precision=lax.Precision.HIGHEST
    )
    return moved.astype(jnp.bfloat16)


def dense_body(
    amplitude_maps, kept_blocks, block_owner, observed, error_scale, perturbation, model_slab
):
    members, rows_here, map_width = amplitude_maps.shape
    devices = lax.axis_size("map")
    map_height = rows_here * devices
    table_w = dct_table(map_width)
    table_h = dct_table(map_height)
    rowwise = jnp.einsum(
        "ehw,kw->hke", amplitude_maps, table_w, preferred_element_type=jnp.float32
    ).astype(jnp.bfloat16)
    coefficients = jnp.einsum(
        "kh,hwe->wke",
        table_h,
        lax.all_to_all(rowwise, "map", split_axis=1, concat_axis=0, tiled=True),
        preferred_element_type=jnp.float32,
    ).astype(jnp.bfloat16)
    block_rows = coefficients.reshape(-1, BLK * members)
    candidates = block_rows.shape[0]
    keep_count = kept_blocks.shape[0]
    slot_count = devices * CAP
    dest_owner = block_owner[:, 0]
    positions = jnp.arange(keep_count, dtype=jnp.int32)
    earlier = (dest_owner[:, None] == dest_owner[None, :]) & (
        positions[None, :] < positions[:, None]
    )
    slot_rank = jnp.sum(earlier.astype(jnp.int32), axis=1)
    slot_index = dest_owner * CAP + slot_rank
    pick_slot = (slot_index[:, None] == jnp.arange(slot_count, dtype=jnp.int32)[None, :]).astype(
        jnp.bfloat16
    )
    weight_scale = members / (devices * keep_count * BLK)
    contract = (((0,), (0,)), ((), ()))
    pick_block = (kept_blocks[:, None] == jnp.arange(candidates, dtype=jnp.int32)[None, :]).astype(
        jnp.bfloat16
    )
    routing = lax.dot_general(
        pick_slot, pick_block, contract, preferred_element_type=jnp.float32
    ).astype(jnp.bfloat16)
    outgoing = jnp.dot(routing, block_rows, preferred_element_type=jnp.float32).astype(jnp.bfloat16)
    live_slots = jnp.sum(pick_slot.astype(jnp.float32), axis=0).astype(jnp.bfloat16)
    arrived, arrived_live = (
        lax.all_to_all(
            outgoing.reshape(devices, CAP, BLK * members),
            "map",
            split_axis=0,
            concat_axis=0,
            tiled=True,
        ),
        lax.all_to_all(
            live_slots.reshape(devices, CAP), "map", split_axis=0, concat_axis=0, tiled=True
        ),
    )
    predicted = arrived.reshape(-1, members).astype(jnp.float32)
    live_mask = jnp.repeat(arrived_live.astype(jnp.float32).reshape(-1), BLK)
    gram_matrix, cross_terms, data_misfit = gram_terms(
        predicted,
        observed.astype(jnp.float32),
        error_scale.astype(jnp.float32),
        perturbation.astype(jnp.float32),
        live_mask,
        weight_scale,
    )
    gram_matrix, cross_terms = lax.psum((gram_matrix, cross_terms), "map")
    update_weights = solve_weights(gram_matrix, cross_terms)
    updated_slab = update_state(model_slab, update_weights)
    return (updated_slab, update_weights, data_misfit)


def swap(value, delta):
    pairs = [(i, i ^ delta) for i in range(lax.axis_size("map"))]
    return lax.ppermute(value, "map", pairs)


VMEM = pl.BlockSpec(memory_space=pltpu.VMEM)
SMEM = pl.BlockSpec(memory_space=pltpu.SMEM)
HBM = pl.BlockSpec(memory_space=pltpu.HBM)


def by_row_kernel(maps_ref, out_ref, held_ref, arrived):
    width = maps_ref.shape[2]
    copies = []
    for i in range(width // LANE):
        part = pl.ds(i * LANE, LANE)
        copies.append(
            pltpu.make_async_copy(maps_ref.at[:, :, part], held_ref.at[i], arrived.at[i])
        )
        copies[i].start()
    for i in range(width // LANE):
        copies[i].wait()
        out_ref[:, :, i * LANE : (i + 1) * LANE] = jnp.swapaxes(held_ref[i], 0, 1)


def by_row(amplitude_maps):
    members, rows, width = amplitude_maps.shape
    parts = width // LANE
    return pl.pallas_call(
        by_row_kernel,
        in_specs=[HBM],
        out_specs=VMEM,
        out_shape=jax.ShapeDtypeStruct((rows, members, width), jnp.bfloat16),
        scratch_shapes=[
            pltpu.VMEM((parts, members, rows, LANE), jnp.bfloat16),
            pltpu.SemaphoreType.DMA((parts,)),
        ],
        compiler_params=pltpu.CompilerParams(vmem_limit_bytes=MAPS_LIMIT),
        cost_estimate=pl.CostEstimate(
            flops=0, bytes_accessed=4 * members * rows * width, transcendentals=0
        ),
        name="maps_by_row",
    )(amplitude_maps)


def shares_kernel(
    list0_ref, list1_ref, list2_ref, list3_ref, maps_ref, table_w_ref, table_h_ref,
    k0_ref, k1_ref, s0_ref, s1_ref,
    lists_ref, arrived, full_ref, pick_ref, row_ref, spread_ref,
):
    rows, members, width = maps_ref.shape
    devices, depth, _ = row_ref.shape
    keep = depth // rows
    height = table_h_ref.shape[0]
    per_column = height // BLK
    columns_here = width // devices
    me = lax.axis_index("map")
    copies = [
        pltpu.make_async_copy(ref, lists_ref.at[i], arrived.at[i])
        for i, ref in enumerate((list0_ref, list1_ref, list2_ref, list3_ref))
    ]
    for copy in copies:
        copy.start()

    def column_of(delta, p):
        number = lists_ref[delta // 4, delta % 4, p]
        if per_column & (per_column - 1) == 0:
            return number >> per_column.bit_length() - 1
        return lax.div(number, per_column)

    def row_of(delta, p):
        number = lists_ref[delta // 4, delta % 4, p]
        if per_column & (per_column - 1) == 0:
            return (number & per_column - 1) * BLK
        return lax.rem(number, per_column) * BLK

    full_ref[...] = table_w_ref[...].astype(jnp.float32)
    sample = lax.broadcasted_iota(jnp.int32, (height, depth), 0) - me * rows
    held = lax.broadcasted_iota(jnp.int32, (height, depth), 1) // keep
    spread_ref[...] = jnp.dot(
        table_h_ref[...], (sample == held).astype(jnp.bfloat16), preferred_element_type=jnp.float32
    )
    for copy in copies:
        copy.wait()
    for delta in range(devices):
        for p in range(keep):
            column = (me ^ delta) * columns_here + column_of(delta, p)
            pick_ref[pl.ds(delta * keep + p, 1), :] = full_ref[pl.ds(column, 1), :]
    pick = pick_ref[...].astype(jnp.bfloat16)
    for row in range(rows):
        rowwise = lax.dot_general(
            pick, maps_ref[row], (((1,), (1,)), ((), ())), preferred_element_type=jnp.float32
        ).astype(jnp.bfloat16)
        row_ref[:, row * keep : (row + 1) * keep, :] = rowwise.reshape(devices, keep, members)

    position = lax.broadcasted_iota(jnp.int32, (BLK, depth), 1) % keep
    for out_ref, low in ((s1_ref, 3), (k1_ref, 2), (s0_ref, 1), (k0_ref, 0)):
        for high in range(out_ref.shape[0]):
            delta = high * 4 + low
            wide = []
            for p in range(keep):
                start = pl.multiple_of(row_of(delta, p), BLK)
                wide.append(jnp.where(position == p, spread_ref[pl.ds(start, BLK), :], 0.0))
            wide = jnp.concatenate(wide, axis=0).astype(jnp.bfloat16)
            out_ref[high] = jnp.dot(
                wide, row_ref[delta], preferred_element_type=jnp.float32
            ).T


def shares(lists, maps, table_w, table_h):
    rows, members, width = maps.shape
    devices = sum(part.shape[0] for part in lists)
    keep = lists[0].shape[1] // 2
    depth = rows * keep
    out = jax.ShapeDtypeStruct((devices // 4, members, keep * BLK), jnp.float32)
    return pl.pallas_call(
        shares_kernel,
        in_specs=[VMEM] * 7,
        out_specs=[VMEM] * 4,
        out_shape=[out] * 4,
        scratch_shapes=[
            pltpu.SMEM((len(lists),) + lists[0].shape, jnp.int32),
            pltpu.SemaphoreType.DMA((len(lists),)),
            pltpu.VMEM(table_w.shape, jnp.float32),
            pltpu.VMEM((devices * keep, width), jnp.float32),
            pltpu.VMEM((devices, depth, members), jnp.bfloat16),
            pltpu.VMEM((table_h.shape[0], depth), jnp.float32),
        ],
        compiler_params=pltpu.CompilerParams(vmem_limit_bytes=VMEM_LIMIT),
        cost_estimate=pl.CostEstimate(
            flops=2 * devices * keep * width * rows * members,
            bytes_accessed=2 * rows * members * width,
            transcendentals=0,
        ),
        name="coefficient_shares",
    )(*lists, maps, table_w, table_h)


def split_noise_kernel(noise_ref, observed_ref, scale_ref, keep_ref, send_ref):
    members, slots = noise_ref.shape
    half = slots // 2
    core = lax.axis_index("map") & 1
    span = 2 * CAP * BLK // 2
    row = lax.broadcasted_iota(jnp.int32, (slots, slots), 0)
    lane = lax.broadcasted_iota(jnp.int32, (slots, slots), 1)
    kind = lane // half ^ core
    source = lane % half // span * (2 * span) + kind * span + lane % span
    picked = (row == source).astype(jnp.bfloat16)
    extra = jnp.zeros((keep_ref.shape[0] - members - 2, slots), jnp.float32)
    value = jnp.concatenate(
        [
            noise_ref[...].astype(jnp.float32),
            observed_ref[...].astype(jnp.float32).reshape(1, slots),
            scale_ref[...].astype(jnp.float32).reshape(1, slots),
            extra,
        ],
        axis=0,
    ).astype(jnp.bfloat16)
    moved = jnp.dot(value, picked, preferred_element_type=jnp.float32).astype(jnp.bfloat16)
    keep_ref[...] = moved[:, 0:half]
    send_ref[...] = moved[:, half:slots]


def split_noise(noise, observed, scale):
    members, slots = noise.shape
    rows = -(-(members + 2) // 16) * 16
    out = jax.ShapeDtypeStruct((rows, slots // 2), jnp.bfloat16)
    return pl.pallas_call(
        split_noise_kernel,
        in_specs=[VMEM] * 3,
        out_specs=[VMEM] * 2,
        out_shape=[out] * 2,
        compiler_params=pltpu.CompilerParams(vmem_limit_bytes=VMEM_LIMIT),
        name="split_noise",
    )(noise, observed, scale)


def select_noise_kernel(starts_ref, near_ref, far_ref, out_ref, wide_ref, rows_ref):
    rows, per = near_ref.shape[-2:]
    chips = out_ref.shape[0]
    keep = per // BLK
    chip = lax.axis_index("map") >> 1
    units = near_ref.shape[0] * near_ref.shape[1]
    wide_ref[:, rows:256] = jnp.zeros((wide_ref.shape[0], 256 - rows), jnp.float32)
    for i, ref in enumerate((near_ref, far_ref)):
        for z in range(near_ref.shape[0]):
            for c in range(near_ref.shape[1]):
                unit = i * units + z * near_ref.shape[1] + c
                wide_ref[unit * per : (unit + 1) * per, 0:rows] = ref[z, c].astype(jnp.float32).T
    for i in range(chips):
        for p in range(keep):
            start = pl.multiple_of(starts_ref[i * keep + p], BLK)
            rows_ref[p * BLK : (p + 1) * BLK, :] = wide_ref[pl.ds(start, BLK), :]
        out_ref[chip ^ i] = rows_ref[...].T[0:rows]


def select_noise(starts, near, far):
    rows, per = near.shape[-2:]
    chips = starts.shape[0] * BLK // per
    return pl.pallas_call(
        select_noise_kernel,
        in_specs=[SMEM, VMEM, VMEM],
        out_specs=VMEM,
        out_shape=jax.ShapeDtypeStruct((chips, rows, per), jnp.float32),
        scratch_shapes=[
            pltpu.VMEM((2 * near.shape[0] * near.shape[1] * per, 256), jnp.float32),
            pltpu.VMEM((per, 256), jnp.float32),
        ],
        compiler_params=pltpu.CompilerParams(vmem_limit_bytes=VMEM_LIMIT),
        name="select_noise",
    )(starts, near, far)


def gram_kernel(target_ref, noise_ref, *refs):
    predicted_refs = refs[:8]
    out_ref, predicted_ref, left_ref, right_ref, misfit_ref = refs[8:]
    groups, members, per = predicted_ref.shape
    coefficients = groups * per
    weight_scale = members / (2 * coefficients)
    chip = lax.axis_index("map") >> 1
    for i, ref in enumerate(predicted_refs):
        predicted_ref[chip ^ i] = ref[...].astype(jnp.float32)
    right_ref[...] = jnp.zeros_like(right_ref)
    for g in range(groups):
        noise = noise_ref[g]
        observed = noise[members : members + 1]
        scale = noise[members + 1 : members + 2]
        predicted = predicted_ref[g]
        center = jnp.sum(predicted, axis=0, keepdims=True) * (1.0 / members)
        anomaly = (predicted - center) * (1.0 / math.sqrt(members - 1))
        weight = weight_scale / (scale * scale)
        mismatch = observed + math.sqrt(inflation) * scale * noise[:members] - predicted
        here = pl.ds(g * per, per)
        left_ref[:, here] = anomaly * weight
        right_ref[0:members, here] = anomaly
        right_ref[256 : 256 + members, here] = mismatch
        relative = mismatch / scale
        misfit = jnp.sqrt(
            jnp.sum(relative * relative, axis=0, keepdims=True) * (1.0 / members) + epsilon
        )
        high = misfit.astype(jnp.bfloat16)
        rest = misfit - high.astype(jnp.float32)
        middle = rest.astype(jnp.bfloat16)
        low = (rest - middle.astype(jnp.float32)).astype(jnp.bfloat16)
        misfit_ref[0:1, here] = high.astype(jnp.float32)
        misfit_ref[1:2, here] = middle.astype(jnp.float32)
        misfit_ref[2:3, here] = low.astype(jnp.float32)
        misfit_ref[3:8, here] = jnp.zeros((5, per), jnp.float32)
    out_ref[0:members, :] = lax.dot_general(
        left_ref[...], right_ref[...], (((1,), (1,)), ((), ())),
        precision=lax.Precision.HIGHEST, preferred_element_type=jnp.float32,
    )
    lanes = lax.broadcasted_iota(jnp.int32, (per, out_ref.shape[1]), 1)
    one_hot = jnp.concatenate(
        [(target_ref[chip ^ g] == lanes).astype(jnp.bfloat16) for g in range(groups)], axis=0
    )
    routed = jnp.dot(
        misfit_ref[...].astype(jnp.bfloat16), one_hot, preferred_element_type=jnp.float32
    )
    out_ref[members : members + 8, :] = jnp.broadcast_to(
        routed[0:1] + routed[1:2] + routed[2:3], (8, out_ref.shape[1])
    )


def gram(target, noise, predicted):
    members, per = predicted[0].shape
    groups = len(predicted)
    coefficients = groups * per
    return pl.pallas_call(
        gram_kernel,
        in_specs=[VMEM] * (2 + len(predicted)),
        out_specs=VMEM,
        out_shape=jax.ShapeDtypeStruct((members + 8, 512), jnp.float32),
        scratch_shapes=[
            pltpu.VMEM((groups, members, per), jnp.float32),
            pltpu.VMEM((members, coefficients), jnp.float32),
            pltpu.VMEM((512, coefficients), jnp.float32),
            pltpu.VMEM((8, coefficients), jnp.float32),
        ],
        compiler_params=pltpu.CompilerParams(vmem_limit_bytes=VMEM_LIMIT),
        name="gram_and_cross",
    )(target, noise, *predicted)


def update_kernel(
    mine_ref, other_ref, slab_ref, out_ref, weights_ref, misfit_ref,
    state_ref, held_ref, arrived, left,
):
    members, cells = held_ref.shape
    tiles = left.shape[0]
    tile = cells // tiles
    parts = [pl.ds(i * tile, tile) for i in range(tiles)]
    writes = [
        pltpu.make_async_copy(held_ref.at[:, part], out_ref.at[:, part], left.at[i])
        for i, part in enumerate(parts)
    ]
    read = pltpu.make_async_copy(slab_ref, held_ref, arrived)
    read.start()

    total = mine_ref[0:members, :] + other_ref[0:members, :]
    misfit_ref[...] = (
        mine_ref[members : members + 1, 0:256] + other_ref[members : members + 1, 256:512]
    )
    row = lax.broadcasted_iota(jnp.int32, (members, 256), 0)
    lane = lax.broadcasted_iota(jnp.int32, (members, 256), 1)
    unit = jnp.where(row == lane, 1.0, 0.0)
    matrix = total[:, 0:256] + inflation * unit
    bound = jnp.max(jnp.sum(jnp.abs(matrix), axis=1, keepdims=True), axis=0, keepdims=True)
    step = 2.0 / (inflation + bound)
    state_ref[members:256, :] = jnp.zeros((256 - members, 512), jnp.float32)
    state_ref[0:members, 0:256] = unit - step * matrix
    state_ref[0:members, 256:512] = step * total[:, 256:512]

    def more(carry):
        return carry[0] > 2.0**-24

    def double(carry):
        power = state_ref[0:members, 0:256]
        size = jnp.sum(power * power)
        moved = jnp.dot(
            power, state_ref[...], precision=lax.Precision.HIGHEST,
            preferred_element_type=jnp.float32,
        )
        state_ref[0:members, 0:256] = moved[:, 0:256]
        state_ref[0:members, 256:512] = state_ref[0:members, 256:512] + moved[:, 256:512]
        return (size,)

    lax.while_loop(more, double, (jnp.float32(1.0),))
    weights_ref[...] = state_ref[0:members, 256 : 256 + members]

    full = state_ref[:, 256:512]
    center = jnp.sum(full, axis=0, keepdims=True) * (1.0 / members)
    spread = ((full - center) * (1.0 / math.sqrt(members - 1))).T[0:members, 0:members]
    high = spread.astype(jnp.bfloat16)
    rest = spread - high.astype(jnp.float32)
    low = rest.astype(jnp.bfloat16).astype(jnp.float32)
    over = jnp.sum(rest - low, axis=1, keepdims=True)
    lane = lax.broadcasted_iota(jnp.int32, (members, members), 1)
    low = (low + jnp.where(lane == 0, over, 0.0)).astype(jnp.bfloat16)
    read.wait()
    for i in range(tiles):
        for j in range(i * tile, (i + 1) * tile, 256):
            state = held_ref[:, j : j + 256]
            moved = jnp.dot(low, state, preferred_element_type=jnp.float32)
            moved = moved + jnp.dot(high, state, preferred_element_type=jnp.float32)
            held_ref[:, j : j + 256] = (state.astype(jnp.float32) + moved).astype(jnp.bfloat16)
        writes[i].start()
    for write in writes:
        write.wait()


def update(mine, other, slab):
    members, cells = slab.shape
    tiles = cells // 1024
    return pl.pallas_call(
        update_kernel,
        in_specs=[VMEM, VMEM, HBM],
        out_specs=[HBM, VMEM, VMEM],
        out_shape=[
            jax.ShapeDtypeStruct(slab.shape, slab.dtype),
            jax.ShapeDtypeStruct((members, members), jnp.float32),
            jax.ShapeDtypeStruct((1, 256), jnp.float32),
        ],
        scratch_shapes=[
            pltpu.VMEM((256, 512), jnp.float32),
            pltpu.VMEM(slab.shape, slab.dtype),
            pltpu.SemaphoreType.DMA,
            pltpu.SemaphoreType.DMA((tiles,)),
        ],
        compiler_params=pltpu.CompilerParams(vmem_limit_bytes=SLAB_LIMIT),
        name="solve_and_update",
    )(mine, other, slab)


def sparse_body(
    amplitude_maps, kept_blocks, block_owner, observed, error_scale, perturbation, model_slab
):
    members, rows_here, map_width = amplitude_maps.shape
    devices = lax.axis_size("map")
    map_height = rows_here * devices
    keep = kept_blocks.shape[0]
    slots = observed.shape[0]
    me = lax.axis_index("map").astype(jnp.int32)
    core, chip = me & 1, me >> 1

    lists = jnp.concatenate([kept_blocks, block_owner[:, 0]])
    lists = jnp.stack([lists] + [swap(lists, delta) for delta in range(1, 4)])

    noise_keep, noise_send = split_noise(perturbation.T, observed, error_scale)
    noise = jnp.stack([noise_keep, swap(noise_send, 1)])
    amplitude_maps, noise, lists = lax.optimization_barrier((amplitude_maps, noise, lists))
    lists = [lists] + [swap(lists, 4 * i) for i in range(1, devices // 4)]
    far_z = swap(noise, 8)

    maps = by_row(amplitude_maps)
    table_w = jnp.asarray(dct_constant(map_width))
    table_h = table_w if map_height == map_width else jnp.asarray(dct_constant(map_height))
    lists, far_z = lax.optimization_barrier((lists, far_z))
    keep_0, keep_1, send_0, send_1 = shares(lists, maps, table_w, table_h)

    share_1 = keep_1 + swap(send_1, 1)
    got_1 = swap(share_1, 2)
    share_0 = keep_0 + swap(send_0, 1)
    share = [share_0[i] + got_1[i] for i in range(devices // 4)]
    noise = jnp.stack([noise, far_z])
    near_z = swap(noise, 4)
    share, near_z = lax.optimization_barrier((share, near_z))
    near_noise = jnp.concatenate([noise, near_z])
    got = [swap(share[i], 4 * i) for i in range(1, devices // 4)]
    got[0], near_noise = lax.optimization_barrier((got[0], near_noise))
    far_noise = swap(near_noise, 2)
    predicted = (share[0] + got[0] + got[1] + got[2]).astype(jnp.bfloat16)

    near = [predicted] + [swap(predicted, 4 * i) for i in range(1, devices // 4)]
    near[3], far_noise = lax.optimization_barrier((near[3], far_noise))
    gathered = []
    for value in near:
        gathered += [value, swap(value, 2)]

    owner = jnp.concatenate(lists)[0::2, keep:]
    positions = jnp.arange(keep, dtype=jnp.int32)
    earlier = (owner[:, :, None] == owner[:, None, :]) & (
        positions[None, None, :] < positions[None, :, None]
    )
    rank = jnp.sum(earlier.astype(jnp.int32), axis=2)
    chips = chip ^ jnp.arange(devices // 2, dtype=jnp.int32)[:, None]
    away = owner ^ me
    held = (away >> 1 & 1) * 8 + (away >> 2 & 1) * 4 + (away >> 3) * 2 + (away & 1)
    noise_rows = held * (slots // 2) + chips * (CAP * BLK) + rank * BLK
    data_row = (chips * 2 + core) * (CAP * BLK) + rank * BLK
    target = jnp.where(away < 2, away * slots + data_row, -1024)
    target = (target[:, :, None] + jnp.arange(BLK, dtype=jnp.int32)).reshape(
        devices // 2, keep * BLK, 1
    )
    noise = select_noise(noise_rows.reshape(-1), near_noise, far_noise)
    mine = gram(target, noise, gathered)
    updated_slab, update_weights, data_misfit = update(mine, swap(mine, 1), model_slab)
    return (updated_slab, update_weights, data_misfit.reshape(-1))


def solution(mesh):
    in_specs = (
        P("groups", "map", None),
        P(("groups", "map")),
        P(("groups", "map"), None),
        P(("groups", "map")),
        P(("groups", "map")),
        P(("groups", "map"), None),
        P(None, ("groups", "map")),
    )
    out_specs = (P(None, ("groups", "map")), P("groups", None), P(("groups", "map")))

    def body(amplitude_maps, kept_blocks, *rest):
        few = mesh.shape["map"] == 16 and kept_blocks.shape[0] * BLK == LANE
        chosen = sparse_body if few else dense_body
        return chosen(amplitude_maps, kept_blocks, *rest)

    return jax.shard_map(body, mesh=mesh, in_specs=in_specs, out_specs=out_specs, check_vma=False)
```

```python
import math

import jax
import jax.numpy as jnp
import numpy as np
from jax import lax
from jax.experimental import pallas as pl
from jax.experimental.pallas import tpu as pltpu
from jax.sharding import PartitionSpec as P

BLK = 8
CAP = 2
LANE = 128

inflation = 4.0
epsilon = 1e-06
well_conditioned = 128.0

VMEM_LIMIT = 24 * 1024 * 1024
MAPS_LIMIT = 44 * 1024 * 1024
SLAB_LIMIT = 50 * 1024 * 1024


def dct_table(length):
    frequency = jnp.arange(length, dtype=jnp.float32)[:, None]
    sample = jnp.arange(length, dtype=jnp.float32)[None, :]
    cosine_table = jnp.cos(math.pi * (2.0 * sample + 1.0) * frequency / (2.0 * length))
    factor = jnp.where(frequency == 0, math.sqrt(1.0 / length), math.sqrt(2.0 / length))
    return (cosine_table * factor).astype(jnp.bfloat16)


def dct_constant(length):
    frequency = np.arange(length, dtype=np.float32)[:, None]
    sample = np.arange(length, dtype=np.float32)[None, :]
    angle = np.float32(math.pi) * (np.float32(2.0) * sample + np.float32(1.0)) * frequency
    cosine_table = np.cos(angle / np.float32(2.0 * length))
    factor = np.where(
        frequency == 0, np.float32(math.sqrt(1.0 / length)), np.float32(math.sqrt(2.0 / length))
    )
    return (cosine_table * factor).astype(jnp.bfloat16)


def gram_terms(predicted, observed_rows, scale_rows, noise_rows, live_mask, weight_scale):
    members = predicted.shape[1]
    center = jnp.mean(predicted, axis=1, keepdims=True)
    anomaly = (predicted - center) / math.sqrt(members - 1)
    weight = live_mask * weight_scale / (scale_rows * scale_rows)
    mismatch = (
        observed_rows[:, None] + math.sqrt(inflation) * scale_rows[:, None] * noise_rows - predicted
    )
    weighted = anomaly * weight[:, None]
    contract = (((0,), (0,)), ((), ()))
    gram_matrix = lax.dot_general(anomaly, weighted, contract, precision=lax.Precision.HIGHEST)
    cross_terms = lax.dot_general(weighted, mismatch, contract, precision=lax.Precision.HIGHEST)
    relative = mismatch / scale_rows[:, None]
    misfit_rows = live_mask * jnp.sqrt(jnp.mean(relative * relative, axis=1) + epsilon)
    return (gram_matrix, cross_terms, misfit_rows)


def solve_weights(gram_matrix, cross_terms):
    members = gram_matrix.shape[0]
    factor = jnp.linalg.cholesky(gram_matrix + inflation * jnp.eye(members, dtype=jnp.float32))
    return jax.scipy.linalg.cho_solve((factor, True), cross_terms)


def update_state(block, update_weights):
    state = block.astype(jnp.float32)
    members = state.shape[0]
    anomaly = (state - jnp.mean(state, axis=0, keepdims=True)) / math.sqrt(members - 1)
    moved = state + lax.dot_general(
        update_weights, anomaly, (((0,), (0,)), ((), ())), precision=lax.Precision.HIGHEST
    )
    return moved.astype(jnp.bfloat16)


def dense_body(
    amplitude_maps, kept_blocks, block_owner, observed, error_scale, perturbation, model_slab
):
    members, rows_here, map_width = amplitude_maps.shape
    devices = lax.axis_size("map")
    map_height = rows_here * devices
    table_w = dct_table(map_width)
    table_h = dct_table(map_height)
    rowwise = jnp.einsum(
        "ehw,kw->hke", amplitude_maps, table_w, preferred_element_type=jnp.float32
    ).astype(jnp.bfloat16)
    coefficients = jnp.einsum(
        "kh,hwe->wke",
        table_h,
        lax.all_to_all(rowwise, "map", split_axis=1, concat_axis=0, tiled=True),
        preferred_element_type=jnp.float32,
    ).astype(jnp.bfloat16)
    block_rows = coefficients.reshape(-1, BLK * members)
    candidates = block_rows.shape[0]
    keep_count = kept_blocks.shape[0]
    slot_count = devices * CAP
    dest_owner = block_owner[:, 0]
    positions = jnp.arange(keep_count, dtype=jnp.int32)
    earlier = (dest_owner[:, None] == dest_owner[None, :]) & (
        positions[None, :] < positions[:, None]
    )
    slot_rank = jnp.sum(earlier.astype(jnp.int32), axis=1)
    slot_index = dest_owner * CAP + slot_rank
    pick_slot = (slot_index[:, None] == jnp.arange(slot_count, dtype=jnp.int32)[None, :]).astype(
        jnp.bfloat16
    )
    weight_scale = members / (devices * keep_count * BLK)
    contract = (((0,), (0,)), ((), ()))
    pick_block = (kept_blocks[:, None] == jnp.arange(candidates, dtype=jnp.int32)[None, :]).astype(
        jnp.bfloat16
    )
    routing = lax.dot_general(
        pick_slot, pick_block, contract, preferred_element_type=jnp.float32
    ).astype(jnp.bfloat16)
    outgoing = jnp.dot(routing, block_rows, preferred_element_type=jnp.float32).astype(jnp.bfloat16)
    live_slots = jnp.sum(pick_slot.astype(jnp.float32), axis=0).astype(jnp.bfloat16)
    arrived, arrived_live = (
        lax.all_to_all(
            outgoing.reshape(devices, CAP, BLK * members),
            "map",
            split_axis=0,
            concat_axis=0,
            tiled=True,
        ),
        lax.all_to_all(
            live_slots.reshape(devices, CAP), "map", split_axis=0, concat_axis=0, tiled=True
        ),
    )
    predicted = arrived.reshape(-1, members).astype(jnp.float32)
    live_mask = jnp.repeat(arrived_live.astype(jnp.float32).reshape(-1), BLK)
    gram_matrix, cross_terms, data_misfit = gram_terms(
        predicted,
        observed.astype(jnp.float32),
        error_scale.astype(jnp.float32),
        perturbation.astype(jnp.float32),
        live_mask,
        weight_scale,
    )
    gram_matrix, cross_terms = lax.psum((gram_matrix, cross_terms), "map")
    update_weights = solve_weights(gram_matrix, cross_terms)
    updated_slab = update_state(model_slab, update_weights)
    return (updated_slab, update_weights, data_misfit)


def swap(value, delta):
    pairs = [(i, i ^ delta) for i in range(lax.axis_size("map"))]
    return lax.ppermute(value, "map", pairs)


VMEM = pl.BlockSpec(memory_space=pltpu.VMEM)
SMEM = pl.BlockSpec(memory_space=pltpu.SMEM)
HBM = pl.BlockSpec(memory_space=pltpu.HBM)


def by_row_kernel(maps_ref, out_ref, held_ref, arrived):
    width = maps_ref.shape[2]
    copies = []
    for i in range(width // LANE):
        part = pl.ds(i * LANE, LANE)
        copies.append(
            pltpu.make_async_copy(maps_ref.at[:, :, part], held_ref.at[i], arrived.at[i])
        )
        copies[i].start()
    for i in range(width // LANE):
        copies[i].wait()
        out_ref[:, :, i * LANE : (i + 1) * LANE] = jnp.swapaxes(held_ref[i], 0, 1)


def by_row(amplitude_maps):
    members, rows, width = amplitude_maps.shape
    parts = width // LANE
    return pl.pallas_call(
        by_row_kernel,
        in_specs=[HBM],
        out_specs=VMEM,
        out_shape=jax.ShapeDtypeStruct((rows, members, width), jnp.bfloat16),
        scratch_shapes=[
            pltpu.VMEM((parts, members, rows, LANE), jnp.bfloat16),
            pltpu.SemaphoreType.DMA((parts,)),
        ],
        compiler_params=pltpu.CompilerParams(vmem_limit_bytes=MAPS_LIMIT),
        cost_estimate=pl.CostEstimate(
            flops=0, bytes_accessed=4 * members * rows * width, transcendentals=0
        ),
        name="maps_by_row",
    )(amplitude_maps)


def shares_kernel(
    list0_ref, list1_ref, list2_ref, list3_ref, maps_ref, table_w_ref, table_h_ref,
    k0_ref, k1_ref, s0_ref, s1_ref,
    lists_ref, arrived, full_ref, pick_ref, row_ref, spread_ref,
):
    rows, members, width = maps_ref.shape
    devices, depth, _ = row_ref.shape
    keep = depth // rows
    height = table_h_ref.shape[0]
    per_column = height // BLK
    columns_here = width // devices
    me = lax.axis_index("map")
    copies = [
        pltpu.make_async_copy(ref, lists_ref.at[i], arrived.at[i])
        for i, ref in enumerate((list0_ref, list1_ref, list2_ref, list3_ref))
    ]
    for copy in copies:
        copy.start()

    def column_of(delta, p):
        number = lists_ref[delta // 4, delta % 4, p]
        if per_column & (per_column - 1) == 0:
            return number >> per_column.bit_length() - 1
        return lax.div(number, per_column)

    def row_of(delta, p):
        number = lists_ref[delta // 4, delta % 4, p]
        if per_column & (per_column - 1) == 0:
            return (number & per_column - 1) * BLK
        return lax.rem(number, per_column) * BLK

    full_ref[...] = table_w_ref[...].astype(jnp.float32)
    sample = lax.broadcasted_iota(jnp.int32, (height, depth), 0) - me * rows
    held = lax.broadcasted_iota(jnp.int32, (height, depth), 1) // keep
    spread_ref[...] = jnp.dot(
        table_h_ref[...], (sample == held).astype(jnp.bfloat16), preferred_element_type=jnp.float32
    )
    for copy in copies:
        copy.wait()
    for delta in range(devices):
        for p in range(keep):
            column = (me ^ delta) * columns_here + column_of(delta, p)
            pick_ref[pl.ds(delta * keep + p, 1), :] = full_ref[pl.ds(column, 1), :]
    pick = pick_ref[...].astype(jnp.bfloat16)
    for row in range(rows):
        rowwise = lax.dot_general(
            pick, maps_ref[row], (((1,), (1,)), ((), ())), preferred_element_type=jnp.float32
        ).astype(jnp.bfloat16)
        row_ref[:, row * keep : (row + 1) * keep, :] = rowwise.reshape(devices, keep, members)

    position = lax.broadcasted_iota(jnp.int32, (BLK, depth), 1) % keep
    for out_ref, low in ((s1_ref, 3), (k1_ref, 2), (s0_ref, 1), (k0_ref, 0)):
        for high in range(out_ref.shape[0]):
            delta = high * 4 + low
            wide = []
            for p in range(keep):
                start = pl.multiple_of(row_of(delta, p), BLK)
                wide.append(jnp.where(position == p, spread_ref[pl.ds(start, BLK), :], 0.0))
            wide = jnp.concatenate(wide, axis=0).astype(jnp.bfloat16)
            out_ref[high] = jnp.dot(
                wide, row_ref[delta], preferred_element_type=jnp.float32
            ).T


def shares(lists, maps, table_w, table_h):
    rows, members, width = maps.shape
    devices = sum(part.shape[0] for part in lists)
    keep = lists[0].shape[1] // 2
    depth = rows * keep
    out = jax.ShapeDtypeStruct((devices // 4, members, keep * BLK), jnp.float32)
    return pl.pallas_call(
        shares_kernel,
        in_specs=[VMEM] * 7,
        out_specs=[VMEM] * 4,
        out_shape=[out] * 4,
        scratch_shapes=[
            pltpu.SMEM((len(lists),) + lists[0].shape, jnp.int32),
            pltpu.SemaphoreType.DMA((len(lists),)),
            pltpu.VMEM(table_w.shape, jnp.float32),
            pltpu.VMEM((devices * keep, width), jnp.float32),
            pltpu.VMEM((devices, depth, members), jnp.bfloat16),
            pltpu.VMEM((table_h.shape[0], depth), jnp.float32),
        ],
        compiler_params=pltpu.CompilerParams(vmem_limit_bytes=VMEM_LIMIT),
        cost_estimate=pl.CostEstimate(
            flops=2 * devices * keep * width * rows * members,
            bytes_accessed=2 * rows * members * width,
            transcendentals=0,
        ),
        name="coefficient_shares",
    )(*lists, maps, table_w, table_h)


def split_noise_kernel(noise_ref, observed_ref, scale_ref, keep_ref, send_ref):
    members, slots = noise_ref.shape
    half = slots // 2
    core = lax.axis_index("map") & 1
    span = 2 * CAP * BLK // 2
    row = lax.broadcasted_iota(jnp.int32, (slots, slots), 0)
    lane = lax.broadcasted_iota(jnp.int32, (slots, slots), 1)
    kind = lane // half ^ core
    source = lane % half // span * (2 * span) + kind * span + lane % span
    picked = (row == source).astype(jnp.bfloat16)
    extra = jnp.zeros((keep_ref.shape[0] - members - 2, slots), jnp.float32)
    value = jnp.concatenate(
        [
            noise_ref[...].astype(jnp.float32),
            observed_ref[...].astype(jnp.float32).reshape(1, slots),
            scale_ref[...].astype(jnp.float32).reshape(1, slots),
            extra,
        ],
        axis=0,
    ).astype(jnp.bfloat16)
    moved = jnp.dot(value, picked, preferred_element_type=jnp.float32).astype(jnp.bfloat16)
    keep_ref[...] = moved[:, 0:half]
    send_ref[...] = moved[:, half:slots]


def split_noise(noise, observed, scale):
    members, slots = noise.shape
    rows = -(-(members + 2) // 16) * 16
    out = jax.ShapeDtypeStruct((rows, slots // 2), jnp.bfloat16)
    return pl.pallas_call(
        split_noise_kernel,
        in_specs=[VMEM] * 3,
        out_specs=[VMEM] * 2,
        out_shape=[out] * 2,
        compiler_params=pltpu.CompilerParams(vmem_limit_bytes=VMEM_LIMIT),
        name="split_noise",
    )(noise, observed, scale)


def select_noise_kernel(starts_ref, near_ref, far_ref, out_ref, wide_ref, rows_ref):
    rows, per = near_ref.shape[-2:]
    chips = out_ref.shape[0]
    keep = per // BLK
    chip = lax.axis_index("map") >> 1
    units = near_ref.shape[0] * near_ref.shape[1]
    wide_ref[:, rows:256] = jnp.zeros((wide_ref.shape[0], 256 - rows), jnp.float32)
    for i, ref in enumerate((near_ref, far_ref)):
        for z in range(near_ref.shape[0]):
            for c in range(near_ref.shape[1]):
                unit = i * units + z * near_ref.shape[1] + c
                wide_ref[unit * per : (unit + 1) * per, 0:rows] = ref[z, c].astype(jnp.float32).T
    for i in range(chips):
        for p in range(keep):
            start = pl.multiple_of(starts_ref[i * keep + p], BLK)
            rows_ref[p * BLK : (p + 1) * BLK, :] = wide_ref[pl.ds(start, BLK), :]
        out_ref[chip ^ i] = rows_ref[...].T[0:rows]


def select_noise(starts, near, far):
    rows, per = near.shape[-2:]
    chips = starts.shape[0] * BLK // per
    return pl.pallas_call(
        select_noise_kernel,
        in_specs=[SMEM, VMEM, VMEM],
        out_specs=VMEM,
        out_shape=jax.ShapeDtypeStruct((chips, rows, per), jnp.float32),
        scratch_shapes=[
            pltpu.VMEM((2 * near.shape[0] * near.shape[1] * per, 256), jnp.float32),
            pltpu.VMEM((per, 256), jnp.float32),
        ],
        compiler_params=pltpu.CompilerParams(vmem_limit_bytes=VMEM_LIMIT),
        name="select_noise",
    )(starts, near, far)


def gram_kernel(target_ref, noise_ref, *refs):
    predicted_refs = refs[:8]
    out_ref, predicted_ref, left_ref, right_ref, misfit_ref = refs[8:]
    groups, members, per = predicted_ref.shape
    coefficients = groups * per
    weight_scale = members / (2 * coefficients)
    chip = lax.axis_index("map") >> 1
    for i, ref in enumerate(predicted_refs):
        predicted_ref[chip ^ i] = ref[...].astype(jnp.float32)
    right_ref[...] = jnp.zeros_like(right_ref)
    for g in range(groups):
        noise = noise_ref[g]
        observed = noise[members : members + 1]
        scale = noise[members + 1 : members + 2]
        predicted = predicted_ref[g]
        center = jnp.sum(predicted, axis=0, keepdims=True) * (1.0 / members)
        anomaly = (predicted - center) * (1.0 / math.sqrt(members - 1))
        weight = weight_scale / (scale * scale)
        mismatch = observed + math.sqrt(inflation) * scale * noise[:members] - predicted
        here = pl.ds(g * per, per)
        left_ref[:, here] = anomaly * weight
        right_ref[0:members, here] = anomaly
        right_ref[256 : 256 + members, here] = mismatch
        relative = mismatch / scale
        misfit = jnp.sqrt(
            jnp.sum(relative * relative, axis=0, keepdims=True) * (1.0 / members) + epsilon
        )
        high = misfit.astype(jnp.bfloat16)
        rest = misfit - high.astype(jnp.float32)
        middle = rest.astype(jnp.bfloat16)
        low = (rest - middle.astype(jnp.float32)).astype(jnp.bfloat16)
        misfit_ref[0:1, here] = high.astype(jnp.float32)
        misfit_ref[1:2, here] = middle.astype(jnp.float32)
        misfit_ref[2:3, here] = low.astype(jnp.float32)
        misfit_ref[3:8, here] = jnp.zeros((5, per), jnp.float32)
    out_ref[0:members, :] = lax.dot_general(
        left_ref[...], right_ref[...], (((1,), (1,)), ((), ())),
        precision=lax.Precision.HIGHEST, preferred_element_type=jnp.float32,
    )
    lanes = lax.broadcasted_iota(jnp.int32, (per, out_ref.shape[1]), 1)
    one_hot = jnp.concatenate(
        [(target_ref[chip ^ g] == lanes).astype(jnp.bfloat16) for g in range(groups)], axis=0
    )
    routed = jnp.dot(
        misfit_ref[...].astype(jnp.bfloat16), one_hot, preferred_element_type=jnp.float32
    )
    out_ref[members : members + 8, :] = jnp.broadcast_to(
        routed[0:1] + routed[1:2] + routed[2:3], (8, out_ref.shape[1])
    )


def gram(target, noise, predicted):
    members, per = predicted[0].shape
    groups = len(predicted)
    coefficients = groups * per
    return pl.pallas_call(
        gram_kernel,
        in_specs=[VMEM] * (2 + len(predicted)),
        out_specs=VMEM,
        out_shape=jax.ShapeDtypeStruct((members + 8, 512), jnp.float32),
        scratch_shapes=[
            pltpu.VMEM((groups, members, per), jnp.float32),
            pltpu.VMEM((members, coefficients), jnp.float32),
            pltpu.VMEM((512, coefficients), jnp.float32),
            pltpu.VMEM((8, coefficients), jnp.float32),
        ],
        compiler_params=pltpu.CompilerParams(vmem_limit_bytes=VMEM_LIMIT),
        name="gram_and_cross",
    )(target, noise, *predicted)


def update_kernel(
    mine_ref, other_ref, slab_ref, out_ref, weights_ref, misfit_ref,
    state_ref, held_ref, arrived, left,
):
    members, cells = held_ref.shape
    tiles = left.shape[0]
    tile = cells // tiles
    parts = [pl.ds(i * tile, tile) for i in range(tiles)]
    writes = [
        pltpu.make_async_copy(held_ref.at[:, part], out_ref.at[:, part], left.at[i])
        for i, part in enumerate(parts)
    ]
    read = pltpu.make_async_copy(slab_ref, held_ref, arrived)
    read.start()

    total = mine_ref[0:members, :] + other_ref[0:members, :]
    misfit_ref[...] = (
        mine_ref[members : members + 1, 0:256] + other_ref[members : members + 1, 256:512]
    )
    row = lax.broadcasted_iota(jnp.int32, (members, 256), 0)
    lane = lax.broadcasted_iota(jnp.int32, (members, 256), 1)
    unit = jnp.where(row == lane, 1.0, 0.0)
    matrix = total[:, 0:256] + inflation * unit
    bound = jnp.max(jnp.sum(jnp.abs(matrix), axis=1, keepdims=True), axis=0, keepdims=True)
    step = 2.0 / (inflation + bound)
    state_ref[members:256, :] = jnp.zeros((256 - members, 512), jnp.float32)
    state_ref[0:members, 0:256] = unit - step * matrix
    state_ref[0:members, 256:512] = step * total[:, 256:512]

    def more(carry):
        return carry[0] > 2.0**-24

    def double(carry):
        power = state_ref[0:members, 0:256]
        size = jnp.sum(power * power)
        moved = jnp.dot(
            power, state_ref[...], precision=lax.Precision.HIGHEST,
            preferred_element_type=jnp.float32,
        )
        state_ref[0:members, 0:256] = moved[:, 0:256]
        state_ref[0:members, 256:512] = state_ref[0:members, 256:512] + moved[:, 256:512]
        return (size,)

    well = jnp.max(bound) <= well_conditioned * inflation
    lax.while_loop(more, double, (jnp.where(well, 1.0, 0.0),))

    @pl.when(jnp.logical_not(well))
    def _():
        state_ref[0:members, 0:256] = matrix
        state_ref[0:members, 256:512] = total[:, 256:512]

        def eliminate(k, carry):
            rows = state_ref[0:members, :]
            pivot_row = state_ref[pl.ds(k, 1), :]
            pivot = jnp.sum(
                jnp.where(lane[0:1] == k, pivot_row[:, 0:256], 0.0), axis=1, keepdims=True
            )
            column = jnp.sum(jnp.where(lane == k, rows[:, 0:256], 0.0), axis=1, keepdims=True)
            pivot_row = pivot_row / pivot
            state_ref[0:members, :] = jnp.where(
                row[:, 0:1] == k, pivot_row, rows - column * pivot_row
            )
            return carry

        lax.fori_loop(0, members, eliminate, 0)

    weights_ref[...] = state_ref[0:members, 256 : 256 + members]

    full = state_ref[:, 256:512]
    center = jnp.sum(full, axis=0, keepdims=True) * (1.0 / members)
    spread = ((full - center) * (1.0 / math.sqrt(members - 1))).T[0:members, 0:members]
    high = spread.astype(jnp.bfloat16)
    rest = spread - high.astype(jnp.float32)
    low = rest.astype(jnp.bfloat16).astype(jnp.float32)
    over = jnp.sum(rest - low, axis=1, keepdims=True)
    lane = lax.broadcasted_iota(jnp.int32, (members, members), 1)
    low = (low + jnp.where(lane == 0, over, 0.0)).astype(jnp.bfloat16)
    read.wait()
    for i in range(tiles):
        for j in range(i * tile, (i + 1) * tile, 256):
            state = held_ref[:, j : j + 256]
            moved = jnp.dot(low, state, preferred_element_type=jnp.float32)
            moved = moved + jnp.dot(high, state, preferred_element_type=jnp.float32)
            held_ref[:, j : j + 256] = (state.astype(jnp.float32) + moved).astype(jnp.bfloat16)
        writes[i].start()
    for write in writes:
        write.wait()


def update(mine, other, slab):
    members, cells = slab.shape
    tiles = cells // 1024
    return pl.pallas_call(
        update_kernel,
        in_specs=[VMEM, VMEM, HBM],
        out_specs=[HBM, VMEM, VMEM],
        out_shape=[
            jax.ShapeDtypeStruct(slab.shape, slab.dtype),
            jax.ShapeDtypeStruct((members, members), jnp.float32),
            jax.ShapeDtypeStruct((1, 256), jnp.float32),
        ],
        scratch_shapes=[
            pltpu.VMEM((256, 512), jnp.float32),
            pltpu.VMEM(slab.shape, slab.dtype),
            pltpu.SemaphoreType.DMA,
            pltpu.SemaphoreType.DMA((tiles,)),
        ],
        compiler_params=pltpu.CompilerParams(vmem_limit_bytes=SLAB_LIMIT),
        name="solve_and_update",
    )(mine, other, slab)


def sparse_body(
    amplitude_maps, kept_blocks, block_owner, observed, error_scale, perturbation, model_slab
):
    members, rows_here, map_width = amplitude_maps.shape
    devices = lax.axis_size("map")
    map_height = rows_here * devices
    keep = kept_blocks.shape[0]
    slots = observed.shape[0]
    me = lax.axis_index("map").astype(jnp.int32)
    core, chip = me & 1, me >> 1

    lists = jnp.concatenate([kept_blocks, block_owner[:, 0]])
    lists = jnp.stack([lists] + [swap(lists, delta) for delta in range(1, 4)])

    noise_keep, noise_send = split_noise(perturbation.T, observed, error_scale)
    noise = jnp.stack([noise_keep, swap(noise_send, 1)])
    amplitude_maps, noise, lists = lax.optimization_barrier((amplitude_maps, noise, lists))
    lists = [lists] + [swap(lists, 4 * i) for i in range(1, devices // 4)]
    far_z = swap(noise, 8)

    maps = by_row(amplitude_maps)
    table_w = jnp.asarray(dct_constant(map_width))
    table_h = table_w if map_height == map_width else jnp.asarray(dct_constant(map_height))
    lists, far_z = lax.optimization_barrier((lists, far_z))
    keep_0, keep_1, send_0, send_1 = shares(lists, maps, table_w, table_h)

    share_1 = keep_1 + swap(send_1, 1)
    got_1 = swap(share_1, 2)
    share_0 = keep_0 + swap(send_0, 1)
    share = [share_0[i] + got_1[i] for i in range(devices // 4)]
    noise = jnp.stack([noise, far_z])
    near_z = swap(noise, 4)
    share, near_z = lax.optimization_barrier((share, near_z))
    near_noise = jnp.concatenate([noise, near_z])
    got = [swap(share[i], 4 * i) for i in range(1, devices // 4)]
    got[0], near_noise = lax.optimization_barrier((got[0], near_noise))
    far_noise = swap(near_noise, 2)
    predicted = (share[0] + got[0] + got[1] + got[2]).astype(jnp.bfloat16)

    near = [predicted] + [swap(predicted, 4 * i) for i in range(1, devices // 4)]
    near[3], far_noise = lax.optimization_barrier((near[3], far_noise))
    gathered = []
    for value in near:
        gathered += [value, swap(value, 2)]

    owner = jnp.concatenate(lists)[0::2, keep:]
    positions = jnp.arange(keep, dtype=jnp.int32)
    earlier = (owner[:, :, None] == owner[:, None, :]) & (
        positions[None, None, :] < positions[None, :, None]
    )
    rank = jnp.sum(earlier.astype(jnp.int32), axis=2)
    chips = chip ^ jnp.arange(devices // 2, dtype=jnp.int32)[:, None]
    away = owner ^ me
    held = (away >> 1 & 1) * 8 + (away >> 2 & 1) * 4 + (away >> 3) * 2 + (away & 1)
    noise_rows = held * (slots // 2) + chips * (CAP * BLK) + rank * BLK
    data_row = (chips * 2 + core) * (CAP * BLK) + rank * BLK
    target = jnp.where(away < 2, away * slots + data_row, -1024)
    target = (target[:, :, None] + jnp.arange(BLK, dtype=jnp.int32)).reshape(
        devices // 2, keep * BLK, 1
    )
    noise = select_noise(noise_rows.reshape(-1), near_noise, far_noise)
    mine = gram(target, noise, gathered)
    updated_slab, update_weights, data_misfit = update(mine, swap(mine, 1), model_slab)
    return (updated_slab, update_weights, data_misfit.reshape(-1))


def solution(mesh):
    in_specs = (
        P("groups", "map", None),
        P(("groups", "map")),
        P(("groups", "map"), None),
        P(("groups", "map")),
        P(("groups", "map")),
        P(("groups", "map"), None),
        P(None, ("groups", "map")),
    )
    out_specs = (P(None, ("groups", "map")), P("groups", None), P(("groups", "map")))

    def body(amplitude_maps, kept_blocks, *rest):
        few = mesh.shape["map"] == 16 and kept_blocks.shape[0] * BLK == LANE
        chosen = sparse_body if few else dense_body
        return chosen(amplitude_maps, kept_blocks, *rest)

    return jax.shard_map(body, mesh=mesh, in_specs=in_specs, out_specs=out_specs, check_vma=False)
```

```python
import math

import jax
import jax.numpy as jnp
import numpy as np
from jax import lax
from jax.experimental import pallas as pl
from jax.experimental.pallas import tpu as pltpu
from jax.sharding import PartitionSpec as P

BLK = 8
CAP = 2
LANE = 128

inflation = 4.0
epsilon = 1e-06
well_conditioned = 128.0

VMEM_LIMIT = 24 * 1024 * 1024
MAPS_LIMIT = 44 * 1024 * 1024
SLAB_LIMIT = 50 * 1024 * 1024


def dct_table(length):
    frequency = jnp.arange(length, dtype=jnp.float32)[:, None]
    sample = jnp.arange(length, dtype=jnp.float32)[None, :]
    cosine_table = jnp.cos(math.pi * (2.0 * sample + 1.0) * frequency / (2.0 * length))
    factor = jnp.where(frequency == 0, math.sqrt(1.0 / length), math.sqrt(2.0 / length))
    return (cosine_table * factor).astype(jnp.bfloat16)


def dct_constant(length):
    frequency = np.arange(length, dtype=np.float32)[:, None]
    sample = np.arange(length, dtype=np.float32)[None, :]
    angle = np.float32(math.pi) * (np.float32(2.0) * sample + np.float32(1.0)) * frequency
    cosine_table = np.cos(angle / np.float32(2.0 * length))
    factor = np.where(
        frequency == 0, np.float32(math.sqrt(1.0 / length)), np.float32(math.sqrt(2.0 / length))
    )
    return (cosine_table * factor).astype(jnp.bfloat16)


def gram_terms(predicted, observed_rows, scale_rows, noise_rows, live_mask, weight_scale):
    members = predicted.shape[1]
    center = jnp.mean(predicted, axis=1, keepdims=True)
    anomaly = (predicted - center) / math.sqrt(members - 1)
    weight = live_mask * weight_scale / (scale_rows * scale_rows)
    mismatch = (
        observed_rows[:, None] + math.sqrt(inflation) * scale_rows[:, None] * noise_rows - predicted
    )
    weighted = anomaly * weight[:, None]
    contract = (((0,), (0,)), ((), ()))
    gram_matrix = lax.dot_general(anomaly, weighted, contract, precision=lax.Precision.HIGHEST)
    cross_terms = lax.dot_general(weighted, mismatch, contract, precision=lax.Precision.HIGHEST)
    relative = mismatch / scale_rows[:, None]
    misfit_rows = live_mask * jnp.sqrt(jnp.mean(relative * relative, axis=1) + epsilon)
    return (gram_matrix, cross_terms, misfit_rows)


def solve_weights(gram_matrix, cross_terms):
    members = gram_matrix.shape[0]
    factor = jnp.linalg.cholesky(gram_matrix + inflation * jnp.eye(members, dtype=jnp.float32))
    return jax.scipy.linalg.cho_solve((factor, True), cross_terms)


def update_state(block, update_weights):
    state = block.astype(jnp.float32)
    members = state.shape[0]
    anomaly = (state - jnp.mean(state, axis=0, keepdims=True)) / math.sqrt(members - 1)
    moved = state + lax.dot_general(
        update_weights, anomaly, (((0,), (0,)), ((), ())), precision=lax.Precision.HIGHEST
    )
    return moved.astype(jnp.bfloat16)


def dense_body(
    amplitude_maps, kept_blocks, block_owner, observed, error_scale, perturbation, model_slab
):
    members, rows_here, map_width = amplitude_maps.shape
    devices = lax.axis_size("map")
    map_height = rows_here * devices
    table_w = dct_table(map_width)
    table_h = dct_table(map_height)
    rowwise = jnp.einsum(
        "ehw,kw->hke", amplitude_maps, table_w, preferred_element_type=jnp.float32
    ).astype(jnp.bfloat16)
    coefficients = jnp.einsum(
        "kh,hwe->wke",
        table_h,
        lax.all_to_all(rowwise, "map", split_axis=1, concat_axis=0, tiled=True),
        preferred_element_type=jnp.float32,
    ).astype(jnp.bfloat16)
    block_rows = coefficients.reshape(-1, BLK * members)
    candidates = block_rows.shape[0]
    keep_count = kept_blocks.shape[0]
    slot_count = devices * CAP
    dest_owner = block_owner[:, 0]
    positions = jnp.arange(keep_count, dtype=jnp.int32)
    earlier = (dest_owner[:, None] == dest_owner[None, :]) & (
        positions[None, :] < positions[:, None]
    )
    slot_rank = jnp.sum(earlier.astype(jnp.int32), axis=1)
    slot_index = dest_owner * CAP + slot_rank
    pick_slot = (slot_index[:, None] == jnp.arange(slot_count, dtype=jnp.int32)[None, :]).astype(
        jnp.bfloat16
    )
    weight_scale = members / (devices * keep_count * BLK)
    contract = (((0,), (0,)), ((), ()))
    pick_block = (kept_blocks[:, None] == jnp.arange(candidates, dtype=jnp.int32)[None, :]).astype(
        jnp.bfloat16
    )
    routing = lax.dot_general(
        pick_slot, pick_block, contract, preferred_element_type=jnp.float32
    ).astype(jnp.bfloat16)
    outgoing = jnp.dot(routing, block_rows, preferred_element_type=jnp.float32).astype(jnp.bfloat16)
    live_slots = jnp.sum(pick_slot.astype(jnp.float32), axis=0).astype(jnp.bfloat16)
    arrived, arrived_live = (
        lax.all_to_all(
            outgoing.reshape(devices, CAP, BLK * members),
            "map",
            split_axis=0,
            concat_axis=0,
            tiled=True,
        ),
        lax.all_to_all(
            live_slots.reshape(devices, CAP), "map", split_axis=0, concat_axis=0, tiled=True
        ),
    )
    predicted = arrived.reshape(-1, members).astype(jnp.float32)
    live_mask = jnp.repeat(arrived_live.astype(jnp.float32).reshape(-1), BLK)
    gram_matrix, cross_terms, data_misfit = gram_terms(
        predicted,
        observed.astype(jnp.float32),
        error_scale.astype(jnp.float32),
        perturbation.astype(jnp.float32),
        live_mask,
        weight_scale,
    )
    gram_matrix, cross_terms = lax.psum((gram_matrix, cross_terms), "map")
    update_weights = solve_weights(gram_matrix, cross_terms)
    updated_slab = update_state(model_slab, update_weights)
    return (updated_slab, update_weights, data_misfit)


def swap(value, delta):
    pairs = [(i, i ^ delta) for i in range(lax.axis_size("map"))]
    return lax.ppermute(value, "map", pairs)


VMEM = pl.BlockSpec(memory_space=pltpu.VMEM)
SMEM = pl.BlockSpec(memory_space=pltpu.SMEM)
HBM = pl.BlockSpec(memory_space=pltpu.HBM)


def by_row_kernel(maps_ref, out_ref, held_ref, arrived):
    width = maps_ref.shape[2]
    copies = []
    for i in range(width // LANE):
        part = pl.ds(i * LANE, LANE)
        copies.append(
            pltpu.make_async_copy(maps_ref.at[:, :, part], held_ref.at[i], arrived.at[i])
        )
        copies[i].start()
    for i in range(width // LANE):
        copies[i].wait()
        out_ref[:, :, i * LANE : (i + 1) * LANE] = jnp.swapaxes(held_ref[i], 0, 1)


def by_row(amplitude_maps):
    members, rows, width = amplitude_maps.shape
    parts = width // LANE
    return pl.pallas_call(
        by_row_kernel,
        in_specs=[HBM],
        out_specs=VMEM,
        out_shape=jax.ShapeDtypeStruct((rows, members, width), jnp.bfloat16),
        scratch_shapes=[
            pltpu.VMEM((parts, members, rows, LANE), jnp.bfloat16),
            pltpu.SemaphoreType.DMA((parts,)),
        ],
        compiler_params=pltpu.CompilerParams(vmem_limit_bytes=MAPS_LIMIT),
        cost_estimate=pl.CostEstimate(
            flops=0, bytes_accessed=4 * members * rows * width, transcendentals=0
        ),
        name="maps_by_row",
    )(amplitude_maps)


def shares_kernel(
    list0_ref, list1_ref, list2_ref, list3_ref, maps_ref, table_w_ref, table_h_ref,
    k0_ref, k1_ref, s0_ref, s1_ref,
    lists_ref, arrived, full_ref, pick_ref, row_ref, spread_ref,
):
    rows, members, width = maps_ref.shape
    devices, depth, _ = row_ref.shape
    keep = depth // rows
    height = table_h_ref.shape[0]
    per_column = height // BLK
    columns_here = width // devices
    me = lax.axis_index("map")
    copies = [
        pltpu.make_async_copy(ref, lists_ref.at[i], arrived.at[i])
        for i, ref in enumerate((list0_ref, list1_ref, list2_ref, list3_ref))
    ]
    for copy in copies:
        copy.start()

    def column_of(delta, p):
        number = lists_ref[delta // 4, delta % 4, p]
        if per_column & (per_column - 1) == 0:
            return number >> per_column.bit_length() - 1
        return lax.div(number, per_column)

    def row_of(delta, p):
        number = lists_ref[delta // 4, delta % 4, p]
        if per_column & (per_column - 1) == 0:
            return (number & per_column - 1) * BLK
        return lax.rem(number, per_column) * BLK

    full_ref[...] = table_w_ref[...].astype(jnp.float32)
    sample = lax.broadcasted_iota(jnp.int32, (height, depth), 0) - me * rows
    held = lax.broadcasted_iota(jnp.int32, (height, depth), 1) // keep
    spread_ref[...] = jnp.dot(
        table_h_ref[...], (sample == held).astype(jnp.bfloat16), preferred_element_type=jnp.float32
    )
    for copy in copies:
        copy.wait()
    for delta in range(devices):
        for p in range(keep):
            column = (me ^ delta) * columns_here + column_of(delta, p)
            pick_ref[pl.ds(delta * keep + p, 1), :] = full_ref[pl.ds(column, 1), :]
    pick = pick_ref[...].astype(jnp.bfloat16)
    for row in range(rows):
        rowwise = lax.dot_general(
            pick, maps_ref[row], (((1,), (1,)), ((), ())), preferred_element_type=jnp.float32
        ).astype(jnp.bfloat16)
        row_ref[:, row * keep : (row + 1) * keep, :] = rowwise.reshape(devices, keep, members)

    position = lax.broadcasted_iota(jnp.int32, (BLK, depth), 1) % keep
    for out_ref, low in ((s1_ref, 3), (k1_ref, 2), (s0_ref, 1), (k0_ref, 0)):
        for high in range(out_ref.shape[0]):
            delta = high * 4 + low
            wide = []
            for p in range(keep):
                start = pl.multiple_of(row_of(delta, p), BLK)
                wide.append(jnp.where(position == p, spread_ref[pl.ds(start, BLK), :], 0.0))
            wide = jnp.concatenate(wide, axis=0).astype(jnp.bfloat16)
            out_ref[high] = jnp.dot(
                wide, row_ref[delta], preferred_element_type=jnp.float32
            ).T


def shares(lists, maps, table_w, table_h):
    rows, members, width = maps.shape
    devices = sum(part.shape[0] for part in lists)
    keep = lists[0].shape[1] // 2
    depth = rows * keep
    out = jax.ShapeDtypeStruct((devices // 4, members, keep * BLK), jnp.float32)
    return pl.pallas_call(
        shares_kernel,
        in_specs=[VMEM] * 7,
        out_specs=[VMEM] * 4,
        out_shape=[out] * 4,
        scratch_shapes=[
            pltpu.SMEM((len(lists),) + lists[0].shape, jnp.int32),
            pltpu.SemaphoreType.DMA((len(lists),)),
            pltpu.VMEM(table_w.shape, jnp.float32),
            pltpu.VMEM((devices * keep, width), jnp.float32),
            pltpu.VMEM((devices, depth, members), jnp.bfloat16),
            pltpu.VMEM((table_h.shape[0], depth), jnp.float32),
        ],
        compiler_params=pltpu.CompilerParams(vmem_limit_bytes=VMEM_LIMIT),
        cost_estimate=pl.CostEstimate(
            flops=2 * devices * keep * width * rows * members,
            bytes_accessed=2 * rows * members * width,
            transcendentals=0,
        ),
        name="coefficient_shares",
    )(*lists, maps, table_w, table_h)


def split_noise_kernel(noise_ref, observed_ref, scale_ref, keep_ref, send_ref):
    members, slots = noise_ref.shape
    half = slots // 2
    core = lax.axis_index("map") & 1
    span = 2 * CAP * BLK // 2
    row = lax.broadcasted_iota(jnp.int32, (slots, slots), 0)
    lane = lax.broadcasted_iota(jnp.int32, (slots, slots), 1)
    kind = lane // half ^ core
    source = lane % half // span * (2 * span) + kind * span + lane % span
    picked = (row == source).astype(jnp.bfloat16)
    extra = jnp.zeros((keep_ref.shape[0] - members - 2, slots), jnp.float32)
    value = jnp.concatenate(
        [
            noise_ref[...].astype(jnp.float32),
            observed_ref[...].astype(jnp.float32).reshape(1, slots),
            scale_ref[...].astype(jnp.float32).reshape(1, slots),
            extra,
        ],
        axis=0,
    ).astype(jnp.bfloat16)
    moved = jnp.dot(value, picked, preferred_element_type=jnp.float32).astype(jnp.bfloat16)
    keep_ref[...] = moved[:, 0:half]
    send_ref[...] = moved[:, half:slots]


def split_noise(noise, observed, scale):
    members, slots = noise.shape
    rows = -(-(members + 2) // 16) * 16
    out = jax.ShapeDtypeStruct((rows, slots // 2), jnp.bfloat16)
    return pl.pallas_call(
        split_noise_kernel,
        in_specs=[VMEM] * 3,
        out_specs=[VMEM] * 2,
        out_shape=[out] * 2,
        compiler_params=pltpu.CompilerParams(vmem_limit_bytes=VMEM_LIMIT),
        name="split_noise",
    )(noise, observed, scale)


def select_noise_kernel(starts_ref, near_ref, far_ref, out_ref, wide_ref, rows_ref):
    rows, per = near_ref.shape[-2:]
    chips = out_ref.shape[0]
    keep = per // BLK
    chip = lax.axis_index("map") >> 1
    units = near_ref.shape[0] * near_ref.shape[1]
    wide_ref[:, rows:256] = jnp.zeros((wide_ref.shape[0], 256 - rows), jnp.float32)
    for i, ref in enumerate((near_ref, far_ref)):
        for z in range(near_ref.shape[0]):
            for c in range(near_ref.shape[1]):
                unit = i * units + z * near_ref.shape[1] + c
                wide_ref[unit * per : (unit + 1) * per, 0:rows] = ref[z, c].astype(jnp.float32).T
    for i in range(chips):
        for p in range(keep):
            start = pl.multiple_of(starts_ref[i * keep + p], BLK)
            rows_ref[p * BLK : (p + 1) * BLK, :] = wide_ref[pl.ds(start, BLK), :]
        out_ref[chip ^ i] = rows_ref[...].T[0:rows]


def select_noise(starts, near, far):
    rows, per = near.shape[-2:]
    chips = starts.shape[0] * BLK // per
    return pl.pallas_call(
        select_noise_kernel,
        in_specs=[SMEM, VMEM, VMEM],
        out_specs=VMEM,
        out_shape=jax.ShapeDtypeStruct((chips, rows, per), jnp.float32),
        scratch_shapes=[
            pltpu.VMEM((2 * near.shape[0] * near.shape[1] * per, 256), jnp.float32),
            pltpu.VMEM((per, 256), jnp.float32),
        ],
        compiler_params=pltpu.CompilerParams(vmem_limit_bytes=VMEM_LIMIT),
        name="select_noise",
    )(starts, near, far)


def gram_kernel(target_ref, noise_ref, *refs):
    predicted_refs = refs[:8]
    out_ref, predicted_ref, left_ref, right_ref, misfit_ref = refs[8:]
    groups, members, per = predicted_ref.shape
    coefficients = groups * per
    weight_scale = members / (2 * coefficients)
    chip = lax.axis_index("map") >> 1
    for i, ref in enumerate(predicted_refs):
        predicted_ref[chip ^ i] = ref[...].astype(jnp.float32)
    padding = jnp.zeros((256 - members, coefficients), jnp.float32)
    right_ref[members:256, :] = padding
    right_ref[256 + members : 512, :] = padding
    for g in range(groups):
        noise = noise_ref[g]
        observed = noise[members : members + 1]
        scale = noise[members + 1 : members + 2]
        predicted = predicted_ref[g]
        center = jnp.sum(predicted, axis=0, keepdims=True) * (1.0 / members)
        anomaly = (predicted - center) * (1.0 / math.sqrt(members - 1))
        weight = weight_scale / (scale * scale)
        mismatch = observed + math.sqrt(inflation) * scale * noise[:members] - predicted
        here = pl.ds(g * per, per)
        left_ref[:, here] = anomaly * weight
        right_ref[0:members, here] = anomaly
        right_ref[256 : 256 + members, here] = mismatch
        relative = mismatch / scale
        misfit = jnp.sqrt(
            jnp.sum(relative * relative, axis=0, keepdims=True) * (1.0 / members) + epsilon
        )
        high = misfit.astype(jnp.bfloat16)
        rest = misfit - high.astype(jnp.float32)
        middle = rest.astype(jnp.bfloat16)
        low = (rest - middle.astype(jnp.float32)).astype(jnp.bfloat16)
        misfit_ref[0:1, here] = high.astype(jnp.float32)
        misfit_ref[1:2, here] = middle.astype(jnp.float32)
        misfit_ref[2:3, here] = low.astype(jnp.float32)
        misfit_ref[3:8, here] = jnp.zeros((5, per), jnp.float32)
    out_ref[0:members, :] = lax.dot_general(
        left_ref[...], right_ref[...], (((1,), (1,)), ((), ())),
        precision=lax.Precision.HIGHEST, preferred_element_type=jnp.float32,
    )
    lanes = lax.broadcasted_iota(jnp.int32, (per, out_ref.shape[1]), 1)
    one_hot = jnp.concatenate(
        [(target_ref[chip ^ g] == lanes).astype(jnp.bfloat16) for g in range(groups)], axis=0
    )
    routed = jnp.dot(
        misfit_ref[...].astype(jnp.bfloat16), one_hot, preferred_element_type=jnp.float32
    )
    out_ref[members : members + 8, :] = jnp.broadcast_to(
        routed[0:1] + routed[1:2] + routed[2:3], (8, out_ref.shape[1])
    )


def gram(target, noise, predicted):
    members, per = predicted[0].shape
    groups = len(predicted)
    coefficients = groups * per
    return pl.pallas_call(
        gram_kernel,
        in_specs=[VMEM] * (2 + len(predicted)),
        out_specs=VMEM,
        out_shape=jax.ShapeDtypeStruct((members + 8, 512), jnp.float32),
        scratch_shapes=[
            pltpu.VMEM((groups, members, per), jnp.float32),
            pltpu.VMEM((members, coefficients), jnp.float32),
            pltpu.VMEM((512, coefficients), jnp.float32),
            pltpu.VMEM((8, coefficients), jnp.float32),
        ],
        compiler_params=pltpu.CompilerParams(vmem_limit_bytes=VMEM_LIMIT),
        name="gram_and_cross",
    )(target, noise, *predicted)


def update_kernel(
    mine_ref, other_ref, slab_ref, out_ref, weights_ref, misfit_ref,
    state_ref, held_ref, arrived, left,
):
    members, cells = held_ref.shape
    tiles = left.shape[0]
    tile = cells // tiles
    parts = [pl.ds(i * tile, tile) for i in range(tiles)]
    writes = [
        pltpu.make_async_copy(held_ref.at[:, part], out_ref.at[:, part], left.at[i])
        for i, part in enumerate(parts)
    ]
    read = pltpu.make_async_copy(slab_ref, held_ref, arrived)
    read.start()

    total = mine_ref[0:members, :] + other_ref[0:members, :]
    misfit_ref[...] = (
        mine_ref[members : members + 1, 0:256] + other_ref[members : members + 1, 256:512]
    )
    row = lax.broadcasted_iota(jnp.int32, (members, 256), 0)
    lane = lax.broadcasted_iota(jnp.int32, (members, 256), 1)
    unit = jnp.where(row == lane, 1.0, 0.0)
    matrix = total[:, 0:256] + inflation * unit
    bound = jnp.max(jnp.sum(jnp.abs(matrix), axis=1, keepdims=True), axis=0, keepdims=True)
    step = 2.0 / (inflation + bound)
    state_ref[members:256, :] = jnp.zeros((256 - members, 512), jnp.float32)
    state_ref[0:members, 0:256] = unit - step * matrix
    state_ref[0:members, 256:512] = step * total[:, 256:512]

    def more(carry):
        return carry[0] > 2.0**-24

    def double(carry):
        power = state_ref[0:members, 0:256]
        size = jnp.sum(power * power)
        moved = jnp.dot(
            power, state_ref[...], precision=lax.Precision.HIGHEST,
            preferred_element_type=jnp.float32,
        )
        state_ref[0:members, 0:256] = moved[:, 0:256]
        state_ref[0:members, 256:512] = state_ref[0:members, 256:512] + moved[:, 256:512]
        return (size,)

    well = jnp.max(bound) <= well_conditioned * inflation
    lax.while_loop(more, double, (jnp.where(well, 1.0, 0.0),))

    @pl.when(jnp.logical_not(well))
    def _():
        state_ref[0:members, 0:256] = matrix
        state_ref[0:members, 256:512] = total[:, 256:512]

        def eliminate(k, carry):
            rows = state_ref[0:members, :]
            pivot_row = state_ref[pl.ds(k, 1), :]
            pivot = jnp.sum(
                jnp.where(lane[0:1] == k, pivot_row[:, 0:256], 0.0), axis=1, keepdims=True
            )
            column = jnp.sum(jnp.where(lane == k, rows[:, 0:256], 0.0), axis=1, keepdims=True)
            pivot_row = pivot_row / pivot
            state_ref[0:members, :] = jnp.where(
                row[:, 0:1] == k, pivot_row, rows - column * pivot_row
            )
            return carry

        lax.fori_loop(0, members, eliminate, 0)

    weights_ref[...] = state_ref[0:members, 256 : 256 + members]

    full = state_ref[:, 256:512]
    center = jnp.sum(full, axis=0, keepdims=True) * (1.0 / members)
    spread = ((full - center) * (1.0 / math.sqrt(members - 1))).T[0:members, 0:members]
    high = spread.astype(jnp.bfloat16)
    rest = spread - high.astype(jnp.float32)
    low = rest.astype(jnp.bfloat16).astype(jnp.float32)
    over = jnp.sum(rest - low, axis=1, keepdims=True)
    lane = lax.broadcasted_iota(jnp.int32, (members, members), 1)
    low = (low + jnp.where(lane == 0, over, 0.0)).astype(jnp.bfloat16)
    read.wait()
    for i in range(tiles):
        for j in range(i * tile, (i + 1) * tile, 256):
            state = held_ref[:, j : j + 256]
            moved = jnp.dot(low, state, preferred_element_type=jnp.float32)
            moved = moved + jnp.dot(high, state, preferred_element_type=jnp.float32)
            held_ref[:, j : j + 256] = (state.astype(jnp.float32) + moved).astype(jnp.bfloat16)
        writes[i].start()
    for write in writes:
        write.wait()


def update(mine, other, slab):
    members, cells = slab.shape
    tiles = cells // 1024
    return pl.pallas_call(
        update_kernel,
        in_specs=[VMEM, VMEM, HBM],
        out_specs=[HBM, VMEM, VMEM],
        out_shape=[
            jax.ShapeDtypeStruct(slab.shape, slab.dtype),
            jax.ShapeDtypeStruct((members, members), jnp.float32),
            jax.ShapeDtypeStruct((1, 256), jnp.float32),
        ],
        scratch_shapes=[
            pltpu.VMEM((256, 512), jnp.float32),
            pltpu.VMEM(slab.shape, slab.dtype),
            pltpu.SemaphoreType.DMA,
            pltpu.SemaphoreType.DMA((tiles,)),
        ],
        compiler_params=pltpu.CompilerParams(vmem_limit_bytes=SLAB_LIMIT),
        name="solve_and_update",
    )(mine, other, slab)


def sparse_body(
    amplitude_maps, kept_blocks, block_owner, observed, error_scale, perturbation, model_slab
):
    members, rows_here, map_width = amplitude_maps.shape
    devices = lax.axis_size("map")
    map_height = rows_here * devices
    keep = kept_blocks.shape[0]
    slots = observed.shape[0]
    me = lax.axis_index("map").astype(jnp.int32)
    core, chip = me & 1, me >> 1

    lists = jnp.concatenate([kept_blocks, block_owner[:, 0]])
    lists = jnp.stack([lists] + [swap(lists, delta) for delta in range(1, 4)])

    noise_keep, noise_send = split_noise(perturbation.T, observed, error_scale)
    noise = jnp.stack([noise_keep, swap(noise_send, 1)])
    amplitude_maps, noise, lists = lax.optimization_barrier((amplitude_maps, noise, lists))
    lists = [lists] + [swap(lists, 4 * i) for i in range(1, devices // 4)]
    far_z = swap(noise, 8)

    maps = by_row(amplitude_maps)
    table_w = jnp.asarray(dct_constant(map_width))
    table_h = table_w if map_height == map_width else jnp.asarray(dct_constant(map_height))
    lists, far_z = lax.optimization_barrier((lists, far_z))
    keep_0, keep_1, send_0, send_1 = shares(lists, maps, table_w, table_h)

    share_1 = keep_1 + swap(send_1, 1)
    got_1 = swap(share_1, 2)
    share_0 = keep_0 + swap(send_0, 1)
    share = [share_0[i] + got_1[i] for i in range(devices // 4)]
    noise = jnp.stack([noise, far_z])
    near_z = swap(noise, 4)
    share, near_z = lax.optimization_barrier((share, near_z))
    near_noise = jnp.concatenate([noise, near_z])
    got = [swap(share[i], 4 * i) for i in range(1, devices // 4)]
    got[0], near_noise = lax.optimization_barrier((got[0], near_noise))
    far_noise = swap(near_noise, 2)
    predicted = (share[0] + got[0] + got[1] + got[2]).astype(jnp.bfloat16)

    near = [predicted] + [swap(predicted, 4 * i) for i in range(1, devices // 4)]
    near[3], far_noise = lax.optimization_barrier((near[3], far_noise))
    gathered = []
    for value in near:
        gathered += [value, swap(value, 2)]

    owner = jnp.concatenate(lists)[0::2, keep:]
    positions = jnp.arange(keep, dtype=jnp.int32)
    earlier = (owner[:, :, None] == owner[:, None, :]) & (
        positions[None, None, :] < positions[None, :, None]
    )
    rank = jnp.sum(earlier.astype(jnp.int32), axis=2)
    chips = chip ^ jnp.arange(devices // 2, dtype=jnp.int32)[:, None]
    away = owner ^ me
    held = (away >> 1 & 1) * 8 + (away >> 2 & 1) * 4 + (away >> 3) * 2 + (away & 1)
    noise_rows = held * (slots // 2) + chips * (CAP * BLK) + rank * BLK
    data_row = (chips * 2 + core) * (CAP * BLK) + rank * BLK
    target = jnp.where(away < 2, away * slots + data_row, -1024)
    target = (target[:, :, None] + jnp.arange(BLK, dtype=jnp.int32)).reshape(
        devices // 2, keep * BLK, 1
    )
    noise = select_noise(noise_rows.reshape(-1), near_noise, far_noise)
    mine = gram(target, noise, gathered)
    updated_slab, update_weights, data_misfit = update(mine, swap(mine, 1), model_slab)
    return (updated_slab, update_weights, data_misfit.reshape(-1))


def solution(mesh):
    in_specs = (
        P("groups", "map", None),
        P(("groups", "map")),
        P(("groups", "map"), None),
        P(("groups", "map")),
        P(("groups", "map")),
        P(("groups", "map"), None),
        P(None, ("groups", "map")),
    )
    out_specs = (P(None, ("groups", "map")), P("groups", None), P(("groups", "map")))

    def body(amplitude_maps, kept_blocks, *rest):
        few = mesh.shape["map"] == 16 and kept_blocks.shape[0] * BLK == LANE
        chosen = sparse_body if few else dense_body
        return chosen(amplitude_maps, kept_blocks, *rest)

    return jax.shard_map(body, mesh=mesh, in_specs=in_specs, out_specs=out_specs, check_vma=False)
```
